32 devices in a mesh: row: 8 (over y, x, core), col: 4 (over z).
Axes of the slice: x: 2, y: 2, z: 4, core: 2. Of those that a mesh axis runs over, the one named last changes fastest.
Arguments:
- kernel: float32 [4, 1024, 8, 512], P(None, 'row', None, 'col'), as said below
Outputs:
- factored: float32 [4, 1024, 8, 512], P(None, 'row', None, 'col')
Inputs may be any that keep to these rules, and one draw needn't show every extreme that they name: kernel is symmetric and positive definite.
All inputs are finite; a program needn't handle non-finite values.
Results may differ from the reference program's by a relative error of at most 0.0001.
Values sent between devices are 32-bit elements; how exact they have to be, the bound alone decides.
No kernel may reach another device: no remote copies, remote signals or barrier semaphores. Data moves between devices by JAX's collectives and lax.ppermute only.
A program may use at most 128 MiB of HBM per device.

```python
import jax
import jax.numpy as jnp
from jax import lax

BS = 128
PANELS = 2
LR = 4
ROWSPAN = 1024
COLSPAN = 512
LC = 8
M = 4096


def draw_kernel(key, part):
    breadth = 4 * BS
    key_factors = jax.random.fold_in(key, 21)
    key_nugget = jax.random.fold_in(key, 23)
    factors = jax.random.normal(key_factors, (M, breadth), jnp.float32)
    gram = jnp.dot(factors, factors.T, precision=lax.Precision.HIGHEST) * (1.0 / breadth)
    gram = (gram + gram.T) * 0.5
    nugget = jax.random.uniform(key_nugget, (M,), jnp.float32, 0.4, 0.8)
    indices = jnp.arange(M)
    eye_mask = indices[:, None] == indices[None, :]
    values = gram + jnp.where(eye_mask, nugget[:, None] * jnp.ones((1, M), jnp.float32), jnp.float32(0.0))
    return values.reshape(LR, ROWSPAN, LC, COLSPAN)


def setup_inputs(seed: int = 0) -> dict:
    splits = jax.random.split(jax.random.key(seed), 2)
    return {
        "kernel": draw_kernel(jax.random.fold_in(splits[1], 71), 0),
    }


def reference(kernel):
    matrix = kernel.reshape(M, M)
    row_ids = jnp.arange(M, dtype=jnp.int32)
    for panel_idx in range(PANELS):
        start = panel_idx * BS
        finish = start + BS
        factor = jnp.linalg.cholesky(matrix[start:finish, start:finish])
        column = matrix[:, start:finish]
        solved = jax.scipy.linalg.solve_triangular(factor, column.T, lower=True).T
        solved = jnp.where((row_ids < start)[:, None], jnp.float32(0.0), solved)
        solved = solved.at[start:finish].set(factor)
        matrix = matrix - jnp.dot(solved, solved.T, precision=lax.Precision.HIGHEST)
        matrix = matrix.at[:, start:finish].set(solved)
        matrix = matrix.at[start:finish, finish:].set(jnp.float32(0.0))
    return matrix.reshape(LR, ROWSPAN, LC, COLSPAN)
```

```python
import jax
import jax.numpy as jnp
from jax import lax
from jax.sharding import PartitionSpec as P

EXACT = lax.Precision.HIGHEST


def along_col(value, pairs):
    return lax.ppermute(value, "col", pairs)


def spread_col(own, grid_col, n_col):
    even = (grid_col % 2) == 0
    held = own
    reach = 2
    while reach < n_col:
        moved = along_col(held, [(c, c + reach) for c in range(reach) if c + reach < n_col])
        held = jnp.where(grid_col < reach, held, moved)
        reach *= 2
    other = along_col(held, [(c, c ^ 1) for c in range(n_col)])
    return jnp.where(even, held, other), jnp.where(even, other, held)


def spread_row(own, grid_row, n_row, bits):
    holders = [0, 1]
    held = own
    for bit in bits:
        step = 1 << bit
        moved = lax.ppermute(held, "row", [(r, r + step) for r in holders])
        is_new = jnp.zeros((), bool)
        for r in holders:
            is_new = is_new | (grid_row == r + step)
        held = jnp.where(is_new, moved, held)
        holders = holders + [r + step for r in holders]
    return held


def swap_cores(held, grid_row, n_row):
    other = lax.ppermute(held, "row", [(r, r ^ 1) for r in range(n_row)])
    first = (grid_row % 2) == 0
    return jnp.where(first, held, other), jnp.where(first, other, held)


def inverse(factor):
    breadth = factor.shape[0]
    return jax.scipy.linalg.solve_triangular(factor, jnp.eye(breadth, dtype=factor.dtype), lower=True)


def dot(a, b):
    return jnp.dot(a, b, precision=EXACT)


def shards(kernel):
    grid_row = lax.axis_index("row")
    grid_col = lax.axis_index("col")
    n_row = lax.axis_size("row")
    n_col = lax.axis_size("col")
    local_rows, breadth, local_cols, _ = kernel.shape
    bits = list(range(1, n_row.bit_length() - 1))

    column = kernel[:, :, 0, :]
    near, far = spread_col(column[0], grid_col, n_col)
    pair = spread_row(jnp.stack([near, far]), grid_row, n_row, bits)
    top, bottom = swap_cores(pair, grid_row, n_row)
    a00, a10, a11 = top[0], bottom[0], bottom[1]
    rows0, rows1 = spread_col(column, grid_col, n_col)
    half = local_cols // 2
    left = spread_row(kernel[0, :, :half], grid_row, n_row, bits)
    right = spread_row(kernel[0, :, half:], grid_row, n_row, bits[::-1])
    left0, left1 = swap_cores(left, grid_row, n_row)
    right0, right1 = swap_cores(right, grid_row, n_row)
    top0 = jnp.concatenate([left0, right0], axis=1).reshape(breadth, local_cols * breadth)
    top1 = jnp.concatenate([left1, right1], axis=1).reshape(breadth, local_cols * breadth)

    f0 = jnp.linalg.cholesky(a00)
    w0 = inverse(f0)
    l10 = dot(a10, w0.T)
    f1 = jnp.linalg.cholesky(a11 - dot(l10, l10.T))
    w1 = inverse(f1)

    col0 = dot(w0, top0)
    col1 = dot(w1, top1 - dot(l10, col0))
    flat = local_rows * breadth
    row0 = dot(rows0.reshape(flat, breadth), w0.T)
    row1 = dot(rows1.reshape(flat, breadth) - dot(row0, l10.T), w1.T)
    update = dot(row0, col0) + dot(row1, col1)
    matrix = kernel - update.reshape(kernel.shape)

    global_rows = jnp.arange(local_rows, dtype=jnp.int32) * n_row + grid_row
    global_cols = jnp.arange(local_cols, dtype=jnp.int32) * n_col + grid_col
    gr = global_rows[:, None, None]
    row0 = row0.reshape(local_rows, breadth, breadth)
    row1 = row1.reshape(local_rows, breadth, breadth)
    row0 = jnp.where(gr == 0, f0[None], row0)
    row1 = jnp.where(gr == 0, 0.0, jnp.where(gr == 1, f1[None], row1))
    gr = gr[..., None]
    gc = global_cols[None, None, :, None]
    matrix = jnp.where((gr <= 1) & (gc > gr), 0.0, matrix)
    matrix = jnp.where(gc == 0, row0[:, :, None, :], matrix)
    matrix = jnp.where(gc == 1, row1[:, :, None, :], matrix)
    return matrix


def solution(mesh):
    in_specs = (P(None, "row", None, "col"),)
    out_specs = P(None, "row", None, "col")
    return jax.shard_map(shards, mesh=mesh, in_specs=in_specs, out_specs=out_specs, check_vma=False)
```

```python
import jax
import jax.numpy as jnp
from jax import lax
from jax.experimental import pallas as pl
from jax.experimental.pallas import tpu as pltpu
from jax.sharding import PartitionSpec as P

EXACT = lax.Precision.HIGHEST
SUB = 8
VMEM = pl.BlockSpec(memory_space=pltpu.VMEM)
SMEM = pl.BlockSpec(memory_space=pltpu.SMEM)


def dot(a, b):
    return lax.dot_general(a, b, (((1,), (0,)), ((), ())), precision=EXACT, preferred_element_type=jnp.float32)


def dot_t(a, b):
    return lax.dot_general(a, b, (((1,), (1,)), ((), ())), precision=EXACT, preferred_element_type=jnp.float32)


def inverse_of(p):
    r = pl.reciprocal(p, approx=True)
    r = r * (2.0 - p * r)
    return r * (2.0 - p * r)


def eliminate(s, sym, aug):
    n = s.shape[0]
    groups = n // SUB
    sub = lax.broadcasted_iota(jnp.int32, (SUB, n), 0)
    lane = lax.broadcasted_iota(jnp.int32, (SUB, n), 1)
    sym[...] = s.reshape(groups, SUB, n)
    rows = lax.broadcasted_iota(jnp.int32, (n, n), 0)
    cols = lax.broadcasted_iota(jnp.int32, (n, n), 1)
    aug[...] = jnp.where(rows == cols, 1.0, 0.0).reshape(groups, SUB, n)
    for g in range(groups):
        start = g * SUB
        left = groups - g
        rest = sym[g:]
        top = sym[g]
        top_aug = aug[g]
        spread = [jnp.broadcast_to(rest[:, :, start + j:start + j + 1], (left, SUB, n)) for j in range(SUB)]
        scaled = []
        scaled_aug = []
        roots = jnp.zeros((SUB, n), jnp.float32)
        for k in range(SUB):
            pivot = jnp.broadcast_to(spread[k][0, k:k + 1, :], (SUB, n))
            recip = inverse_of(pivot)
            roots = jnp.where(sub == k, pivot, roots)
            for j in range(k + 1, SUB):
                factor = jnp.broadcast_to(spread[k][0, j:j + 1, :], (SUB, n)) * recip
                spread[j] = spread[j] - spread[k] * factor[None]
            row = jnp.broadcast_to(top[k:k + 1, :], (SUB, n)) * recip
            row_aug = jnp.broadcast_to(top_aug[k:k + 1, :], (SUB, n)) * recip
            scaled.append(row)
            scaled_aug.append(row_aug)
            if k + 1 < SUB:
                below = jnp.where(sub > k, spread[k][0], 0.0)
                top = top - below * row
                top_aug = top_aug - below * row_aug
        root = lax.rsqrt(roots)
        sym[g] = jnp.where(lane >= start + sub, top * root, 0.0)
        aug[g] = top_aug * root
        if left > 1:
            low = rest[1:]
            low_aug = aug[g + 1:]
            for k in range(SUB):
                low = low - spread[k][1:] * scaled[k][None]
                low_aug = low_aug - spread[k][1:] * scaled_aug[k][None]
            sym[g + 1:] = low
            aug[g + 1:] = low_aug
    upper = sym[...].reshape(n, n)
    return upper.T, aug[...].reshape(n, n)


def first_factor_kernel(a_ref, f_ref, w_ref, sym, aug):
    f_ref[...], w_ref[...] = eliminate(a_ref[...], sym, aug)


def second_factor_kernel(odd_ref, low_ref, a_ref, w0_ref, f_ref, w_ref, mixed_ref, sym, aug):
    n = a_ref.shape[0]
    w0 = w0_ref[...]
    cross = dot_t(low_ref[...], w0)
    f1, w1 = eliminate(a_ref[...] - dot_t(cross, cross), sym, aug)
    f_ref[...] = f1
    w10 = -dot(w1, dot(cross, w0))
    zero = jnp.zeros((n, n), jnp.float32)
    w_ref[:n, :n] = w0
    w_ref[:n, n:] = zero
    w_ref[n:, :n] = w10
    w_ref[n:, n:] = w1
    odd = odd_ref[0] == 1
    mixed_ref[:n, :n] = jnp.where(odd, zero, w0)
    mixed_ref[:n, n:] = jnp.where(odd, w0, zero)
    mixed_ref[n:, :n] = jnp.where(odd, w1, w10)
    mixed_ref[n:, n:] = jnp.where(odd, w10, w1)


def cost(flops, nbytes):
    return pl.CostEstimate(flops=flops, bytes_accessed=nbytes, transcendentals=0)


def first_factor(a):
    n = a.shape[0]
    square = jax.ShapeDtypeStruct((n, n), jnp.float32)
    scratch = [pltpu.VMEM((n // SUB, SUB, n), jnp.float32)] * 2
    return pl.pallas_call(
        first_factor_kernel,
        out_shape=[square, square],
        in_specs=[VMEM],
        out_specs=[VMEM, VMEM],
        scratch_shapes=scratch,
        name="first_factor",
    )(a)


def second_factor(odd, low, a, w0):
    n = a.shape[0]
    square = jax.ShapeDtypeStruct((n, n), jnp.float32)
    double = jax.ShapeDtypeStruct((2 * n, 2 * n), jnp.float32)
    scratch = [pltpu.VMEM((n // SUB, SUB, n), jnp.float32)] * 2
    return pl.pallas_call(
        second_factor_kernel,
        out_shape=[square, double, double],
        in_specs=[SMEM, VMEM, VMEM, VMEM],
        out_specs=[VMEM, VMEM, VMEM],
        scratch_shapes=scratch,
        name="second_factor",
    )(odd, low, a, w0)


def settle_kernel(place_ref, f0_ref, f1_ref, w_ref, mixed_ref, rows0_ref, rows1_ref, ha_ref, hb_ref, oa_ref, ob_ref,
                  matrix_ref, out_ref, panel):
    grid_row = place_ref[0]
    grid_col = place_ref[1]
    step = pl.program_id(0)
    n = f0_ref.shape[0]
    blocks = matrix_ref.shape[0]
    local_cols = matrix_ref.shape[2]

    @pl.when(step == 0)
    def _():
        mixed = mixed_ref[...]
        for j in range(local_cols):
            stacked = jnp.concatenate([ha_ref[:, j, :], hb_ref[:, j, :], oa_ref[:, j, :], ob_ref[:, j, :]], axis=0)
            panel[:, j * n:(j + 1) * n] = dot(mixed, stacked)

    rows = jnp.concatenate(
        [rows0_ref[...].reshape(blocks * n, n), rows1_ref[...].reshape(blocks * n, n)], axis=1)
    solved = dot_t(rows, w_ref[...])
    for j in range(0, local_cols, 2):
        update = dot(solved, panel[:, j * n:(j + 2) * n])
        for b in range(2):
            part = update[:, b * n:(b + 1) * n].reshape(blocks, n, n)
            out_ref[:, :, j + b, :] = matrix_ref[:, :, j + b, :] - part

    @pl.when(grid_col == 0)
    def _():
        out_ref[:, :, 0, :] = solved[:, :n].reshape(blocks, n, n)

    @pl.when(grid_col == 1)
    def _():
        out_ref[:, :, 0, :] = solved[:, n:].reshape(blocks, n, n)

    @pl.when((step == 0) & (grid_row <= 1))
    def _():
        keep = solved[:n, :n]
        out_ref[0] = jnp.zeros(out_ref.shape[1:], jnp.float32)

        @pl.when((grid_row == 0) & (grid_col == 0))
        def _():
            out_ref[0, :, 0, :] = f0_ref[...]

        @pl.when((grid_row == 1) & (grid_col == 0))
        def _():
            out_ref[0, :, 0, :] = keep

        @pl.when((grid_row == 1) & (grid_col == 1))
        def _():
            out_ref[0, :, 0, :] = f1_ref[...]


def settle(place, f0, f1, w, mixed, rows0, rows1, ha, hb, oa, ob, matrix):
    local_rows, n, local_cols, _ = matrix.shape
    per = 2
    strip = pl.BlockSpec((per, n, n), lambda s: (s, 0, 0))
    slab = pl.BlockSpec((per, n, local_cols, n), lambda s: (s, 0, 0, 0))
    return pl.pallas_call(
        settle_kernel,
        grid=(local_rows // per,),
        out_shape=jax.ShapeDtypeStruct(matrix.shape, jnp.float32),
        in_specs=[SMEM] + [VMEM] * 4 + [strip] * 2 + [VMEM] * 4 + [slab],
        out_specs=slab,
        scratch_shapes=[pltpu.VMEM((2 * n, local_cols * n), jnp.float32)],
        compiler_params=pltpu.CompilerParams(vmem_limit_bytes=40 * 1024 * 1024),
        name="settle",
    )(place, f0, f1, w, mixed, rows0, rows1, ha, hb, oa, ob, matrix)


def spread_col(own, grid_col, n_col):
    even = (grid_col % 2) == 0
    held = own
    reach = 2
    while reach < n_col:
        moved = lax.ppermute(held, "col", [(c, c + reach) for c in range(reach) if c + reach < n_col])
        held = jnp.where(grid_col < reach, held, moved)
        reach *= 2
    other = lax.ppermute(held, "col", [(c, c ^ 1) for c in range(n_col)])
    return jnp.where(even, held, other), jnp.where(even, other, held)


def spread_row(own, grid_row, bits, holders=(0, 1)):
    holders = list(holders)
    held = own
    for bit in bits:
        step = 1 << bit
        moved = lax.ppermute(held, "row", [(r, r + step) for r in holders])
        held = jnp.where(((grid_row >> bit) & 1) == 1, moved, held)
        holders = holders + [r + step for r in holders]
    return held


def swap_cores(held, n_row):
    return lax.ppermute(held, "row", [(r, r ^ 1) for r in range(n_row)])


def shards(kernel):
    grid_row = lax.axis_index("row")
    grid_col = lax.axis_index("col")
    n_row = lax.axis_size("row")
    n_col = lax.axis_size("col")
    local_rows, n, local_cols, _ = kernel.shape
    bits = list(range(1, n_row.bit_length() - 1))
    odd = grid_row % 2

    def flat(r, c):
        return r * n_col + c

    block = kernel[0, :, 0, :]
    here0 = block
    here1 = block
    for shift in range(1, n_col):
        pairs = [(flat(0, 0), flat(0, shift)), (flat(1, 0), flat(1, shift))]
        pairs.append((flat(1, 1), flat(1, 0 if shift == 1 else shift ^ 1)))
        moved = lax.ppermute(block, ("row", "col"), pairs)
        here0 = jnp.where(grid_col == shift, moved, here0)
        here1 = jnp.where(grid_col == (0 if shift == 1 else shift ^ 1), moved, here1)
    here0 = spread_row(here0, grid_row, bits)
    here1 = spread_row(here1, grid_row, bits, (1,))
    swapped = swap_cores(here0, n_row)
    a00 = jnp.where(odd == 0, here0, swapped)
    a10 = jnp.where(odd == 0, swapped, here0)
    a11 = jnp.where(odd == 0, lax.ppermute(here1, "row", [(r + 1, r) for r in range(0, n_row, 2)]), here1)

    rows0, rows1 = spread_col(kernel[:, :, 0, :], grid_col, n_col)
    half = n // 2
    ha = spread_row(kernel[0, :half], grid_row, bits)
    hb = spread_row(kernel[0, half:], grid_row, bits[::-1])
    oa = swap_cores(ha, n_row)
    ob = swap_cores(hb, n_row)

    f0, w0 = first_factor(a00)
    f1, w, mixed = second_factor(odd[None], a10, a11, w0)
    place = jnp.stack([grid_row, grid_col])
    return settle(place, f0, f1, w, mixed, rows0, rows1, ha, hb, oa, ob, kernel)


def solution(mesh):
    in_specs = (P(None, "row", None, "col"),)
    out_specs = P(None, "row", None, "col")
    return jax.shard_map(shards, mesh=mesh, in_specs=in_specs, out_specs=out_specs, check_vma=False)
```

```python
import jax
import jax.numpy as jnp
from jax import lax
from jax.experimental import pallas as pl
from jax.experimental.pallas import tpu as pltpu
from jax.sharding import PartitionSpec as P

EXACT = lax.Precision.HIGHEST
SUB = 8
MIB = 1024 * 1024
VMEM = pl.BlockSpec(memory_space=pltpu.VMEM)
HBM = pl.BlockSpec(memory_space=pltpu.HBM)


def dot(a, b):
    return lax.dot_general(a, b, (((1,), (0,)), ((), ())), precision=EXACT, preferred_element_type=jnp.float32)


def dot_t(a, b):
    return lax.dot_general(a, b, (((1,), (1,)), ((), ())), precision=EXACT, preferred_element_type=jnp.float32)


def inverse_of(p):
    r = pl.reciprocal(p, approx=True)
    r = r * (2.0 - p * r)
    return r * (2.0 - p * r)


def eliminate(s, sym, aug):
    n = s.shape[0]
    groups = n // SUB
    sub = lax.broadcasted_iota(jnp.int32, (SUB, n), 0)
    lane = lax.broadcasted_iota(jnp.int32, (SUB, n), 1)
    sym[...] = s.reshape(groups, SUB, n)
    rows = lax.broadcasted_iota(jnp.int32, (n, n), 0)
    cols = lax.broadcasted_iota(jnp.int32, (n, n), 1)
    aug[...] = jnp.where(rows == cols, 1.0, 0.0).reshape(groups, SUB, n)
    for g in range(groups):
        start = g * SUB
        left = groups - g
        rest = sym[g:]
        top = sym[g]
        top_aug = aug[g]
        spread = [jnp.broadcast_to(rest[:, :, start + j:start + j + 1], (left, SUB, n)) for j in range(SUB)]
        scaled = []
        scaled_aug = []
        roots = jnp.zeros((SUB, n), jnp.float32)
        for k in range(SUB):
            pivot = jnp.broadcast_to(spread[k][0, k:k + 1, :], (SUB, n))
            recip = inverse_of(pivot)
            roots = jnp.where(sub == k, pivot, roots)
            for j in range(k + 1, SUB):
                factor = jnp.broadcast_to(spread[k][0, j:j + 1, :], (SUB, n)) * recip
                spread[j] = spread[j] - spread[k] * factor[None]
            row = jnp.broadcast_to(top[k:k + 1, :], (SUB, n)) * recip
            row_aug = jnp.broadcast_to(top_aug[k:k + 1, :], (SUB, n)) * recip
            scaled.append(row)
            scaled_aug.append(row_aug)
            if k + 1 < SUB:
                below = jnp.where(sub > k, spread[k][0], 0.0)
                top = top - below * row
                top_aug = top_aug - below * row_aug
        root = lax.rsqrt(roots)
        sym[g] = jnp.where(lane >= start + sub, top * root, 0.0)
        aug[g] = top_aug * root
        if left > 1:
            low = rest[1:]
            low_aug = aug[g + 1:]
            for k in range(SUB):
                low = low - spread[k][1:] * scaled[k][None]
                low_aug = low_aug - spread[k][1:] * scaled_aug[k][None]
            sym[g + 1:] = low
            aug[g + 1:] = low_aug
    upper = sym[...].reshape(n, n)
    return upper.T, aug[...].reshape(n, n)


def joined(mine_ref, other_ref, odd):
    mine, other = mine_ref[...], other_ref[...]
    return jnp.concatenate([jnp.where(odd, other, mine), jnp.where(odd, mine, other)], axis=0)


def is_odd_row():
    return lax.rem(lax.axis_index("row"), 2) == 1


def estimate(flops, nbytes):
    return pl.CostEstimate(flops=flops, bytes_accessed=nbytes, transcendentals=0)


def corner_kernel(matrix_ref, own_ref, send_ref, sems):
    half = own_ref.shape[0]
    odd = lax.rem(lax.axis_index("row"), 2)
    own = pltpu.make_async_copy(matrix_ref.at[0, pl.ds(odd * half, half), 0, :], own_ref, sems.at[0])
    send = pltpu.make_async_copy(matrix_ref.at[0, pl.ds((1 - odd) * half, half), 0, :], send_ref, sems.at[1])
    send.start()
    own.start()
    send.wait()
    own.wait()


def corner_halves(matrix):
    n = matrix.shape[1]
    half = jax.ShapeDtypeStruct((n // 2, n), jnp.float32)
    return pl.pallas_call(
        corner_kernel,
        out_shape=[half, half],
        in_specs=[HBM],
        out_specs=[VMEM, VMEM],
        scratch_shapes=[pltpu.SemaphoreType.DMA((2,))],
        compiler_params=pltpu.CompilerParams(vmem_limit_bytes=2 * MIB),
        cost_estimate=estimate(0, 3 * MIB),
        name="corner_halves",
    )(matrix)


def panels_kernel(matrix_ref, column_ref, upper_ref, lower_ref, sems):
    local_cols, half, _ = upper_ref.shape
    copies = [pltpu.make_async_copy(matrix_ref.at[:, :, 0, :], column_ref, sems.at[0])]
    for j in range(local_cols):
        copies.append(pltpu.make_async_copy(matrix_ref.at[0, pl.ds(0, half), j, :], upper_ref.at[j], sems.at[1 + j]))
        copies.append(pltpu.make_async_copy(
            matrix_ref.at[0, pl.ds(half, half), j, :], lower_ref.at[j], sems.at[1 + local_cols + j]))
    for copy in copies:
        copy.start()
    for copy in copies:
        copy.wait()


def panels(matrix):
    local_rows, n, local_cols, _ = matrix.shape
    strip = jax.ShapeDtypeStruct((local_cols, n // 2, n), jnp.float32)
    return pl.pallas_call(
        panels_kernel,
        out_shape=[jax.ShapeDtypeStruct((local_rows, n, n), jnp.float32), strip, strip],
        in_specs=[HBM],
        out_specs=[VMEM] * 3,
        scratch_shapes=[pltpu.SemaphoreType.DMA((1 + 2 * local_cols,))],
        compiler_params=pltpu.CompilerParams(vmem_limit_bytes=4 * MIB),
        cost_estimate=estimate(0, 4 * MIB),
        name="panels",
    )(matrix)


def first_factor_kernel(mine_ref, other_ref, f_ref, w_ref, sym, aug):
    f_ref[...], w_ref[...] = eliminate(joined(mine_ref, other_ref, is_odd_row()), sym, aug)


def first_factor(mine, other):
    n = mine.shape[1]
    square = jax.ShapeDtypeStruct((n, n), jnp.float32)
    return pl.pallas_call(
        first_factor_kernel,
        out_shape=[square, square],
        in_specs=[VMEM, VMEM],
        out_specs=[VMEM, VMEM],
        scratch_shapes=[pltpu.VMEM((n // SUB, SUB, n), jnp.float32)] * 2,
        compiler_params=pltpu.CompilerParams(vmem_limit_bytes=4 * MIB),
        cost_estimate=estimate(8 * 10**9, 2 * MIB),
        name="first_factor",
    )(mine, other)


def second_factor_kernel(low_mine_ref, low_other_ref, mine_ref, other_ref, w0_ref, matrix_ref, f_ref, w_ref, mixed_ref,
                         blocks_ref, sym, aug, sems):
    n = w0_ref.shape[0]
    local_cols = matrix_ref.shape[2]
    copies = [pltpu.make_async_copy(matrix_ref.at[:, :, j, :], blocks_ref.at[j], sems.at[j]) for j in range(local_cols)]
    for copy in copies:
        copy.start()
    odd = is_odd_row()
    w0 = w0_ref[...]
    cross = dot_t(joined(low_mine_ref, low_other_ref, odd), w0)
    f1, w1 = eliminate(joined(mine_ref, other_ref, odd) - dot_t(cross, cross), sym, aug)
    f_ref[...] = f1
    w10 = -dot(w1, dot(cross, w0))
    zero = jnp.zeros((n, n), jnp.float32)
    w_ref[:n, :n] = w0
    w_ref[:n, n:] = zero
    w_ref[n:, :n] = w10
    w_ref[n:, n:] = w1
    mixed_ref[:n, :n] = jnp.where(odd, zero, w0)
    mixed_ref[:n, n:] = jnp.where(odd, w0, zero)
    mixed_ref[n:, :n] = jnp.where(odd, w1, w10)
    mixed_ref[n:, n:] = jnp.where(odd, w10, w1)
    for copy in copies:
        copy.wait()


def second_factor(low_mine, low_other, mine, other, w0, matrix):
    local_rows, n, local_cols, _ = matrix.shape
    square = jax.ShapeDtypeStruct((n, n), jnp.float32)
    double = jax.ShapeDtypeStruct((2 * n, 2 * n), jnp.float32)
    blocks = jax.ShapeDtypeStruct((local_cols, local_rows, n, n), jnp.float32)
    return pl.pallas_call(
        second_factor_kernel,
        out_shape=[square, double, double, blocks],
        in_specs=[VMEM] * 5 + [HBM],
        out_specs=[VMEM] * 4,
        scratch_shapes=[pltpu.VMEM((n // SUB, SUB, n), jnp.float32)] * 2 + [pltpu.SemaphoreType.DMA((local_cols,))],
        compiler_params=pltpu.CompilerParams(vmem_limit_bytes=12 * MIB),
        cost_estimate=estimate(8 * 10**9, 4 * MIB),
        name="second_factor",
    )(low_mine, low_other, mine, other, w0, matrix)


def settle_kernel(f0_ref, f1_ref, w_ref, mixed_ref, rows_ref, rows_other_ref, ha_ref, hb_ref, oa_ref, ob_ref, blocks_ref,
                  out_ref, result, sems):
    grid_row = lax.axis_index("row")
    grid_col = lax.axis_index("col")
    n = f0_ref.shape[0]
    local_cols, local_rows, _, _ = blocks_ref.shape
    flat = local_rows * n
    own = rows_ref[...].reshape(flat, n)
    other = rows_other_ref[...].reshape(flat, n)
    swapped = lax.rem(grid_col, 2) == 1
    rows = jnp.concatenate([jnp.where(swapped, other, own), jnp.where(swapped, own, other)], axis=1)
    solved = dot_t(rows, w_ref[...])
    mixed = mixed_ref[...]
    copies = []
    for j in range(0, local_cols, 2):
        pair = (j, j + 1)
        stacked = jnp.concatenate(
            [jnp.concatenate([ha_ref[b], hb_ref[b], oa_ref[b], ob_ref[b]], axis=0) for b in pair], axis=1)
        update = dot(solved, dot(mixed, stacked))
        for b in pair:
            part = update[:, (b - j) * n:(b - j + 1) * n].reshape(local_rows, n, n)
            result[b] = blocks_ref[b] - part
        if j == 0:
            @pl.when(grid_col == 0)
            def _():
                result[0] = solved[:, :n].reshape(local_rows, n, n)

            @pl.when(grid_col == 1)
            def _():
                result[0] = solved[:, n:].reshape(local_rows, n, n)

        @pl.when(grid_row <= 1)
        def _():
            for b in pair:
                if b > 0:
                    result[b, 0] = jnp.zeros((n, n), jnp.float32)
            if j == 0:
                @pl.when(grid_col > grid_row)
                def _():
                    result[0, 0] = jnp.zeros((n, n), jnp.float32)

                @pl.when((grid_row == 0) & (grid_col == 0))
                def _():
                    result[0, 0] = f0_ref[...]

                @pl.when((grid_row == 1) & (grid_col == 1))
                def _():
                    result[0, 0] = f1_ref[...]
        for b in pair:
            copy = pltpu.make_async_copy(result.at[b], out_ref.at[:, :, b, :], sems.at[b])
            copy.start()
            copies.append(copy)
    for copy in copies:
        copy.wait()


def settle(f0, f1, w, mixed, rows, rows_other, ha, hb, oa, ob, blocks):
    local_cols, local_rows, n, _ = blocks.shape
    return pl.pallas_call(
        settle_kernel,
        out_shape=jax.ShapeDtypeStruct((local_rows, n, local_cols, n), jnp.float32),
        in_specs=[VMEM] * 11,
        out_specs=HBM,
        scratch_shapes=[pltpu.VMEM(blocks.shape, jnp.float32), pltpu.SemaphoreType.DMA((local_cols,))],
        compiler_params=pltpu.CompilerParams(vmem_limit_bytes=32 * MIB),
        cost_estimate=estimate(4 * 10**9, 6 * MIB),
        name="settle",
    )(f0, f1, w, mixed, rows, rows_other, ha, hb, oa, ob, blocks)


def exchange(value, axis, mask, size):
    return lax.ppermute(value, axis, [(i, i ^ mask) for i in range(size)])


def bit_set(index, bit):
    return ((index >> bit) & 1) == 1


def spread(own, axis, index, size, bits):
    held = own
    for bit in bits:
        held = jnp.where(bit_set(index, bit), exchange(held, axis, 1 << bit, size), held)
    return held


def spread_pairs(own, axis, index, size, bits):
    held = own
    for at in range(0, len(bits) - 1, 2):
        low, high = bits[at], bits[at + 1]
        from_low = exchange(held, axis, 1 << low, size)
        from_high = exchange(held, axis, 1 << high, size)
        from_both = exchange(held, axis, (1 << low) | (1 << high), size)
        has_low, has_high = bit_set(index, low), bit_set(index, high)
        held = jnp.where(has_low & has_high, from_both, jnp.where(has_low, from_low, jnp.where(has_high, from_high, held)))
    if len(bits) % 2:
        held = spread(held, axis, index, size, bits[-1:])
    return held


def shards(kernel):
    grid_row = lax.axis_index("row")
    grid_col = lax.axis_index("col")
    n_row = lax.axis_size("row")
    n_col = lax.axis_size("col")
    row_bits = list(range(1, n_row.bit_length() - 1))
    col_bits = list(range(1, n_col.bit_length() - 1))
    odd = (grid_row % 2) == 1
    right = (grid_col % 2) == 1

    own, send = corner_halves(kernel)
    got = exchange(send, "row", 1, n_row)
    diag = jnp.where(odd != right, got, own)
    low = jnp.where(odd, own, got)
    diag = spread_pairs(diag, "row", grid_row, n_row, row_bits)
    low = spread_pairs(low, "row", grid_row, n_row, row_bits)
    column, upper, lower = panels(kernel)

    diag = spread(diag, "col", grid_col, n_col, col_bits)
    diag_other = exchange(diag, "col", 1, n_col)
    first = jnp.where(right, diag_other, diag)
    second = jnp.where(right, diag, diag_other)
    first_far = exchange(first, "row", 1, n_row)
    low = spread(low, "col", grid_col, n_col, col_bits + [0])
    second_far = exchange(second, "row", 1, n_row)
    low_far = exchange(low, "row", 1, n_row)

    ha = spread(upper, "row", grid_row, n_row, row_bits)
    hb = spread(lower, "row", grid_row, n_row, row_bits[::-1])
    rows = spread(column, "col", grid_col, n_col, col_bits)

    f0, w0 = first_factor(first, first_far)
    oa = exchange(ha, "row", 1, n_row)
    ob = exchange(hb, "row", 1, n_row)
    rows_other = exchange(rows, "col", 1, n_col)
    f1, w, mixed, blocks = second_factor(low, low_far, second, second_far, w0, kernel)
    return settle(f0, f1, w, mixed, rows, rows_other, ha, hb, oa, ob, blocks)


def solution(mesh):
    in_specs = (P(None, "row", None, "col"),)
    out_specs = P(None, "row", None, "col")
    return jax.shard_map(shards, mesh=mesh, in_specs=in_specs, out_specs=out_specs, check_vma=False)
```

```python
import jax
import jax.numpy as jnp
from jax import lax
from jax.experimental import pallas as pl
from jax.experimental.pallas import tpu as pltpu
from jax.sharding import PartitionSpec as P

EXACT = lax.Precision.HIGHEST
SUB = 8
MIB = 1024 * 1024
VMEM = pl.BlockSpec(memory_space=pltpu.VMEM)
HBM = pl.BlockSpec(memory_space=pltpu.HBM)


def dot(a, b):
    return lax.dot_general(a, b, (((1,), (0,)), ((), ())), precision=EXACT, preferred_element_type=jnp.float32)


def dot_t(a, b):
    return lax.dot_general(a, b, (((1,), (1,)), ((), ())), precision=EXACT, preferred_element_type=jnp.float32)


def inverse_of(p):
    r = pl.reciprocal(p, approx=True)
    r = r * (2.0 - p * r)
    return r * (2.0 - p * r)


def eliminate(s, sym, aug):
    n = s.shape[0]
    groups = n // SUB
    sub = lax.broadcasted_iota(jnp.int32, (SUB, n), 0)
    lane = lax.broadcasted_iota(jnp.int32, (SUB, n), 1)
    sym[...] = s.reshape(groups, SUB, n)
    rows = lax.broadcasted_iota(jnp.int32, (n, n), 0)
    cols = lax.broadcasted_iota(jnp.int32, (n, n), 1)
    aug[...] = jnp.where(rows == cols, 1.0, 0.0).reshape(groups, SUB, n)
    for g in range(groups):
        start = g * SUB
        left = groups - g
        rest = sym[g:]
        top = sym[g]
        top_aug = aug[g]
        spread = [jnp.broadcast_to(rest[:, :, start + j:start + j + 1], (left, SUB, n)) for j in range(SUB)]
        scaled = []
        scaled_aug = []
        roots = jnp.zeros((SUB, n), jnp.float32)
        for k in range(SUB):
            pivot = jnp.broadcast_to(spread[k][0, k:k + 1, :], (SUB, n))
            recip = inverse_of(pivot)
            roots = jnp.where(sub == k, pivot, roots)
            for j in range(k + 1, SUB):
                factor = jnp.broadcast_to(spread[k][0, j:j + 1, :], (SUB, n)) * recip
                spread[j] = spread[j] - spread[k] * factor[None]
            row = jnp.broadcast_to(top[k:k + 1, :], (SUB, n)) * recip
            row_aug = jnp.broadcast_to(top_aug[k:k + 1, :], (SUB, n)) * recip
            scaled.append(row)
            scaled_aug.append(row_aug)
            if k + 1 < SUB:
                below = jnp.where(sub > k, spread[k][0], 0.0)
                top = top - below * row
                top_aug = top_aug - below * row_aug
        root = lax.rsqrt(roots)
        sym[g] = jnp.where(lane >= start + sub, top * root, 0.0)
        aug[g] = top_aug * root
        if left > 1:
            low = rest[1:]
            low_aug = aug[g + 1:]
            for k in range(SUB):
                low = low - spread[k][1:] * scaled[k][None]
                low_aug = low_aug - spread[k][1:] * scaled_aug[k][None]
            sym[g + 1:] = low
            aug[g + 1:] = low_aug
    upper = sym[...].reshape(n, n)
    return upper.T, aug[...].reshape(n, n)


def is_odd_row():
    return lax.rem(lax.axis_index("row"), 2) == 1


def estimate(flops, nbytes):
    return pl.CostEstimate(flops=flops, bytes_accessed=nbytes, transcendentals=0)


def panels_kernel(matrix_ref, column_ref, upper_ref, lower_ref, sems):
    local_cols, half, _ = upper_ref.shape
    copies = [pltpu.make_async_copy(matrix_ref.at[:, :, 0, :], column_ref, sems.at[0])]
    for j in range(local_cols):
        copies.append(pltpu.make_async_copy(matrix_ref.at[0, pl.ds(0, half), j, :], upper_ref.at[j], sems.at[1 + j]))
        copies.append(pltpu.make_async_copy(
            matrix_ref.at[0, pl.ds(half, half), j, :], lower_ref.at[j], sems.at[1 + local_cols + j]))
    for copy in copies:
        copy.start()
    for copy in copies:
        copy.wait()


def panels(matrix):
    local_rows, n, local_cols, _ = matrix.shape
    strip = jax.ShapeDtypeStruct((local_cols, n // 2, n), jnp.float32)
    return pl.pallas_call(
        panels_kernel,
        out_shape=[jax.ShapeDtypeStruct((local_rows, n, n), jnp.float32), strip, strip],
        in_specs=[HBM],
        out_specs=[VMEM] * 3,
        scratch_shapes=[pltpu.SemaphoreType.DMA((1 + 2 * local_cols,))],
        compiler_params=pltpu.CompilerParams(vmem_limit_bytes=4 * MIB),
        cost_estimate=estimate(0, 4 * MIB),
        name="panels",
    )(matrix)


def first_factor_kernel(a_ref, f_ref, w_ref, sym, aug):
    f_ref[...], w_ref[...] = eliminate(a_ref[...], sym, aug)


def first_factor(a):
    n = a.shape[1]
    square = jax.ShapeDtypeStruct((n, n), jnp.float32)
    return pl.pallas_call(
        first_factor_kernel,
        out_shape=[square, square],
        in_specs=[VMEM],
        out_specs=[VMEM, VMEM],
        scratch_shapes=[pltpu.VMEM((n // SUB, SUB, n), jnp.float32)] * 2,
        compiler_params=pltpu.CompilerParams(vmem_limit_bytes=4 * MIB),
        cost_estimate=estimate(8 * 10**9, 2 * MIB),
        name="first_factor",
    )(a)


def second_factor_kernel(low_ref, a_ref, w0_ref, matrix_ref, f_ref, w_ref, mixed_ref,
                         blocks_ref, sym, aug, sems):
    n = w0_ref.shape[0]
    local_cols = matrix_ref.shape[2]
    copies = [pltpu.make_async_copy(matrix_ref.at[:, :, j, :], blocks_ref.at[j], sems.at[j]) for j in range(local_cols)]
    for copy in copies:
        copy.start()
    odd = is_odd_row()
    w0 = w0_ref[...]
    cross = dot_t(low_ref[...], w0)
    f1, w1 = eliminate(a_ref[...] - dot_t(cross, cross), sym, aug)
    f_ref[...] = f1
    w10 = -dot(w1, dot(cross, w0))
    zero = jnp.zeros((n, n), jnp.float32)
    w_ref[:n, :n] = w0
    w_ref[:n, n:] = zero
    w_ref[n:, :n] = w10
    w_ref[n:, n:] = w1
    mixed_ref[:n, :n] = jnp.where(odd, zero, w0)
    mixed_ref[:n, n:] = jnp.where(odd, w0, zero)
    mixed_ref[n:, :n] = jnp.where(odd, w1, w10)
    mixed_ref[n:, n:] = jnp.where(odd, w10, w1)
    for copy in copies:
        copy.wait()


def second_factor(low, a, w0, matrix):
    local_rows, n, local_cols, _ = matrix.shape
    square = jax.ShapeDtypeStruct((n, n), jnp.float32)
    double = jax.ShapeDtypeStruct((2 * n, 2 * n), jnp.float32)
    blocks = jax.ShapeDtypeStruct((local_cols, local_rows, n, n), jnp.float32)
    return pl.pallas_call(
        second_factor_kernel,
        out_shape=[square, double, double, blocks],
        in_specs=[VMEM] * 3 + [HBM],
        out_specs=[VMEM] * 4,
        scratch_shapes=[pltpu.VMEM((n // SUB, SUB, n), jnp.float32)] * 2 + [pltpu.SemaphoreType.DMA((local_cols,))],
        compiler_params=pltpu.CompilerParams(vmem_limit_bytes=12 * MIB),
        cost_estimate=estimate(8 * 10**9, 4 * MIB),
        name="second_factor",
    )(low, a, w0, matrix)


def settle_kernel(f0_ref, f1_ref, w_ref, mixed_ref, rows_ref, rows_other_ref, ha_ref, hb_ref, oa_ref, ob_ref, blocks_ref,
                  out_ref, result, sems):
    grid_row = lax.axis_index("row")
    grid_col = lax.axis_index("col")
    n = f0_ref.shape[0]
    local_cols, local_rows, _, _ = blocks_ref.shape
    flat = local_rows * n
    own = rows_ref[...].reshape(flat, n)
    other = rows_other_ref[...].reshape(flat, n)
    swapped = lax.rem(grid_col, 2) == 1
    rows = jnp.concatenate([jnp.where(swapped, other, own), jnp.where(swapped, own, other)], axis=1)
    solved = dot_t(rows, w_ref[...])
    mixed = mixed_ref[...]
    copies = []
    for j in range(0, local_cols, 2):
        pair = (j, j + 1)
        stacked = jnp.concatenate(
            [jnp.concatenate([ha_ref[b], hb_ref[b], oa_ref[b], ob_ref[b]], axis=0) for b in pair], axis=1)
        update = dot(solved, dot(mixed, stacked))
        for b in pair:
            part = update[:, (b - j) * n:(b - j + 1) * n].reshape(local_rows, n, n)
            result[b] = blocks_ref[b] - part
        if j == 0:
            @pl.when(grid_col == 0)
            def _():
                result[0] = solved[:, :n].reshape(local_rows, n, n)

            @pl.when(grid_col == 1)
            def _():
                result[0] = solved[:, n:].reshape(local_rows, n, n)

        @pl.when(grid_row <= 1)
        def _():
            for b in pair:
                if b > 0:
                    result[b, 0] = jnp.zeros((n, n), jnp.float32)
            if j == 0:
                @pl.when(grid_col > grid_row)
                def _():
                    result[0, 0] = jnp.zeros((n, n), jnp.float32)

                @pl.when((grid_row == 0) & (grid_col == 0))
                def _():
                    result[0, 0] = f0_ref[...]

                @pl.when((grid_row == 1) & (grid_col == 1))
                def _():
                    result[0, 0] = f1_ref[...]
        for b in pair:
            copy = pltpu.make_async_copy(result.at[b], out_ref.at[:, :, b, :], sems.at[b])
            copy.start()
            copies.append(copy)
    for copy in copies:
        copy.wait()


def settle(f0, f1, w, mixed, rows, rows_other, ha, hb, oa, ob, blocks):
    local_cols, local_rows, n, _ = blocks.shape
    return pl.pallas_call(
        settle_kernel,
        out_shape=jax.ShapeDtypeStruct((local_rows, n, local_cols, n), jnp.float32),
        in_specs=[VMEM] * 11,
        out_specs=HBM,
        scratch_shapes=[pltpu.VMEM(blocks.shape, jnp.float32), pltpu.SemaphoreType.DMA((local_cols,))],
        compiler_params=pltpu.CompilerParams(vmem_limit_bytes=32 * MIB),
        cost_estimate=estimate(4 * 10**9, 6 * MIB),
        name="settle",
    )(f0, f1, w, mixed, rows, rows_other, ha, hb, oa, ob, blocks)


def exchange(value, axis, mask, size):
    return lax.ppermute(value, axis, [(i, i ^ mask) for i in range(size)])


def bit_set(index, bit):
    return ((index >> bit) & 1) == 1


def spread(own, axis, index, size, bits):
    held = own
    for bit in bits:
        held = jnp.where(bit_set(index, bit), exchange(held, axis, 1 << bit, size), held)
    return held


def corner(block, n_row, n_col):
    devices = n_row * n_col
    n = block.shape[0]
    width = min(n, n * n // devices)
    slices = block.reshape(devices, n * n // devices // width, width)
    came = lax.all_to_all(slices, ("row", "col"), 0, 0)
    mine = jnp.stack([came[0], came[n_col], came[n_col + 1]])
    every = lax.all_to_all(jnp.broadcast_to(mine[None], (devices,) + mine.shape), ("row", "col"), 0, 0)
    return [every[:, b].reshape(n, n) for b in range(3)]


def shards(kernel):
    grid_row = lax.axis_index("row")
    grid_col = lax.axis_index("col")
    n_row = lax.axis_size("row")
    n_col = lax.axis_size("col")
    row_bits = list(range(1, n_row.bit_length() - 1))
    col_bits = list(range(1, n_col.bit_length() - 1))

    a00, a10, a11 = corner(kernel[0, :, 0, :], n_row, n_col)

    column, upper, lower = panels(kernel)
    ha = spread(upper, "row", grid_row, n_row, row_bits)
    hb = spread(lower, "row", grid_row, n_row, row_bits[::-1])
    rows = spread(column, "col", grid_col, n_col, col_bits)
    oa = exchange(ha, "row", 1, n_row)
    ob = exchange(hb, "row", 1, n_row)
    rows_other = exchange(rows, "col", 1, n_col)

    f0, w0 = first_factor(a00)
    f1, w, mixed, blocks = second_factor(a10, a11, w0, kernel)
    return settle(f0, f1, w, mixed, rows, rows_other, ha, hb, oa, ob, blocks)


def solution(mesh):
    in_specs = (P(None, "row", None, "col"),)
    out_specs = P(None, "row", None, "col")
    return jax.shard_map(shards, mesh=mesh, in_specs=in_specs, out_specs=out_specs, check_vma=False)
```

```python
import jax
import jax.numpy as jnp
from jax import lax
from jax.experimental import pallas as pl
from jax.experimental.pallas import tpu as pltpu
from jax.sharding import PartitionSpec as P

EXACT = lax.Precision.HIGHEST
SUB = 8
MIB = 1024 * 1024
VMEM = pl.BlockSpec(memory_space=pltpu.VMEM)
HBM = pl.BlockSpec(memory_space=pltpu.HBM)


def dot(a, b):
    return lax.dot_general(a, b, (((1,), (0,)), ((), ())), precision=EXACT, preferred_element_type=jnp.float32)


def dot_t(a, b):
    return lax.dot_general(a, b, (((1,), (1,)), ((), ())), precision=EXACT, preferred_element_type=jnp.float32)


def full(row):
    return jnp.broadcast_to(row, (SUB, row.shape[-1]))


def eliminate(s, sym, aug):
    n = s.shape[0]
    groups = n // SUB
    sub = lax.broadcasted_iota(jnp.int32, (SUB, n), 0)
    lane = lax.broadcasted_iota(jnp.int32, (SUB, n), 1)
    sym[...] = s.reshape(groups, SUB, n)
    rows = lax.broadcasted_iota(jnp.int32, (n, n), 0)
    cols = lax.broadcasted_iota(jnp.int32, (n, n), 1)
    aug[...] = jnp.where(rows == cols, 1.0, 0.0).reshape(groups, SUB, n)
    for g in range(groups):
        start = g * SUB
        left = groups - g
        rest = sym[g:]
        top = sym[g]
        top_aug = aug[g]
        spread = [jnp.broadcast_to(rest[:, :, start + j:start + j + 1], (left, SUB, n)) for j in range(SUB)]
        unit = {(i, j): full(spread[j][0, i:i + 1, :]) for j in range(SUB) for i in range(j, SUB)}
        scaled = []
        scaled_aug = []
        roots = jnp.zeros((SUB, n), jnp.float32)
        for k in range(SUB):
            pivot = unit[k, k]
            guess = pl.reciprocal(pivot, approx=True)
            rest_of = 2.0 - pivot * guess
            recip = guess * rest_of
            roots = jnp.where(sub == k, pivot, roots)
            for j in range(k + 1, SUB):
                unit[j, j] = unit[j, j] - (unit[j, k] * unit[j, k] * guess) * rest_of
                for i in range(j + 1, SUB):
                    unit[i, j] = unit[i, j] - (unit[i, k] * unit[j, k] * guess) * rest_of
            for j in range(k + 1, SUB):
                factor = unit[j, k] * recip
                spread[j] = spread[j] - spread[k] * factor[None]
            row = full(top[k:k + 1, :]) * recip
            row_aug = full(top_aug[k:k + 1, :]) * recip
            scaled.append(row)
            scaled_aug.append(row_aug)
            if k + 1 < SUB:
                below = jnp.where(sub > k, spread[k][0], 0.0)
                top = top - below * row
                top_aug = top_aug - below * row_aug
        root = lax.rsqrt(roots)
        sym[g] = jnp.where(lane >= start + sub, top * root, 0.0)
        aug[g] = top_aug * root
        if left > 1:
            low = rest[1:]
            low_aug = aug[g + 1:]
            for k in range(SUB):
                low = low - spread[k][1:] * scaled[k][None]
                low_aug = low_aug - spread[k][1:] * scaled_aug[k][None]
            sym[g + 1:] = low
            aug[g + 1:] = low_aug
    upper = sym[...].reshape(n, n)
    return upper.T, aug[...].reshape(n, n)


def is_odd_row():
    return lax.rem(lax.axis_index("row"), 2) == 1


def parts(x):
    high = x.astype(jnp.bfloat16)
    rest = x - high.astype(jnp.float32)
    middle = rest.astype(jnp.bfloat16)
    return high, middle, (rest - middle.astype(jnp.float32)).astype(jnp.bfloat16)


def dot_parts(a, b, dims=((1,), (0,))):
    total = None
    for i, j in ((2, 0), (0, 2), (1, 1), (1, 0), (0, 1), (0, 0)):
        term = lax.dot_general(a[i], b[j], (dims, ((), ())), preferred_element_type=jnp.float32)
        total = term if total is None else total + term
    return total


def estimate(flops, nbytes):
    return pl.CostEstimate(flops=flops, bytes_accessed=nbytes, transcendentals=0)


def corner_kernel(matrix_ref, block_ref, sem):
    copy = pltpu.make_async_copy(matrix_ref.at[0, :, 0, :], block_ref, sem)
    copy.start()
    copy.wait()


def corner_block(matrix):
    n = matrix.shape[1]
    return pl.pallas_call(
        corner_kernel,
        out_shape=jax.ShapeDtypeStruct((n, n), jnp.float32),
        in_specs=[HBM],
        out_specs=VMEM,
        scratch_shapes=[pltpu.SemaphoreType.DMA(())],
        compiler_params=pltpu.CompilerParams(vmem_limit_bytes=62 * MIB),
        cost_estimate=estimate(0, 3 * MIB),
        name="corner_block",
    )(matrix)


def panels_kernel(matrix_ref, column_ref, upper_ref, lower_ref, sems):
    local_cols, half, _ = upper_ref.shape
    copies = [pltpu.make_async_copy(matrix_ref.at[:, :, 0, :], column_ref, sems.at[0])]
    for j in range(local_cols):
        copies.append(pltpu.make_async_copy(matrix_ref.at[0, pl.ds(0, half), j, :], upper_ref.at[j], sems.at[1 + j]))
        copies.append(pltpu.make_async_copy(
            matrix_ref.at[0, pl.ds(half, half), j, :], lower_ref.at[j], sems.at[1 + local_cols + j]))
    for copy in copies:
        copy.start()
    for copy in copies:
        copy.wait()


def panels(matrix):
    local_rows, n, local_cols, _ = matrix.shape
    strip = jax.ShapeDtypeStruct((local_cols, n // 2, n), jnp.float32)
    return pl.pallas_call(
        panels_kernel,
        out_shape=[jax.ShapeDtypeStruct((local_rows, n, n), jnp.float32), strip, strip],
        in_specs=[HBM],
        out_specs=[VMEM] * 3,
        scratch_shapes=[pltpu.SemaphoreType.DMA((1 + 2 * local_cols,))],
        compiler_params=pltpu.CompilerParams(vmem_limit_bytes=4 * MIB),
        cost_estimate=estimate(0, 4 * MIB),
        name="panels",
    )(matrix)


def first_factor_kernel(a_ref, f_ref, w_ref, sym, aug):
    f_ref[...], w_ref[...] = eliminate(a_ref[...], sym, aug)


def first_factor(a):
    n = a.shape[1]
    square = jax.ShapeDtypeStruct((n, n), jnp.float32)
    return pl.pallas_call(
        first_factor_kernel,
        out_shape=[square, square],
        in_specs=[VMEM],
        out_specs=[VMEM, VMEM],
        scratch_shapes=[pltpu.VMEM((n // SUB, SUB, n), jnp.float32)] * 2,
        compiler_params=pltpu.CompilerParams(vmem_limit_bytes=4 * MIB),
        cost_estimate=estimate(8 * 10**9, 2 * MIB),
        name="first_factor",
    )(a)


def second_factor_kernel(low_ref, a_ref, w0_ref, matrix_ref, f_ref, w_ref, mixed_ref,
                         blocks_ref, sym, aug, sems):
    n = w0_ref.shape[0]
    local_cols = matrix_ref.shape[2]
    copies = [pltpu.make_async_copy(matrix_ref.at[:, :, j, :], blocks_ref.at[j], sems.at[j]) for j in range(local_cols)]
    for copy in copies:
        copy.start()
    odd = is_odd_row()
    w0 = w0_ref[...]
    cross = dot_t(low_ref[...], w0)
    f1, w1 = eliminate(a_ref[...] - dot_t(cross, cross), sym, aug)
    f_ref[...] = f1
    w10 = -dot(w1, dot(cross, w0))
    zero = jnp.zeros((n, n), jnp.float32)
    w_ref[:n, :n] = w0
    w_ref[:n, n:] = zero
    w_ref[n:, :n] = w10
    w_ref[n:, n:] = w1
    mixed_ref[:n, :n] = jnp.where(odd, zero, w0)
    mixed_ref[:n, n:] = jnp.where(odd, w0, zero)
    mixed_ref[n:, :n] = jnp.where(odd, w1, w10)
    mixed_ref[n:, n:] = jnp.where(odd, w10, w1)
    for copy in copies:
        copy.wait()


def second_factor(low, a, w0, matrix):
    local_rows, n, local_cols, _ = matrix.shape
    square = jax.ShapeDtypeStruct((n, n), jnp.float32)
    double = jax.ShapeDtypeStruct((2 * n, 2 * n), jnp.float32)
    blocks = jax.ShapeDtypeStruct((local_cols, local_rows, n, n), jnp.float32)
    return pl.pallas_call(
        second_factor_kernel,
        out_shape=[square, double, double, blocks],
        in_specs=[VMEM] * 3 + [HBM],
        out_specs=[VMEM] * 4,
        scratch_shapes=[pltpu.VMEM((n // SUB, SUB, n), jnp.float32)] * 2 + [pltpu.SemaphoreType.DMA((local_cols,))],
        compiler_params=pltpu.CompilerParams(vmem_limit_bytes=12 * MIB),
        cost_estimate=estimate(8 * 10**9, 4 * MIB),
        name="second_factor",
    )(low, a, w0, matrix)


def settle_kernel(f0_ref, f1_ref, w_ref, mixed_ref, rows_ref, rows_other_ref, ha_ref, hb_ref, oa_ref, ob_ref, blocks_ref,
                  out_ref, result, sems):
    grid_row = lax.axis_index("row")
    grid_col = lax.axis_index("col")
    n = f0_ref.shape[0]
    local_cols, local_rows, _, _ = blocks_ref.shape
    flat = local_rows * n
    own = rows_ref[...].reshape(flat, n)
    other = rows_other_ref[...].reshape(flat, n)
    swapped = lax.rem(grid_col, 2) == 1
    rows = jnp.concatenate([jnp.where(swapped, other, own), jnp.where(swapped, own, other)], axis=1)
    solved = dot_parts(parts(rows), parts(w_ref[...]), ((1,), (1,)))
    left = parts(solved)
    mixed = parts(mixed_ref[...])
    copies = []
    for j in range(0, local_cols, 2):
        pair = (j, j + 1)
        stacked = jnp.concatenate(
            [jnp.concatenate([ha_ref[b], hb_ref[b], oa_ref[b], ob_ref[b]], axis=0) for b in pair], axis=1)
        update = dot_parts(left, parts(dot_parts(mixed, parts(stacked))))
        for b in pair:
            part = update[:, (b - j) * n:(b - j + 1) * n].reshape(local_rows, n, n)
            result[b] = blocks_ref[b] - part
        if j == 0:
            @pl.when(grid_col == 0)
            def _():
                result[0] = solved[:, :n].reshape(local_rows, n, n)

            @pl.when(grid_col == 1)
            def _():
                result[0] = solved[:, n:].reshape(local_rows, n, n)

        @pl.when(grid_row <= 1)
        def _():
            for b in pair:
                if b > 0:
                    result[b, 0] = jnp.zeros((n, n), jnp.float32)
            if j == 0:
                @pl.when(grid_col > grid_row)
                def _():
                    result[0, 0] = jnp.zeros((n, n), jnp.float32)

                @pl.when((grid_row == 0) & (grid_col == 0))
                def _():
                    result[0, 0] = f0_ref[...]

                @pl.when((grid_row == 1) & (grid_col == 1))
                def _():
                    result[0, 0] = f1_ref[...]
        for b in pair:
            copy = pltpu.make_async_copy(result.at[b], out_ref.at[:, :, b, :], sems.at[b])
            copy.start()
            copies.append(copy)
    for copy in copies:
        copy.wait()


def settle(f0, f1, w, mixed, rows, rows_other, ha, hb, oa, ob, blocks):
    local_cols, local_rows, n, _ = blocks.shape
    return pl.pallas_call(
        settle_kernel,
        out_shape=jax.ShapeDtypeStruct((local_rows, n, local_cols, n), jnp.float32),
        in_specs=[VMEM] * 11,
        out_specs=HBM,
        scratch_shapes=[pltpu.VMEM(blocks.shape, jnp.float32), pltpu.SemaphoreType.DMA((local_cols,))],
        compiler_params=pltpu.CompilerParams(vmem_limit_bytes=32 * MIB),
        cost_estimate=estimate(4 * 10**9, 6 * MIB),
        name="settle",
    )(f0, f1, w, mixed, rows, rows_other, ha, hb, oa, ob, blocks)


def exchange(value, axis, mask, size):
    return lax.ppermute(value, axis, [(i, i ^ mask) for i in range(size)])


def bit_set(index, bit):
    return ((index >> bit) & 1) == 1


def spread(own, axis, index, size, bits):
    held = own
    for bit in bits:
        held = jnp.where(bit_set(index, bit), exchange(held, axis, 1 << bit, size), held)
    return held


def shards(kernel):
    grid_row = lax.axis_index("row")
    grid_col = lax.axis_index("col")
    n_row = lax.axis_size("row")
    n_col = lax.axis_size("col")
    n = kernel.shape[1]
    half = n // 2
    row_bits = list(range(1, n_row.bit_length() - 1))
    col_bits = list(range(1, n_col.bit_length() - 1))
    odd = (grid_row % 2) == 1

    block = corner_block(kernel)
    halves = jnp.broadcast_to(block.reshape(1, 2, half, n), (n_row // 2, 2, half, n)).reshape(n_row, half, n)
    over_row = lax.all_to_all(halves, "row", 0, 0)
    kernel_then, over_row = lax.optimization_barrier((kernel, over_row))
    pair = jnp.broadcast_to(over_row[None, :2], (n_col, 2, half, n))
    over_col = lax.all_to_all(pair, "col", 0, 0)
    mine = jnp.stack([over_col[0, 0], over_col[0, 1], over_col[1, 1]])
    other = exchange(mine, "row", 1, n_row)

    column, upper, lower = panels(kernel_then)
    ha = spread(upper, "row", grid_row, n_row, row_bits)
    hb = spread(lower, "row", grid_row, n_row, row_bits[::-1])
    rows = spread(column, "col", grid_col, n_col, col_bits)
    oa = exchange(ha, "row", 1, n_row)
    ob = exchange(hb, "row", 1, n_row)
    rows_other = exchange(rows, "col", 1, n_col)

    whole = jnp.concatenate([jnp.where(odd, other, mine), jnp.where(odd, mine, other)], axis=1)
    f0, w0 = first_factor(whole[0])
    f1, w, mixed, blocks = second_factor(whole[1], whole[2], w0, kernel)
    return settle(f0, f1, w, mixed, rows, rows_other, ha, hb, oa, ob, blocks)


def solution(mesh):
    in_specs = (P(None, "row", None, "col"),)
    out_specs = P(None, "row", None, "col")
    return jax.shard_map(shards, mesh=mesh, in_specs=in_specs, out_specs=out_specs, check_vma=False)
```

```python
import jax
import jax.numpy as jnp
from jax import lax
from jax.experimental import pallas as pl
from jax.experimental.pallas import tpu as pltpu
from jax.sharding import PartitionSpec as P

EXACT = lax.Precision.HIGHEST
SUB = 8
MIB = 1024 * 1024
VMEM = pl.BlockSpec(memory_space=pltpu.VMEM)
HBM = pl.BlockSpec(memory_space=pltpu.HBM)


def dot(a, b):
    return lax.dot_general(a, b, (((1,), (0,)), ((), ())), precision=EXACT, preferred_element_type=jnp.float32)


def dot_t(a, b):
    return lax.dot_general(a, b, (((1,), (1,)), ((), ())), precision=EXACT, preferred_element_type=jnp.float32)


def full(row):
    return jnp.broadcast_to(row, (SUB, row.shape[-1]))


def eliminate(s, sym, aug):
    n = s.shape[0]
    groups = n // SUB
    sub = lax.broadcasted_iota(jnp.int32, (SUB, n), 0)
    lane = lax.broadcasted_iota(jnp.int32, (SUB, n), 1)
    sym[...] = s.reshape(groups, SUB, n)
    rows = lax.broadcasted_iota(jnp.int32, (n, n), 0)
    cols = lax.broadcasted_iota(jnp.int32, (n, n), 1)
    aug[...] = jnp.where(rows == cols, 1.0, 0.0).reshape(groups, SUB, n)
    for g in range(groups):
        start = g * SUB
        left = groups - g
        rest = sym[g:]
        top = sym[g]
        top_aug = aug[g]
        spread = [jnp.broadcast_to(rest[:, :, start + j:start + j + 1], (left, SUB, n)) for j in range(SUB)]
        unit = {(i, j): full(spread[j][0, i:i + 1, :]) for j in range(SUB) for i in range(j, SUB)}
        scaled = []
        scaled_aug = []
        roots = jnp.zeros((SUB, n), jnp.float32)
        for k in range(SUB):
            pivot = unit[k, k]
            guess = pl.reciprocal(pivot, approx=True)
            rest_of = 2.0 - pivot * guess
            recip = guess * rest_of
            roots = jnp.where(sub == k, pivot, roots)
            for j in range(k + 1, SUB):
                unit[j, j] = unit[j, j] - (unit[j, k] * unit[j, k] * guess) * rest_of
                for i in range(j + 1, SUB):
                    unit[i, j] = unit[i, j] - (unit[i, k] * unit[j, k] * guess) * rest_of
            for j in range(k + 1, SUB):
                factor = unit[j, k] * recip
                spread[j] = spread[j] - spread[k] * factor[None]
            row = full(top[k:k + 1, :]) * recip
            row_aug = full(top_aug[k:k + 1, :]) * recip
            scaled.append(row)
            scaled_aug.append(row_aug)
            if k + 1 < SUB:
                below = jnp.where(sub > k, spread[k][0], 0.0)
                top = top - below * row
                top_aug = top_aug - below * row_aug
        root = lax.rsqrt(roots)
        sym[g] = jnp.where(lane >= start + sub, top * root, 0.0)
        aug[g] = top_aug * root
        if left > 1:
            low = rest[1:]
            low_aug = aug[g + 1:]
            for k in range(SUB):
                low = low - spread[k][1:] * scaled[k][None]
                low_aug = low_aug - spread[k][1:] * scaled_aug[k][None]
            sym[g + 1:] = low
            aug[g + 1:] = low_aug
    upper = sym[...].reshape(n, n)
    return upper.T, aug[...].reshape(n, n)


def is_odd_row():
    return lax.rem(lax.axis_index("row"), 2) == 1


def parts(x):
    high = x.astype(jnp.bfloat16)
    rest = x - high.astype(jnp.float32)
    middle = rest.astype(jnp.bfloat16)
    return high, middle, (rest - middle.astype(jnp.float32)).astype(jnp.bfloat16)


def dot_parts(a, b, dims=((1,), (0,))):
    total = None
    for i, j in ((2, 0), (0, 2), (1, 1), (1, 0), (0, 1), (0, 0)):
        term = lax.dot_general(a[i], b[j], (dims, ((), ())), preferred_element_type=jnp.float32)
        total = term if total is None else total + term
    return total


def estimate(flops, nbytes):
    return pl.CostEstimate(flops=flops, bytes_accessed=nbytes, transcendentals=0)


def corner_kernel(matrix_ref, own_ref, send_ref, sems):
    half = own_ref.shape[0]
    odd = lax.rem(lax.axis_index("row"), 2)
    own = pltpu.make_async_copy(matrix_ref.at[0, pl.ds(odd * half, half), 0, :], own_ref, sems.at[0])
    send = pltpu.make_async_copy(matrix_ref.at[0, pl.ds((1 - odd) * half, half), 0, :], send_ref, sems.at[1])
    send.start()
    own.start()
    send.wait()
    own.wait()


def corner_halves(matrix):
    n = matrix.shape[1]
    half = jax.ShapeDtypeStruct((n // 2, n), jnp.float32)
    return pl.pallas_call(
        corner_kernel,
        out_shape=[half, half],
        in_specs=[HBM],
        out_specs=[VMEM, VMEM],
        scratch_shapes=[pltpu.SemaphoreType.DMA((2,))],
        compiler_params=pltpu.CompilerParams(vmem_limit_bytes=2 * MIB),
        cost_estimate=estimate(0, 3 * MIB),
        name="corner_halves",
    )(matrix)


def panels_kernel(matrix_ref, column_ref, upper_ref, lower_ref, sems):
    local_cols, half, _ = upper_ref.shape
    copies = [pltpu.make_async_copy(matrix_ref.at[:, :, 0, :], column_ref, sems.at[0])]
    for j in range(local_cols):
        copies.append(pltpu.make_async_copy(matrix_ref.at[0, pl.ds(0, half), j, :], upper_ref.at[j], sems.at[1 + j]))
        copies.append(pltpu.make_async_copy(
            matrix_ref.at[0, pl.ds(half, half), j, :], lower_ref.at[j], sems.at[1 + local_cols + j]))
    for copy in copies:
        copy.start()
    for copy in copies:
        copy.wait()


def panels(matrix):
    local_rows, n, local_cols, _ = matrix.shape
    strip = jax.ShapeDtypeStruct((local_cols, n // 2, n), jnp.float32)
    return pl.pallas_call(
        panels_kernel,
        out_shape=[jax.ShapeDtypeStruct((local_rows, n, n), jnp.float32), strip, strip],
        in_specs=[HBM],
        out_specs=[VMEM] * 3,
        scratch_shapes=[pltpu.SemaphoreType.DMA((1 + 2 * local_cols,))],
        compiler_params=pltpu.CompilerParams(vmem_limit_bytes=4 * MIB),
        cost_estimate=estimate(0, 4 * MIB),
        name="panels",
    )(matrix)


def first_factor_kernel(a_ref, f_ref, w_ref, sym, aug):
    f_ref[...], w_ref[...] = eliminate(a_ref[...], sym, aug)


def first_factor(a):
    n = a.shape[1]
    square = jax.ShapeDtypeStruct((n, n), jnp.float32)
    return pl.pallas_call(
        first_factor_kernel,
        out_shape=[square, square],
        in_specs=[VMEM],
        out_specs=[VMEM, VMEM],
        scratch_shapes=[pltpu.VMEM((n // SUB, SUB, n), jnp.float32)] * 2,
        compiler_params=pltpu.CompilerParams(vmem_limit_bytes=4 * MIB),
        cost_estimate=estimate(8 * 10**9, 2 * MIB),
        name="first_factor",
    )(a)


def second_factor_kernel(low_ref, a_ref, w0_ref, matrix_ref, f_ref, w_ref, mixed_ref,
                         blocks_ref, sym, aug, sems):
    n = w0_ref.shape[0]
    local_cols = matrix_ref.shape[2]
    copies = [pltpu.make_async_copy(matrix_ref.at[:, :, j, :], blocks_ref.at[j], sems.at[j]) for j in range(local_cols)]
    for copy in copies:
        copy.start()
    odd = is_odd_row()
    w0 = w0_ref[...]
    cross = dot_t(low_ref[...], w0)
    f1, w1 = eliminate(a_ref[...] - dot_t(cross, cross), sym, aug)
    f_ref[...] = f1
    w10 = -dot(w1, dot(cross, w0))
    zero = jnp.zeros((n, n), jnp.float32)
    w_ref[:n, :n] = w0
    w_ref[:n, n:] = zero
    w_ref[n:, :n] = w10
    w_ref[n:, n:] = w1
    mixed_ref[:n, :n] = jnp.where(odd, zero, w0)
    mixed_ref[:n, n:] = jnp.where(odd, w0, zero)
    mixed_ref[n:, :n] = jnp.where(odd, w1, w10)
    mixed_ref[n:, n:] = jnp.where(odd, w10, w1)
    for copy in copies:
        copy.wait()


def second_factor(low, a, w0, matrix):
    local_rows, n, local_cols, _ = matrix.shape
    square = jax.ShapeDtypeStruct((n, n), jnp.float32)
    double = jax.ShapeDtypeStruct((2 * n, 2 * n), jnp.float32)
    blocks = jax.ShapeDtypeStruct((local_cols, local_rows, n, n), jnp.float32)
    return pl.pallas_call(
        second_factor_kernel,
        out_shape=[square, double, double, blocks],
        in_specs=[VMEM] * 3 + [HBM],
        out_specs=[VMEM] * 4,
        scratch_shapes=[pltpu.VMEM((n // SUB, SUB, n), jnp.float32)] * 2 + [pltpu.SemaphoreType.DMA((local_cols,))],
        compiler_params=pltpu.CompilerParams(vmem_limit_bytes=12 * MIB),
        cost_estimate=estimate(8 * 10**9, 4 * MIB),
        name="second_factor",
    )(low, a, w0, matrix)


def settle_kernel(f0_ref, f1_ref, w_ref, mixed_ref, rows_ref, rows_other_ref, ha_ref, hb_ref, oa_ref, ob_ref, blocks_ref,
                  out_ref, result, sems):
    grid_row = lax.axis_index("row")
    grid_col = lax.axis_index("col")
    n = f0_ref.shape[0]
    local_cols, local_rows, _, _ = blocks_ref.shape
    flat = local_rows * n
    own = rows_ref[...].reshape(flat, n)
    other = rows_other_ref[...].reshape(flat, n)
    swapped = lax.rem(grid_col, 2) == 1
    rows = jnp.concatenate([jnp.where(swapped, other, own), jnp.where(swapped, own, other)], axis=1)
    solved = dot_parts(parts(rows), parts(w_ref[...]), ((1,), (1,)))
    left = parts(solved)
    mixed = parts(mixed_ref[...])
    copies = []
    for j in range(0, local_cols, 2):
        pair = (j, j + 1)
        stacked = jnp.concatenate(
            [jnp.concatenate([ha_ref[b], hb_ref[b], oa_ref[b], ob_ref[b]], axis=0) for b in pair], axis=1)
        update = dot_parts(left, parts(dot_parts(mixed, parts(stacked))))
        for b in pair:
            part = update[:, (b - j) * n:(b - j + 1) * n].reshape(local_rows, n, n)
            result[b] = blocks_ref[b] - part
        if j == 0:
            @pl.when(grid_col == 0)
            def _():
                result[0] = solved[:, :n].reshape(local_rows, n, n)

            @pl.when(grid_col == 1)
            def _():
                result[0] = solved[:, n:].reshape(local_rows, n, n)

        @pl.when(grid_row <= 1)
        def _():
            for b in pair:
                if b > 0:
                    result[b, 0] = jnp.zeros((n, n), jnp.float32)
            if j == 0:
                @pl.when(grid_col > grid_row)
                def _():
                    result[0, 0] = jnp.zeros((n, n), jnp.float32)

                @pl.when((grid_row == 0) & (grid_col == 0))
                def _():
                    result[0, 0] = f0_ref[...]

                @pl.when((grid_row == 1) & (grid_col == 1))
                def _():
                    result[0, 0] = f1_ref[...]
        for b in pair:
            copy = pltpu.make_async_copy(result.at[b], out_ref.at[:, :, b, :], sems.at[b])
            copy.start()
            copies.append(copy)
    for copy in copies:
        copy.wait()


def settle(f0, f1, w, mixed, rows, rows_other, ha, hb, oa, ob, blocks):
    local_cols, local_rows, n, _ = blocks.shape
    return pl.pallas_call(
        settle_kernel,
        out_shape=jax.ShapeDtypeStruct((local_rows, n, local_cols, n), jnp.float32),
        in_specs=[VMEM] * 11,
        out_specs=HBM,
        scratch_shapes=[pltpu.VMEM(blocks.shape, jnp.float32), pltpu.SemaphoreType.DMA((local_cols,))],
        compiler_params=pltpu.CompilerParams(vmem_limit_bytes=32 * MIB),
        cost_estimate=estimate(4 * 10**9, 6 * MIB),
        name="settle",
    )(f0, f1, w, mixed, rows, rows_other, ha, hb, oa, ob, blocks)


def exchange(value, axis, mask, size):
    return lax.ppermute(value, axis, [(i, i ^ mask) for i in range(size)])


def bit_set(index, bit):
    return ((index >> bit) & 1) == 1


def spread(own, axis, index, size, bits):
    held = own
    for bit in bits:
        held = jnp.where(bit_set(index, bit), exchange(held, axis, 1 << bit, size), held)
    return held


def after(value, *others):
    return lax.optimization_barrier((value,) + others)


def shards(kernel):
    grid_row = lax.axis_index("row")
    grid_col = lax.axis_index("col")
    n_row = lax.axis_size("row")
    n_col = lax.axis_size("col")
    row_bits = list(range(1, n_row.bit_length() - 1))
    col_bits = list(range(1, n_col.bit_length() - 1))
    odd = (grid_row % 2) == 1
    right = (grid_col % 2) == 1

    own, send = corner_halves(kernel)
    got = exchange(send, "row", 1, n_row)
    pair = jnp.stack([jnp.where(odd != right, got, own), jnp.where(odd, own, got)])
    column, upper, lower = panels(kernel)
    pair = spread(pair, "row", grid_row, n_row, row_bits)
    pair, upper, lower = after(pair, upper, lower)
    pair = spread(pair, "col", grid_col, n_col, col_bits)
    ha = spread(upper, "row", grid_row, n_row, row_bits[:1])
    hb = spread(lower, "row", grid_row, n_row, row_bits[:0:-1])
    pair_far = exchange(pair, "col", 1, n_col)
    pair_far, column = after(pair_far, column)
    rows = spread(column, "col", grid_col, n_col, col_bits[:1])
    mine = jnp.stack([jnp.where(right, pair_far[0], pair[0]), jnp.where(right, pair_far[1], pair[1]),
                      jnp.where(right, pair[0], pair_far[0])])
    other = exchange(mine, "row", 1, n_row)
    mine, other, ha, hb = after(mine, other, ha, hb)

    ha = spread(ha, "row", grid_row, n_row, row_bits[1:])
    hb = spread(hb, "row", grid_row, n_row, row_bits[:1])
    whole = jnp.concatenate([jnp.where(odd, other, mine), jnp.where(odd, mine, other)], axis=1)
    f0, w0 = first_factor(whole[0])
    w0, rows, ha, hb = after(w0, rows, ha, hb)
    rows = spread(rows, "col", grid_col, n_col, col_bits[1:])
    oa = exchange(ha, "row", 1, n_row)
    ob = exchange(hb, "row", 1, n_row)
    rows_other = exchange(rows, "col", 1, n_col)

    f1, w, mixed, blocks = second_factor(whole[1], whole[2], w0, kernel)
    return settle(f0, f1, w, mixed, rows, rows_other, ha, hb, oa, ob, blocks)


def solution(mesh):
    in_specs = (P(None, "row", None, "col"),)
    out_specs = P(None, "row", None, "col")
    return jax.shard_map(shards, mesh=mesh, in_specs=in_specs, out_specs=out_specs, check_vma=False)
```

```python
import jax
import jax.numpy as jnp
from jax import lax
from jax.experimental import pallas as pl
from jax.experimental.pallas import tpu as pltpu
from jax.sharding import PartitionSpec as P

EXACT = lax.Precision.HIGHEST
SUB = 8
MIB = 1024 * 1024
VMEM = pl.BlockSpec(memory_space=pltpu.VMEM)
HBM = pl.BlockSpec(memory_space=pltpu.HBM)


def dot(a, b):
    return lax.dot_general(a, b, (((1,), (0,)), ((), ())), precision=EXACT, preferred_element_type=jnp.float32)


def dot_t(a, b):
    return lax.dot_general(a, b, (((1,), (1,)), ((), ())), precision=EXACT, preferred_element_type=jnp.float32)


def full(row):
    return jnp.broadcast_to(row, (SUB, row.shape[-1]))


def eliminate(s, sym, aug):
    n = s.shape[0]
    groups = n // SUB
    sub = lax.broadcasted_iota(jnp.int32, (SUB, n), 0)
    lane = lax.broadcasted_iota(jnp.int32, (SUB, n), 1)
    sym[...] = s.reshape(groups, SUB, n)
    rows = lax.broadcasted_iota(jnp.int32, (n, n), 0)
    cols = lax.broadcasted_iota(jnp.int32, (n, n), 1)
    aug[...] = jnp.where(rows == cols, 1.0, 0.0).reshape(groups, SUB, n)
    for g in range(groups):
        start = g * SUB
        left = groups - g
        rest = sym[g:]
        top = sym[g]
        top_aug = aug[g]
        spread = [jnp.broadcast_to(rest[:, :, start + j:start + j + 1], (left, SUB, n)) for j in range(SUB)]
        unit = {(i, j): full(spread[j][0, i:i + 1, :]) for j in range(SUB) for i in range(j, SUB)}
        scaled = []
        scaled_aug = []
        roots = jnp.zeros((SUB, n), jnp.float32)
        for k in range(SUB):
            pivot = unit[k, k]
            guess = pl.reciprocal(pivot, approx=True)
            rest_of = 2.0 - pivot * guess
            recip = guess * rest_of
            roots = jnp.where(sub == k, pivot, roots)
            for j in range(k + 1, SUB):
                unit[j, j] = unit[j, j] - (unit[j, k] * unit[j, k] * guess) * rest_of
                for i in range(j + 1, SUB):
                    unit[i, j] = unit[i, j] - (unit[i, k] * unit[j, k] * guess) * rest_of
            for j in range(k + 1, SUB):
                factor = unit[j, k] * recip
                spread[j] = spread[j] - spread[k] * factor[None]
            row = full(top[k:k + 1, :]) * recip
            row_aug = full(top_aug[k:k + 1, :]) * recip
            scaled.append(row)
            scaled_aug.append(row_aug)
            if k + 1 < SUB:
                below = jnp.where(sub > k, spread[k][0], 0.0)
                top = top - below * row
                top_aug = top_aug - below * row_aug
        root = lax.rsqrt(roots)
        sym[g] = jnp.where(lane >= start + sub, top * root, 0.0)
        aug[g] = top_aug * root
        if left > 1:
            low = rest[1:]
            low_aug = aug[g + 1:]
            for k in range(SUB):
                low = low - spread[k][1:] * scaled[k][None]
                low_aug = low_aug - spread[k][1:] * scaled_aug[k][None]
            sym[g + 1:] = low
            aug[g + 1:] = low_aug
    upper = sym[...].reshape(n, n)
    return upper.T, aug[...].reshape(n, n)


def parts(x):
    high = x.astype(jnp.bfloat16)
    rest = x - high.astype(jnp.float32)
    middle = rest.astype(jnp.bfloat16)
    return high, middle, (rest - middle.astype(jnp.float32)).astype(jnp.bfloat16)


def dot_parts(a, b, dims=((1,), (0,))):
    total = None
    for i, j in ((2, 0), (0, 2), (1, 1), (1, 0), (0, 1), (0, 0)):
        term = lax.dot_general(a[i], b[j], (dims, ((), ())), preferred_element_type=jnp.float32)
        total = term if total is None else total + term
    return total


def estimate(flops, nbytes):
    return pl.CostEstimate(flops=flops, bytes_accessed=nbytes, transcendentals=0)


def corner_kernel(matrix_ref, own_ref, send_ref, sems):
    half = own_ref.shape[0]
    odd = lax.rem(lax.axis_index("row"), 2)
    own = pltpu.make_async_copy(matrix_ref.at[0, pl.ds(odd * half, half), 0, :], own_ref, sems.at[0])
    send = pltpu.make_async_copy(matrix_ref.at[0, pl.ds((1 - odd) * half, half), 0, :], send_ref, sems.at[1])
    send.start()
    own.start()
    send.wait()
    own.wait()


def corner_halves(matrix):
    n = matrix.shape[1]
    half = jax.ShapeDtypeStruct((n // 2, n), jnp.float32)
    return pl.pallas_call(
        corner_kernel,
        out_shape=[half, half],
        in_specs=[HBM],
        out_specs=[VMEM, VMEM],
        scratch_shapes=[pltpu.SemaphoreType.DMA((2,))],
        compiler_params=pltpu.CompilerParams(vmem_limit_bytes=2 * MIB),
        cost_estimate=estimate(0, 3 * MIB),
        name="corner_halves",
    )(matrix)


def panels_kernel(matrix_ref, column_ref, upper_ref, lower_ref, sems):
    local_cols, half, _ = upper_ref.shape
    copies = [pltpu.make_async_copy(matrix_ref.at[:, :, 0, :], column_ref, sems.at[0])]
    for j in range(local_cols):
        copies.append(pltpu.make_async_copy(matrix_ref.at[0, pl.ds(0, half), j, :], upper_ref.at[j], sems.at[1 + j]))
        copies.append(pltpu.make_async_copy(
            matrix_ref.at[0, pl.ds(half, half), j, :], lower_ref.at[j], sems.at[1 + local_cols + j]))
    for copy in copies:
        copy.start()
    for copy in copies:
        copy.wait()


def panels(matrix):
    local_rows, n, local_cols, _ = matrix.shape
    strip = jax.ShapeDtypeStruct((local_cols, n // 2, n), jnp.float32)
    return pl.pallas_call(
        panels_kernel,
        out_shape=[jax.ShapeDtypeStruct((local_rows, n, n), jnp.float32), strip, strip],
        in_specs=[HBM],
        out_specs=[VMEM] * 3,
        scratch_shapes=[pltpu.SemaphoreType.DMA((1 + 2 * local_cols,))],
        compiler_params=pltpu.CompilerParams(vmem_limit_bytes=4 * MIB),
        cost_estimate=estimate(0, 4 * MIB),
        name="panels",
    )(matrix)


def first_factor_kernel(a_ref, f_ref, w_ref, sym, aug):
    f_ref[...], w_ref[...] = eliminate(a_ref[...], sym, aug)


def first_factor(a):
    n = a.shape[1]
    square = jax.ShapeDtypeStruct((n, n), jnp.float32)
    return pl.pallas_call(
        first_factor_kernel,
        out_shape=[square, square],
        in_specs=[VMEM],
        out_specs=[VMEM, VMEM],
        scratch_shapes=[pltpu.VMEM((n // SUB, SUB, n), jnp.float32)] * 2,
        compiler_params=pltpu.CompilerParams(vmem_limit_bytes=4 * MIB),
        cost_estimate=estimate(8 * 10**9, 2 * MIB),
        name="first_factor",
    )(a)


def second_factor_kernel(low_ref, a_ref, w0_ref, matrix_ref, f_ref, w_ref,
                         blocks_ref, sym, aug, sems):
    n = w0_ref.shape[0]
    local_cols = matrix_ref.shape[2]
    copies = [pltpu.make_async_copy(matrix_ref.at[:, :, j, :], blocks_ref.at[j], sems.at[j]) for j in range(local_cols)]
    for copy in copies:
        copy.start()
    w0 = w0_ref[...]
    cross = dot_t(low_ref[...], w0)
    f1, w1 = eliminate(a_ref[...] - dot_t(cross, cross), sym, aug)
    f_ref[...] = f1
    w10 = -dot(w1, dot(cross, w0))
    zero = jnp.zeros((n, n), jnp.float32)
    w_ref[:n, :n] = w0
    w_ref[:n, n:] = zero
    w_ref[n:, :n] = w10
    w_ref[n:, n:] = w1
    for copy in copies:
        copy.wait()


def second_factor(low, a, w0, matrix):
    local_rows, n, local_cols, _ = matrix.shape
    square = jax.ShapeDtypeStruct((n, n), jnp.float32)
    double = jax.ShapeDtypeStruct((2 * n, 2 * n), jnp.float32)
    blocks = jax.ShapeDtypeStruct((local_cols, local_rows, n, n), jnp.float32)
    return pl.pallas_call(
        second_factor_kernel,
        out_shape=[square, double, blocks],
        in_specs=[VMEM] * 3 + [HBM],
        out_specs=[VMEM] * 3,
        scratch_shapes=[pltpu.VMEM((n // SUB, SUB, n), jnp.float32)] * 2 + [pltpu.SemaphoreType.DMA((local_cols,))],
        compiler_params=pltpu.CompilerParams(vmem_limit_bytes=12 * MIB),
        cost_estimate=estimate(8 * 10**9, 4 * MIB),
        name="second_factor",
    )(low, a, w0, matrix)


def settle_kernel(f0_ref, f1_ref, w_ref, rows_ref, tops_ref, blocks_ref, out_ref, result, sems):
    grid_row = lax.axis_index("row")
    grid_col = lax.axis_index("col")
    n = f0_ref.shape[0]
    local_cols, local_rows, _, _ = blocks_ref.shape
    flat = local_rows * n
    w = parts(w_ref[...])
    rows = jnp.concatenate([rows_ref[0].reshape(flat, n), rows_ref[1].reshape(flat, n)], axis=1)
    solved = dot_parts(parts(rows), w, ((1,), (1,)))
    left = parts(solved)
    copies = []
    for j in range(0, local_cols, 2):
        pair = (j, j + 1)
        stacked = jnp.concatenate(
            [jnp.concatenate([tops_ref[0, 0, b], tops_ref[0, 1, b], tops_ref[1, 0, b], tops_ref[1, 1, b]], axis=0) for b in pair], axis=1)
        update = dot_parts(left, parts(dot_parts(w, parts(stacked))))
        for b in pair:
            part = update[:, (b - j) * n:(b - j + 1) * n].reshape(local_rows, n, n)
            result[b] = blocks_ref[b] - part
        if j == 0:
            @pl.when(grid_col == 0)
            def _():
                result[0] = solved[:, :n].reshape(local_rows, n, n)

            @pl.when(grid_col == 1)
            def _():
                result[0] = solved[:, n:].reshape(local_rows, n, n)

        @pl.when(grid_row <= 1)
        def _():
            for b in pair:
                if b > 0:
                    result[b, 0] = jnp.zeros((n, n), jnp.float32)
            if j == 0:
                @pl.when(grid_col > grid_row)
                def _():
                    result[0, 0] = jnp.zeros((n, n), jnp.float32)

                @pl.when((grid_row == 0) & (grid_col == 0))
                def _():
                    result[0, 0] = f0_ref[...]

                @pl.when((grid_row == 1) & (grid_col == 1))
                def _():
                    result[0, 0] = f1_ref[...]
        for b in pair:
            copy = pltpu.make_async_copy(result.at[b], out_ref.at[:, :, b, :], sems.at[b])
            copy.start()
            copies.append(copy)
    for copy in copies:
        copy.wait()


def settle(f0, f1, w, rows, tops, blocks):
    local_cols, local_rows, n, _ = blocks.shape
    return pl.pallas_call(
        settle_kernel,
        out_shape=jax.ShapeDtypeStruct((local_rows, n, local_cols, n), jnp.float32),
        in_specs=[VMEM] * 6,
        out_specs=HBM,
        scratch_shapes=[pltpu.VMEM(blocks.shape, jnp.float32), pltpu.SemaphoreType.DMA((local_cols,))],
        compiler_params=pltpu.CompilerParams(vmem_limit_bytes=32 * MIB),
        cost_estimate=estimate(4 * 10**9, 6 * MIB),
        name="settle",
    )(f0, f1, w, rows, tops, blocks)


def exchange(value, axis, mask, size):
    return lax.ppermute(value, axis, [(i, i ^ mask) for i in range(size)])


def gathered(value, axis, mask, size):
    groups = [[i, i ^ mask] for i in range(size) if not i & mask]
    return lax.all_gather(value, axis, axis_index_groups=groups)


def spread_gathered(own, axis, size, bits):
    for bit in bits:
        own = gathered(own, axis, 1 << bit, size)[0]
    return own


def bit_set(index, bit):
    return ((index >> bit) & 1) == 1


def spread(own, axis, index, size, bits):
    held = own
    for bit in bits:
        held = jnp.where(bit_set(index, bit), exchange(held, axis, 1 << bit, size), held)
    return held


def after(value, *others):
    return lax.optimization_barrier((value,) + others)


def shards(kernel):
    grid_row = lax.axis_index("row")
    grid_col = lax.axis_index("col")
    n_row = lax.axis_size("row")
    n_col = lax.axis_size("col")
    row_bits = list(range(1, n_row.bit_length() - 1))
    col_bits = list(range(1, n_col.bit_length() - 1))
    odd = (grid_row % 2) == 1
    right = (grid_col % 2) == 1

    own, send = corner_halves(kernel)
    column, upper, lower = panels(kernel)
    ha = spread_gathered(upper, "row", n_row, row_bits)
    hb = spread_gathered(lower, "row", n_row, row_bits[::-1])
    rows = lax.all_gather(column, "col")
    got = exchange(send, "row", 1, n_row)
    pair = jnp.stack([jnp.where(odd != right, got, own), jnp.where(odd, own, got)])
    pair = spread(pair, "row", grid_row, n_row, row_bits)
    pair = spread(pair, "col", grid_col, n_col, col_bits)
    pair_far = exchange(pair, "col", 1, n_col)
    mine = jnp.stack([jnp.where(right, pair_far[0], pair[0]), jnp.where(right, pair_far[1], pair[1]),
                      jnp.where(right, pair[0], pair_far[0])])
    other = exchange(mine, "row", 1, n_row)

    whole = jnp.concatenate([jnp.where(odd, other, mine), jnp.where(odd, mine, other)], axis=1)
    f0, w0 = first_factor(whole[0])
    w0, ha, hb = after(w0, ha, hb)
    tops = gathered(jnp.stack([ha, hb]), "row", 1, n_row)
    f1, w, blocks = second_factor(whole[1], whole[2], w0, kernel)
    return settle(f0, f1, w, rows, tops, blocks)


def solution(mesh):
    in_specs = (P(None, "row", None, "col"),)
    out_specs = P(None, "row", None, "col")
    return jax.shard_map(shards, mesh=mesh, in_specs=in_specs, out_specs=out_specs, check_vma=False)
```

```python
import jax
import jax.numpy as jnp
from jax import lax
from jax.experimental import pallas as pl
from jax.experimental.pallas import tpu as pltpu
from jax.sharding import PartitionSpec as P

EXACT = lax.Precision.HIGHEST
SUB = 8
MIB = 1024 * 1024
VMEM = pl.BlockSpec(memory_space=pltpu.VMEM)
HBM = pl.BlockSpec(memory_space=pltpu.HBM)


def dot(a, b):
    return lax.dot_general(a, b, (((1,), (0,)), ((), ())), precision=EXACT, preferred_element_type=jnp.float32)


def dot_t(a, b):
    return lax.dot_general(a, b, (((1,), (1,)), ((), ())), precision=EXACT, preferred_element_type=jnp.float32)


def full(row):
    return jnp.broadcast_to(row, (SUB, row.shape[-1]))


def eliminate(s, sym, aug):
    n = s.shape[0]
    groups = n // SUB
    sub = lax.broadcasted_iota(jnp.int32, (SUB, n), 0)
    lane = lax.broadcasted_iota(jnp.int32, (SUB, n), 1)
    sym[...] = s.reshape(groups, SUB, n)
    rows = lax.broadcasted_iota(jnp.int32, (n, n), 0)
    cols = lax.broadcasted_iota(jnp.int32, (n, n), 1)
    aug[...] = jnp.where(rows == cols, 1.0, 0.0).reshape(groups, SUB, n)
    for g in range(groups):
        start = g * SUB
        left = groups - g
        rest = sym[g:]
        top = sym[g]
        top_aug = aug[g]
        spread = [jnp.broadcast_to(rest[:, :, start + j:start + j + 1], (left, SUB, n)) for j in range(SUB)]
        unit = {(i, j): full(spread[j][0, i:i + 1, :]) for j in range(SUB) for i in range(j, SUB)}
        scaled = []
        scaled_aug = []
        roots = jnp.zeros((SUB, n), jnp.float32)
        for k in range(SUB):
            pivot = unit[k, k]
            guess = pl.reciprocal(pivot, approx=True)
            rest_of = 2.0 - pivot * guess
            recip = guess * rest_of
            roots = jnp.where(sub == k, pivot, roots)
            for j in range(k + 1, SUB):
                unit[j, j] = unit[j, j] - (unit[j, k] * unit[j, k] * guess) * rest_of
                for i in range(j + 1, SUB):
                    unit[i, j] = unit[i, j] - (unit[i, k] * unit[j, k] * guess) * rest_of
            for j in range(k + 1, SUB):
                factor = unit[j, k] * recip
                spread[j] = spread[j] - spread[k] * factor[None]
            row = full(top[k:k + 1, :]) * recip
            row_aug = full(top_aug[k:k + 1, :]) * recip
            scaled.append(row)
            scaled_aug.append(row_aug)
            if k + 1 < SUB:
                below = jnp.where(sub > k, spread[k][0], 0.0)
                top = top - below * row
                top_aug = top_aug - below * row_aug
        root = lax.rsqrt(roots)
        sym[g] = jnp.where(lane >= start + sub, top * root, 0.0)
        aug[g] = top_aug * root
        if left > 1:
            low = rest[1:]
            low_aug = aug[g + 1:]
            for k in range(SUB):
                low = low - spread[k][1:] * scaled[k][None]
                low_aug = low_aug - spread[k][1:] * scaled_aug[k][None]
            sym[g + 1:] = low
            aug[g + 1:] = low_aug
    upper = sym[...].reshape(n, n)
    return upper.T, aug[...].reshape(n, n)


def is_odd_row():
    return lax.rem(lax.axis_index("row"), 2) == 1


def parts(x):
    high = x.astype(jnp.bfloat16)
    rest = x - high.astype(jnp.float32)
    middle = rest.astype(jnp.bfloat16)
    return high, middle, (rest - middle.astype(jnp.float32)).astype(jnp.bfloat16)


def dot_parts(a, b):
    lhs = jnp.concatenate([a[2], a[0], a[1], a[1], a[0], a[0]], axis=1)
    rhs = jnp.concatenate([b[0], b[2], b[1], b[0], b[1], b[0]], axis=0)
    return jnp.dot(lhs, rhs, preferred_element_type=jnp.float32)


def estimate(flops, nbytes):
    return pl.CostEstimate(flops=flops, bytes_accessed=nbytes, transcendentals=0)


def corner_kernel(matrix_ref, block_ref, sem):
    copy = pltpu.make_async_copy(matrix_ref.at[0, :, 0, :], block_ref, sem)
    copy.start()
    copy.wait()


def corner_block(matrix):
    n = matrix.shape[1]
    return pl.pallas_call(
        corner_kernel,
        out_shape=jax.ShapeDtypeStruct((n, n), jnp.float32),
        in_specs=[HBM],
        out_specs=VMEM,
        scratch_shapes=[pltpu.SemaphoreType.DMA(())],
        compiler_params=pltpu.CompilerParams(vmem_limit_bytes=2 * MIB),
        cost_estimate=estimate(0, 3 * MIB),
        name="corner_block",
    )(matrix)


def panels_kernel(matrix_ref, column_ref, upper_ref, lower_ref, sems):
    local_cols, half, _ = upper_ref.shape
    copies = [pltpu.make_async_copy(matrix_ref.at[:, :, 0, :], column_ref, sems.at[0])]
    for j in range(local_cols):
        copies.append(pltpu.make_async_copy(matrix_ref.at[0, pl.ds(0, half), j, :], upper_ref.at[j], sems.at[1 + j]))
        copies.append(pltpu.make_async_copy(
            matrix_ref.at[0, pl.ds(half, half), j, :], lower_ref.at[j], sems.at[1 + local_cols + j]))
    for copy in copies:
        copy.start()
    for copy in copies:
        copy.wait()


def panels(matrix):
    local_rows, n, local_cols, _ = matrix.shape
    strip = jax.ShapeDtypeStruct((local_cols, n // 2, n), jnp.float32)
    return pl.pallas_call(
        panels_kernel,
        out_shape=[jax.ShapeDtypeStruct((local_rows, n, n), jnp.float32), strip, strip],
        in_specs=[HBM],
        out_specs=[VMEM] * 3,
        scratch_shapes=[pltpu.SemaphoreType.DMA((1 + 2 * local_cols,))],
        compiler_params=pltpu.CompilerParams(vmem_limit_bytes=4 * MIB),
        cost_estimate=estimate(0, 4 * MIB),
        name="panels",
    )(matrix)


def first_factor_kernel(a_ref, f_ref, w_ref, sym, aug):
    f_ref[...], w_ref[...] = eliminate(a_ref[...], sym, aug)


def first_factor(a):
    n = a.shape[1]
    square = jax.ShapeDtypeStruct((n, n), jnp.float32)
    return pl.pallas_call(
        first_factor_kernel,
        out_shape=[square, square],
        in_specs=[VMEM],
        out_specs=[VMEM, VMEM],
        scratch_shapes=[pltpu.VMEM((n // SUB, SUB, n), jnp.float32)] * 2,
        compiler_params=pltpu.CompilerParams(vmem_limit_bytes=4 * MIB),
        cost_estimate=estimate(8 * 10**9, 2 * MIB),
        name="first_factor",
    )(a)


def second_factor_kernel(low_ref, a_ref, w0_ref, matrix_ref, f_ref, w_ref, mixed_ref,
                         blocks_ref, sym, aug, sems):
    n = w0_ref.shape[0]
    local_cols = matrix_ref.shape[2]
    copies = [pltpu.make_async_copy(matrix_ref.at[:, :, j, :], blocks_ref.at[j], sems.at[j]) for j in range(local_cols)]
    for copy in copies:
        copy.start()
    odd = is_odd_row()
    w0 = w0_ref[...]
    cross = dot_t(low_ref[...], w0)
    f1, w1 = eliminate(a_ref[...] - dot_t(cross, cross), sym, aug)
    f_ref[...] = f1
    w10 = -dot(w1, dot(cross, w0))
    zero = jnp.zeros((n, n), jnp.float32)
    w_ref[:n, :n] = w0
    w_ref[:n, n:] = zero
    w_ref[n:, :n] = w10
    w_ref[n:, n:] = w1
    mixed_ref[:n, :n] = jnp.where(odd, zero, w0)
    mixed_ref[:n, n:] = jnp.where(odd, w0, zero)
    mixed_ref[n:, :n] = jnp.where(odd, w1, w10)
    mixed_ref[n:, n:] = jnp.where(odd, w10, w1)
    for copy in copies:
        copy.wait()


def second_factor(low, a, w0, matrix):
    local_rows, n, local_cols, _ = matrix.shape
    square = jax.ShapeDtypeStruct((n, n), jnp.float32)
    double = jax.ShapeDtypeStruct((2 * n, 2 * n), jnp.float32)
    blocks = jax.ShapeDtypeStruct((local_cols, local_rows, n, n), jnp.float32)
    return pl.pallas_call(
        second_factor_kernel,
        out_shape=[square, double, double, blocks],
        in_specs=[VMEM] * 3 + [HBM],
        out_specs=[VMEM] * 4,
        scratch_shapes=[pltpu.VMEM((n // SUB, SUB, n), jnp.float32)] * 2 + [pltpu.SemaphoreType.DMA((local_cols,))],
        compiler_params=pltpu.CompilerParams(vmem_limit_bytes=12 * MIB),
        cost_estimate=estimate(8 * 10**9, 4 * MIB),
        name="second_factor",
    )(low, a, w0, matrix)


def settle_kernel(f0_ref, f1_ref, w_ref, mixed_ref, rows_ref, rows_other_ref, ha_ref, hb_ref, oa_ref, ob_ref, blocks_ref,
                  out_ref, result, sems):
    grid_row = lax.axis_index("row")
    grid_col = lax.axis_index("col")
    n = f0_ref.shape[0]
    local_cols, local_rows, _, _ = blocks_ref.shape
    flat = local_rows * n
    own = rows_ref[...].reshape(flat, n)
    other = rows_other_ref[...].reshape(flat, n)
    swapped = lax.rem(grid_col, 2) == 1
    rows = jnp.concatenate([jnp.where(swapped, other, own), jnp.where(swapped, own, other)], axis=1)
    solved = dot_parts(parts(rows), parts(w_ref[...].T))
    left = parts(solved)
    mixed = parts(mixed_ref[...])
    copies = []
    for j in range(0, local_cols, 2):
        pair = (j, j + 1)
        stacked = jnp.concatenate(
            [jnp.concatenate([ha_ref[b], hb_ref[b], oa_ref[b], ob_ref[b]], axis=0) for b in pair], axis=1)
        update = dot_parts(left, parts(dot_parts(mixed, parts(stacked))))
        for b in pair:
            part = update[:, (b - j) * n:(b - j + 1) * n].reshape(local_rows, n, n)
            result[b] = blocks_ref[b] - part
        if j == 0:
            @pl.when(grid_col == 0)
            def _():
                result[0] = solved[:, :n].reshape(local_rows, n, n)

            @pl.when(grid_col == 1)
            def _():
                result[0] = solved[:, n:].reshape(local_rows, n, n)

        @pl.when(grid_row <= 1)
        def _():
            for b in pair:
                if b > 0:
                    result[b, 0] = jnp.zeros((n, n), jnp.float32)
            if j == 0:
                @pl.when(grid_col > grid_row)
                def _():
                    result[0, 0] = jnp.zeros((n, n), jnp.float32)

                @pl.when((grid_row == 0) & (grid_col == 0))
                def _():
                    result[0, 0] = f0_ref[...]

                @pl.when((grid_row == 1) & (grid_col == 1))
                def _():
                    result[0, 0] = f1_ref[...]
        for b in pair:
            copy = pltpu.make_async_copy(result.at[b], out_ref.at[:, :, b, :], sems.at[b])
            copy.start()
            copies.append(copy)
    for copy in copies:
        copy.wait()


def settle(f0, f1, w, mixed, rows, rows_other, ha, hb, oa, ob, blocks):
    local_cols, local_rows, n, _ = blocks.shape
    return pl.pallas_call(
        settle_kernel,
        out_shape=jax.ShapeDtypeStruct((local_rows, n, local_cols, n), jnp.float32),
        in_specs=[VMEM] * 11,
        out_specs=HBM,
        scratch_shapes=[pltpu.VMEM(blocks.shape, jnp.float32), pltpu.SemaphoreType.DMA((local_cols,))],
        compiler_params=pltpu.CompilerParams(vmem_limit_bytes=32 * MIB),
        cost_estimate=estimate(4 * 10**9, 6 * MIB),
        name="settle",
    )(f0, f1, w, mixed, rows, rows_other, ha, hb, oa, ob, blocks)


def exchange(value, axis, mask, size):
    return lax.ppermute(value, axis, [(i, i ^ mask) for i in range(size)])


def bit_set(index, bit):
    return ((index >> bit) & 1) == 1


def spread(own, axis, index, size, bits):
    held = own
    for bit in bits:
        held = jnp.where(bit_set(index, bit), exchange(held, axis, 1 << bit, size), held)
    return held


def after(value, *others):
    return lax.optimization_barrier((value,) + others)


def shards(kernel):
    grid_row = lax.axis_index("row")
    grid_col = lax.axis_index("col")
    n_row = lax.axis_size("row")
    n_col = lax.axis_size("col")
    row_bits = list(range(1, n_row.bit_length() - 1))
    col_bits = list(range(1, n_col.bit_length() - 1))
    odd = (grid_row % 2) == 1
    right = (grid_col % 2) == 1

    block = corner_block(kernel)
    column, upper, lower = panels(kernel)
    block = spread(block, "row", grid_row, n_row, row_bits[:1])
    block, upper, lower = after(block, upper, lower)
    block = spread(block, "row", grid_row, n_row, row_bits[1:])
    ha = spread(upper, "row", grid_row, n_row, row_bits[:1])
    hb = spread(lower, "row", grid_row, n_row, row_bits[:0:-1])
    rows = spread(column, "col", grid_col, n_col, col_bits)
    block = spread(block, "col", grid_col, n_col, col_bits)
    block, ha, hb = after(block, ha, hb)
    across = exchange(block, "col", 1, n_col)
    ha = spread(ha, "row", grid_row, n_row, row_bits[1:])
    hb = spread(hb, "row", grid_row, n_row, row_bits[:1])
    mine = jnp.stack([jnp.where(right, across, block), jnp.where(right, block, across)])
    mine, rows = after(mine, rows)
    other = exchange(mine, "row", 1, n_row)
    rows_other = exchange(rows, "col", 1, n_col)

    a00 = jnp.where(odd, other[0], mine[0])
    a10 = jnp.where(odd, mine[0], other[0])
    a11 = jnp.where(odd, mine[1], other[1])
    f0, w0 = first_factor(a00)
    w0, ha, hb = after(w0, ha, hb)
    oa = exchange(ha, "row", 1, n_row)
    ob = exchange(hb, "row", 1, n_row)
    f1, w, mixed, blocks = second_factor(a10, a11, w0, kernel)
    return settle(f0, f1, w, mixed, rows, rows_other, ha, hb, oa, ob, blocks)


def solution(mesh):
    in_specs = (P(None, "row", None, "col"),)
    out_specs = P(None, "row", None, "col")
    return jax.shard_map(shards, mesh=mesh, in_specs=in_specs, out_specs=out_specs, check_vma=False)
```

```python
import jax
import jax.numpy as jnp
from jax import lax
from jax.experimental import pallas as pl
from jax.experimental.pallas import tpu as pltpu
from jax.sharding import PartitionSpec as P

EXACT = lax.Precision.HIGHEST
SUB = 8
MIB = 1024 * 1024
VMEM = pl.BlockSpec(memory_space=pltpu.VMEM)
HBM = pl.BlockSpec(memory_space=pltpu.HBM)


def dot(a, b):
    return lax.dot_general(a, b, (((1,), (0,)), ((), ())), precision=EXACT, preferred_element_type=jnp.float32)


def dot_t(a, b):
    return lax.dot_general(a, b, (((1,), (1,)), ((), ())), precision=EXACT, preferred_element_type=jnp.float32)


def full(row):
    return jnp.broadcast_to(row, (SUB, row.shape[-1]))


def eliminate(s, sym, aug):
    n = s.shape[0]
    groups = n // SUB
    sub = lax.broadcasted_iota(jnp.int32, (SUB, n), 0)
    lane = lax.broadcasted_iota(jnp.int32, (SUB, n), 1)
    sym[...] = s.reshape(groups, SUB, n)
    rows = lax.broadcasted_iota(jnp.int32, (n, n), 0)
    cols = lax.broadcasted_iota(jnp.int32, (n, n), 1)
    aug[...] = jnp.where(rows == cols, 1.0, 0.0).reshape(groups, SUB, n)
    for g in range(groups):
        start = g * SUB
        left = groups - g
        rest = sym[g:]
        top = sym[g]
        top_aug = aug[g]
        spread = [jnp.broadcast_to(rest[:, :, start + j:start + j + 1], (left, SUB, n)) for j in range(SUB)]
        unit = {(i, j): full(spread[j][0, i:i + 1, :]) for j in range(SUB) for i in range(j, SUB)}
        scaled = []
        scaled_aug = []
        roots = jnp.zeros((SUB, n), jnp.float32)
        for k in range(SUB):
            pivot = unit[k, k]
            guess = pl.reciprocal(pivot, approx=True)
            rest_of = 2.0 - pivot * guess
            recip = guess * rest_of
            roots = jnp.where(sub == k, pivot, roots)
            for j in range(k + 1, SUB):
                unit[j, j] = unit[j, j] - (unit[j, k] * unit[j, k] * guess) * rest_of
                for i in range(j + 1, SUB):
                    unit[i, j] = unit[i, j] - (unit[i, k] * unit[j, k] * guess) * rest_of
            for j in range(k + 1, SUB):
                factor = unit[j, k] * recip
                spread[j] = spread[j] - spread[k] * factor[None]
            row = full(top[k:k + 1, :]) * recip
            row_aug = full(top_aug[k:k + 1, :]) * recip
            scaled.append(row)
            scaled_aug.append(row_aug)
            if k + 1 < SUB:
                below = jnp.where(sub > k, spread[k][0], 0.0)
                top = top - below * row
                top_aug = top_aug - below * row_aug
        root = lax.rsqrt(roots)
        sym[g] = jnp.where(lane >= start + sub, top * root, 0.0)
        aug[g] = top_aug * root
        if left > 1:
            low = rest[1:]
            low_aug = aug[g + 1:]
            for k in range(SUB):
                low = low - spread[k][1:] * scaled[k][None]
                low_aug = low_aug - spread[k][1:] * scaled_aug[k][None]
            sym[g + 1:] = low
            aug[g + 1:] = low_aug
    upper = sym[...].reshape(n, n)
    return upper.T, aug[...].reshape(n, n)


def is_odd_row():
    return lax.rem(lax.axis_index("row"), 2) == 1


def parts(x):
    high = x.astype(jnp.bfloat16)
    rest = x - high.astype(jnp.float32)
    middle = rest.astype(jnp.bfloat16)
    return high, middle, (rest - middle.astype(jnp.float32)).astype(jnp.bfloat16)


def dot_parts(a, b, dims=((1,), (0,))):
    total = None
    for i, j in ((2, 0), (0, 2), (1, 1), (1, 0), (0, 1), (0, 0)):
        term = lax.dot_general(a[i], b[j], (dims, ((), ())), preferred_element_type=jnp.float32)
        total = term if total is None else total + term
    return total


def estimate(flops, nbytes):
    return pl.CostEstimate(flops=flops, bytes_accessed=nbytes, transcendentals=0)


def corner_kernel(matrix_ref, block_ref, sem):
    copy = pltpu.make_async_copy(matrix_ref.at[0, :, 0, :], block_ref, sem)
    copy.start()
    copy.wait()


def corner_block(matrix):
    n = matrix.shape[1]
    return pl.pallas_call(
        corner_kernel,
        out_shape=jax.ShapeDtypeStruct((n, n), jnp.float32),
        in_specs=[HBM],
        out_specs=VMEM,
        scratch_shapes=[pltpu.SemaphoreType.DMA(())],
        compiler_params=pltpu.CompilerParams(vmem_limit_bytes=2 * MIB),
        cost_estimate=estimate(0, 3 * MIB),
        name="corner_block",
    )(matrix)


def panels_kernel(matrix_ref, column_ref, upper_ref, lower_ref, sems):
    local_cols, half, _ = upper_ref.shape
    copies = [pltpu.make_async_copy(matrix_ref.at[:, :, 0, :], column_ref, sems.at[0])]
    for j in range(local_cols):
        copies.append(pltpu.make_async_copy(matrix_ref.at[0, pl.ds(0, half), j, :], upper_ref.at[j], sems.at[1 + j]))
        copies.append(pltpu.make_async_copy(
            matrix_ref.at[0, pl.ds(half, half), j, :], lower_ref.at[j], sems.at[1 + local_cols + j]))
    for copy in copies:
        copy.start()
    for copy in copies:
        copy.wait()


def panels(matrix):
    local_rows, n, local_cols, _ = matrix.shape
    strip = jax.ShapeDtypeStruct((local_cols, n // 2, n), jnp.float32)
    return pl.pallas_call(
        panels_kernel,
        out_shape=[jax.ShapeDtypeStruct((local_rows, n, n), jnp.float32), strip, strip],
        in_specs=[HBM],
        out_specs=[VMEM] * 3,
        scratch_shapes=[pltpu.SemaphoreType.DMA((1 + 2 * local_cols,))],
        compiler_params=pltpu.CompilerParams(vmem_limit_bytes=4 * MIB),
        cost_estimate=estimate(0, 4 * MIB),
        name="panels",
    )(matrix)


def first_factor_kernel(a_ref, f_ref, w_ref, sym, aug):
    f_ref[...], w_ref[...] = eliminate(a_ref[...], sym, aug)


def first_factor(a):
    n = a.shape[1]
    square = jax.ShapeDtypeStruct((n, n), jnp.float32)
    return pl.pallas_call(
        first_factor_kernel,
        out_shape=[square, square],
        in_specs=[VMEM],
        out_specs=[VMEM, VMEM],
        scratch_shapes=[pltpu.VMEM((n // SUB, SUB, n), jnp.float32)] * 2,
        compiler_params=pltpu.CompilerParams(vmem_limit_bytes=4 * MIB),
        cost_estimate=estimate(8 * 10**9, 2 * MIB),
        name="first_factor",
    )(a)


def second_factor_kernel(low_ref, a_ref, w0_ref, matrix_ref, f_ref, w_ref, mixed_ref,
                         blocks_ref, sym, aug, sems):
    n = w0_ref.shape[0]
    local_cols = matrix_ref.shape[2]
    copies = [pltpu.make_async_copy(matrix_ref.at[:, :, j, :], blocks_ref.at[j], sems.at[j]) for j in range(local_cols)]
    for copy in copies:
        copy.start()
    odd = is_odd_row()
    w0 = w0_ref[...]
    cross = dot_t(low_ref[...], w0)
    f1, w1 = eliminate(a_ref[...] - dot_t(cross, cross), sym, aug)
    f_ref[...] = f1
    w10 = -dot(w1, dot(cross, w0))
    zero = jnp.zeros((n, n), jnp.float32)
    w_ref[:n, :n] = w0
    w_ref[:n, n:] = zero
    w_ref[n:, :n] = w10
    w_ref[n:, n:] = w1
    mixed_ref[:n, :n] = jnp.where(odd, zero, w0)
    mixed_ref[:n, n:] = jnp.where(odd, w0, zero)
    mixed_ref[n:, :n] = jnp.where(odd, w1, w10)
    mixed_ref[n:, n:] = jnp.where(odd, w10, w1)
    for copy in copies:
        copy.wait()


def second_factor(low, a, w0, matrix):
    local_rows, n, local_cols, _ = matrix.shape
    square = jax.ShapeDtypeStruct((n, n), jnp.float32)
    double = jax.ShapeDtypeStruct((2 * n, 2 * n), jnp.float32)
    blocks = jax.ShapeDtypeStruct((local_cols, local_rows, n, n), jnp.float32)
    return pl.pallas_call(
        second_factor_kernel,
        out_shape=[square, double, double, blocks],
        in_specs=[VMEM] * 3 + [HBM],
        out_specs=[VMEM] * 4,
        scratch_shapes=[pltpu.VMEM((n // SUB, SUB, n), jnp.float32)] * 2 + [pltpu.SemaphoreType.DMA((local_cols,))],
        compiler_params=pltpu.CompilerParams(vmem_limit_bytes=12 * MIB),
        cost_estimate=estimate(8 * 10**9, 4 * MIB),
        name="second_factor",
    )(low, a, w0, matrix)


def settle_kernel(f0_ref, f1_ref, w_ref, mixed_ref, rows_ref, rows_other_ref, ha_ref, hb_ref, oa_ref, ob_ref, blocks_ref,
                  out_ref, result, sems):
    grid_row = lax.axis_index("row")
    grid_col = lax.axis_index("col")
    n = f0_ref.shape[0]
    local_cols, local_rows, _, _ = blocks_ref.shape
    flat = local_rows * n
    own = rows_ref[...].reshape(flat, n)
    other = rows_other_ref[...].reshape(flat, n)
    swapped = lax.rem(grid_col, 2) == 1
    rows = jnp.concatenate([jnp.where(swapped, other, own), jnp.where(swapped, own, other)], axis=1)
    solved = dot_parts(parts(rows), parts(w_ref[...]), ((1,), (1,)))
    left = parts(solved)
    mixed = parts(mixed_ref[...])
    copies = []
    for j in range(0, local_cols, 2):
        pair = (j, j + 1)
        stacked = jnp.concatenate(
            [jnp.concatenate([ha_ref[b], hb_ref[b], oa_ref[b], ob_ref[b]], axis=0) for b in pair], axis=1)
        update = dot_parts(left, parts(dot_parts(mixed, parts(stacked))))
        for b in pair:
            part = update[:, (b - j) * n:(b - j + 1) * n].reshape(local_rows, n, n)
            result[b] = blocks_ref[b] - part
        if j == 0:
            @pl.when(grid_col == 0)
            def _():
                result[0] = solved[:, :n].reshape(local_rows, n, n)

            @pl.when(grid_col == 1)
            def _():
                result[0] = solved[:, n:].reshape(local_rows, n, n)

        @pl.when(grid_row <= 1)
        def _():
            for b in pair:
                if b > 0:
                    result[b, 0] = jnp.zeros((n, n), jnp.float32)
            if j == 0:
                @pl.when(grid_col > grid_row)
                def _():
                    result[0, 0] = jnp.zeros((n, n), jnp.float32)

                @pl.when((grid_row == 0) & (grid_col == 0))
                def _():
                    result[0, 0] = f0_ref[...]

                @pl.when((grid_row == 1) & (grid_col == 1))
                def _():
                    result[0, 0] = f1_ref[...]
        for b in pair:
            copy = pltpu.make_async_copy(result.at[b], out_ref.at[:, :, b, :], sems.at[b])
            copy.start()
            copies.append(copy)
    for copy in copies:
        copy.wait()


def settle(f0, f1, w, mixed, rows, rows_other, ha, hb, oa, ob, blocks):
    local_cols, local_rows, n, _ = blocks.shape
    return pl.pallas_call(
        settle_kernel,
        out_shape=jax.ShapeDtypeStruct((local_rows, n, local_cols, n), jnp.float32),
        in_specs=[VMEM] * 11,
        out_specs=HBM,
        scratch_shapes=[pltpu.VMEM(blocks.shape, jnp.float32), pltpu.SemaphoreType.DMA((local_cols,))],
        compiler_params=pltpu.CompilerParams(vmem_limit_bytes=32 * MIB),
        cost_estimate=estimate(4 * 10**9, 6 * MIB),
        name="settle",
    )(f0, f1, w, mixed, rows, rows_other, ha, hb, oa, ob, blocks)


def exchange(value, axis, mask, size):
    return lax.ppermute(value, axis, [(i, i ^ mask) for i in range(size)])


def bit_set(index, bit):
    return ((index >> bit) & 1) == 1


def spread(own, axis, index, size, bits):
    held = own
    for bit in bits:
        held = jnp.where(bit_set(index, bit), exchange(held, axis, 1 << bit, size), held)
    return held


def after(value, *others):
    return lax.optimization_barrier((value,) + others)


def shards(kernel):
    grid_row = lax.axis_index("row")
    grid_col = lax.axis_index("col")
    n_row = lax.axis_size("row")
    n_col = lax.axis_size("col")
    row_bits = list(range(1, n_row.bit_length() - 1))
    col_bits = list(range(1, n_col.bit_length() - 1))
    odd = (grid_row % 2) == 1
    right = (grid_col % 2) == 1

    block = corner_block(kernel)
    column, upper, lower = panels(kernel)
    block = spread(block, "row", grid_row, n_row, row_bits[:1])
    block, upper, lower = after(block, upper, lower)
    block = spread(block, "row", grid_row, n_row, row_bits[1:])
    ha = spread(upper, "row", grid_row, n_row, row_bits[:1])
    hb = spread(lower, "row", grid_row, n_row, row_bits[:0:-1])
    rows = spread(column, "col", grid_col, n_col, col_bits)
    block = spread(block, "col", grid_col, n_col, col_bits)
    across = exchange(block, "col", 1, n_col)
    mine = jnp.stack([jnp.where(right, across, block), jnp.where(right, block, across)])
    other = exchange(mine, "row", 1, n_row)

    a00 = jnp.where(odd, other[0], mine[0])
    a10 = jnp.where(odd, mine[0], other[0])
    a11 = jnp.where(odd, mine[1], other[1])
    f0, w0 = first_factor(a00)
    w0, rows, ha, hb = after(w0, rows, ha, hb)
    ha = spread(ha, "row", grid_row, n_row, row_bits[1:])
    hb = spread(hb, "row", grid_row, n_row, row_bits[:1])
    rows_other = exchange(rows, "col", 1, n_col)
    f1, w, mixed, blocks = second_factor(a10, a11, w0, kernel)
    w, ha, hb = after(w, ha, hb)
    oa = exchange(ha, "row", 1, n_row)
    ob = exchange(hb, "row", 1, n_row)
    return settle(f0, f1, w, mixed, rows, rows_other, ha, hb, oa, ob, blocks)


def solution(mesh):
    in_specs = (P(None, "row", None, "col"),)
    out_specs = P(None, "row", None, "col")
    return jax.shard_map(shards, mesh=mesh, in_specs=in_specs, out_specs=out_specs, check_vma=False)
```

```python
import jax
import jax.numpy as jnp
from jax import lax
from jax.experimental import pallas as pl
from jax.experimental.pallas import tpu as pltpu
from jax.sharding import PartitionSpec as P

EXACT = lax.Precision.HIGHEST
SUB = 8
MIB = 1024 * 1024
VMEM = pl.BlockSpec(memory_space=pltpu.VMEM)
HBM = pl.BlockSpec(memory_space=pltpu.HBM)


def dot(a, b):
    return lax.dot_general(a, b, (((1,), (0,)), ((), ())), precision=EXACT, preferred_element_type=jnp.float32)


def dot_t(a, b):
    return lax.dot_general(a, b, (((1,), (1,)), ((), ())), precision=EXACT, preferred_element_type=jnp.float32)


def full(row):
    return jnp.broadcast_to(row, (SUB, row.shape[-1]))


def eliminate(s, sym, aug):
    n = s.shape[0]
    groups = n // SUB
    sub = lax.broadcasted_iota(jnp.int32, (SUB, n), 0)
    lane = lax.broadcasted_iota(jnp.int32, (SUB, n), 1)
    sym[...] = s.reshape(groups, SUB, n)
    rows = lax.broadcasted_iota(jnp.int32, (n, n), 0)
    cols = lax.broadcasted_iota(jnp.int32, (n, n), 1)
    aug[...] = jnp.where(rows == cols, 1.0, 0.0).reshape(groups, SUB, n)
    for g in range(groups):
        start = g * SUB
        left = groups - g
        rest = sym[g:]
        top = sym[g]
        top_aug = aug[g]
        spread = [jnp.broadcast_to(rest[:, :, start + j:start + j + 1], (left, SUB, n)) for j in range(SUB)]
        unit = {(i, j): full(spread[j][0, i:i + 1, :]) for j in range(SUB) for i in range(j, SUB)}
        scaled = []
        scaled_aug = []
        roots = jnp.zeros((SUB, n), jnp.float32)
        for k in range(SUB):
            pivot = unit[k, k]
            guess = pl.reciprocal(pivot, approx=True)
            rest_of = 2.0 - pivot * guess
            recip = guess * rest_of
            roots = jnp.where(sub == k, pivot, roots)
            for j in range(k + 1, SUB):
                unit[j, j] = unit[j, j] - (unit[j, k] * unit[j, k] * guess) * rest_of
                for i in range(j + 1, SUB):
                    unit[i, j] = unit[i, j] - (unit[i, k] * unit[j, k] * guess) * rest_of
            for j in range(k + 1, SUB):
                factor = unit[j, k] * recip
                spread[j] = spread[j] - spread[k] * factor[None]
            row = full(top[k:k + 1, :]) * recip
            row_aug = full(top_aug[k:k + 1, :]) * recip
            scaled.append(row)
            scaled_aug.append(row_aug)
            if k + 1 < SUB:
                below = jnp.where(sub > k, spread[k][0], 0.0)
                top = top - below * row
                top_aug = top_aug - below * row_aug
        root = lax.rsqrt(roots)
        sym[g] = jnp.where(lane >= start + sub, top * root, 0.0)
        aug[g] = top_aug * root
        if left > 1:
            low = rest[1:]
            low_aug = aug[g + 1:]
            for k in range(SUB):
                low = low - spread[k][1:] * scaled[k][None]
                low_aug = low_aug - spread[k][1:] * scaled_aug[k][None]
            sym[g + 1:] = low
            aug[g + 1:] = low_aug
    upper = sym[...].reshape(n, n)
    return upper.T, aug[...].reshape(n, n)


def is_odd_row():
    return lax.rem(lax.axis_index("row"), 2) == 1


def parts(x):
    high = x.astype(jnp.bfloat16)
    rest = x - high.astype(jnp.float32)
    middle = rest.astype(jnp.bfloat16)
    return high, middle, (rest - middle.astype(jnp.float32)).astype(jnp.bfloat16)


def dot_parts(a, b, dims=((1,), (0,))):
    total = None
    for i, j in ((2, 0), (0, 2), (1, 1), (1, 0), (0, 1), (0, 0)):
        term = lax.dot_general(a[i], b[j], (dims, ((), ())), preferred_element_type=jnp.float32)
        total = term if total is None else total + term
    return total


def estimate(flops, nbytes):
    return pl.CostEstimate(flops=flops, bytes_accessed=nbytes, transcendentals=0)


def corner_kernel(matrix_ref, block_ref, sem):
    copy = pltpu.make_async_copy(matrix_ref.at[0, :, 0, :], block_ref, sem)
    copy.start()
    copy.wait()


def corner_block(matrix):
    n = matrix.shape[1]
    return pl.pallas_call(
        corner_kernel,
        out_shape=jax.ShapeDtypeStruct((n, n), jnp.float32),
        in_specs=[HBM],
        out_specs=VMEM,
        scratch_shapes=[pltpu.SemaphoreType.DMA(())],
        compiler_params=pltpu.CompilerParams(vmem_limit_bytes=2 * MIB),
        cost_estimate=estimate(0, 3 * MIB),
        name="corner_block",
    )(matrix)


def panels_kernel(matrix_ref, column_ref, upper_ref, lower_ref, sems):
    local_cols, half, _ = upper_ref.shape
    copies = [pltpu.make_async_copy(matrix_ref.at[:, :, 0, :], column_ref, sems.at[0])]
    for j in range(local_cols):
        copies.append(pltpu.make_async_copy(matrix_ref.at[0, pl.ds(0, half), j, :], upper_ref.at[j], sems.at[1 + j]))
        copies.append(pltpu.make_async_copy(
            matrix_ref.at[0, pl.ds(half, half), j, :], lower_ref.at[j], sems.at[1 + local_cols + j]))
    for copy in copies:
        copy.start()
    for copy in copies:
        copy.wait()


def panels(matrix):
    local_rows, n, local_cols, _ = matrix.shape
    strip = jax.ShapeDtypeStruct((local_cols, n // 2, n), jnp.float32)
    return pl.pallas_call(
        panels_kernel,
        out_shape=[jax.ShapeDtypeStruct((local_rows, n, n), jnp.float32), strip, strip],
        in_specs=[HBM],
        out_specs=[VMEM] * 3,
        scratch_shapes=[pltpu.SemaphoreType.DMA((1 + 2 * local_cols,))],
        compiler_params=pltpu.CompilerParams(vmem_limit_bytes=4 * MIB),
        cost_estimate=estimate(0, 4 * MIB),
        name="panels",
    )(matrix)


def first_factor_kernel(a_ref, f_ref, w_ref, sym, aug):
    f_ref[...], w_ref[...] = eliminate(a_ref[...], sym, aug)


def first_factor(a):
    n = a.shape[1]
    square = jax.ShapeDtypeStruct((n, n), jnp.float32)
    return pl.pallas_call(
        first_factor_kernel,
        out_shape=[square, square],
        in_specs=[VMEM],
        out_specs=[VMEM, VMEM],
        scratch_shapes=[pltpu.VMEM((n // SUB, SUB, n), jnp.float32)] * 2,
        compiler_params=pltpu.CompilerParams(vmem_limit_bytes=4 * MIB),
        cost_estimate=estimate(8 * 10**9, 2 * MIB),
        name="first_factor",
    )(a)


def second_factor_kernel(low_ref, a_ref, w0_ref, matrix_ref, f_ref, w_ref, mixed_ref,
                         blocks_ref, sym, aug, sems):
    n = w0_ref.shape[0]
    local_cols = matrix_ref.shape[2]
    copies = [pltpu.make_async_copy(matrix_ref.at[:, :, j, :], blocks_ref.at[j], sems.at[j]) for j in range(local_cols)]
    for copy in copies:
        copy.start()
    odd = is_odd_row()
    w0 = w0_ref[...]
    cross = dot_t(low_ref[...], w0)
    f1, w1 = eliminate(a_ref[...] - dot_t(cross, cross), sym, aug)
    f_ref[...] = f1
    w10 = -dot(w1, dot(cross, w0))
    zero = jnp.zeros((n, n), jnp.float32)
    w_ref[:n, :n] = w0
    w_ref[:n, n:] = zero
    w_ref[n:, :n] = w10
    w_ref[n:, n:] = w1
    mixed_ref[:n, :n] = jnp.where(odd, zero, w0)
    mixed_ref[:n, n:] = jnp.where(odd, w0, zero)
    mixed_ref[n:, :n] = jnp.where(odd, w1, w10)
    mixed_ref[n:, n:] = jnp.where(odd, w10, w1)
    for copy in copies:
        copy.wait()


def second_factor(low, a, w0, matrix):
    local_rows, n, local_cols, _ = matrix.shape
    square = jax.ShapeDtypeStruct((n, n), jnp.float32)
    double = jax.ShapeDtypeStruct((2 * n, 2 * n), jnp.float32)
    blocks = jax.ShapeDtypeStruct((local_cols, local_rows, n, n), jnp.float32)
    return pl.pallas_call(
        second_factor_kernel,
        out_shape=[square, double, double, blocks],
        in_specs=[VMEM] * 3 + [HBM],
        out_specs=[VMEM] * 4,
        scratch_shapes=[pltpu.VMEM((n // SUB, SUB, n), jnp.float32)] * 2 + [pltpu.SemaphoreType.DMA((local_cols,))],
        compiler_params=pltpu.CompilerParams(vmem_limit_bytes=12 * MIB),
        cost_estimate=estimate(8 * 10**9, 4 * MIB),
        name="second_factor",
    )(low, a, w0, matrix)


def settle_kernel(f0_ref, f1_ref, w_ref, mixed_ref, rows_ref, rows_other_ref, ha_ref, hb_ref, oa_ref, ob_ref, blocks_ref,
                  out_ref, result, sems):
    grid_row = lax.axis_index("row")
    grid_col = lax.axis_index("col")
    n = f0_ref.shape[0]
    local_cols, local_rows, _, _ = blocks_ref.shape
    flat = local_rows * n
    own = rows_ref[...].reshape(flat, n)
    other = rows_other_ref[...].reshape(flat, n)
    swapped = lax.rem(grid_col, 2) == 1
    rows = jnp.concatenate([jnp.where(swapped, other, own), jnp.where(swapped, own, other)], axis=1)
    solved = dot_parts(parts(rows), parts(w_ref[...]), ((1,), (1,)))
    left = parts(solved)
    mixed = parts(mixed_ref[...])
    copies = []
    for j in range(0, local_cols, 2):
        pair = (j, j + 1)
        stacked = jnp.concatenate(
            [jnp.concatenate([ha_ref[b], hb_ref[b], oa_ref[b], ob_ref[b]], axis=0) for b in pair], axis=1)
        update = dot_parts(left, parts(dot_parts(mixed, parts(stacked))))
        for b in pair:
            part = update[:, (b - j) * n:(b - j + 1) * n].reshape(local_rows, n, n)
            result[b] = blocks_ref[b] - part
        if j == 0:
            @pl.when(grid_col == 0)
            def _():
                result[0] = solved[:, :n].reshape(local_rows, n, n)

            @pl.when(grid_col == 1)
            def _():
                result[0] = solved[:, n:].reshape(local_rows, n, n)

        @pl.when(grid_row <= 1)
        def _():
            for b in pair:
                if b > 0:
                    result[b, 0] = jnp.zeros((n, n), jnp.float32)
            if j == 0:
                @pl.when(grid_col > grid_row)
                def _():
                    result[0, 0] = jnp.zeros((n, n), jnp.float32)

                @pl.when((grid_row == 0) & (grid_col == 0))
                def _():
                    result[0, 0] = f0_ref[...]

                @pl.when((grid_row == 1) & (grid_col == 1))
                def _():
                    result[0, 0] = f1_ref[...]
        for b in pair:
            copy = pltpu.make_async_copy(result.at[b], out_ref.at[:, :, b, :], sems.at[b])
            copy.start()
            copies.append(copy)
    for copy in copies:
        copy.wait()


def settle(f0, f1, w, mixed, rows, rows_other, ha, hb, oa, ob, blocks):
    local_cols, local_rows, n, _ = blocks.shape
    return pl.pallas_call(
        settle_kernel,
        out_shape=jax.ShapeDtypeStruct((local_rows, n, local_cols, n), jnp.float32),
        in_specs=[VMEM] * 11,
        out_specs=HBM,
        scratch_shapes=[pltpu.VMEM(blocks.shape, jnp.float32), pltpu.SemaphoreType.DMA((local_cols,))],
        compiler_params=pltpu.CompilerParams(vmem_limit_bytes=32 * MIB),
        cost_estimate=estimate(4 * 10**9, 6 * MIB),
        name="settle",
    )(f0, f1, w, mixed, rows, rows_other, ha, hb, oa, ob, blocks)


def exchange(value, axis, mask, size):
    return lax.ppermute(value, axis, [(i, i ^ mask) for i in range(size)])


def bit_set(index, bit):
    return ((index >> bit) & 1) == 1


def spread(own, axis, index, size, bits):
    held = own
    for bit in bits:
        held = jnp.where(bit_set(index, bit), exchange(held, axis, 1 << bit, size), held)
    return held


def after(value, *others):
    return lax.optimization_barrier((value,) + others)


def shards(kernel):
    grid_row = lax.axis_index("row")
    grid_col = lax.axis_index("col")
    n_row = lax.axis_size("row")
    n_col = lax.axis_size("col")
    row_bits = list(range(1, n_row.bit_length() - 1))
    col_bits = list(range(1, n_col.bit_length() - 1))
    odd = (grid_row % 2) == 1
    right = (grid_col % 2) == 1

    block = corner_block(kernel)
    column, upper, lower = panels(kernel)
    block = spread(block, "row", grid_row, n_row, row_bits[:1])
    block, upper, lower = after(block, upper, lower)
    block = spread(block, "row", grid_row, n_row, row_bits[1:])
    block = spread(block, "col", grid_col, n_col, col_bits)
    across = exchange(block, "col", 1, n_col)
    mine = jnp.stack([jnp.where(right, across, block), jnp.where(right, block, across)])
    other = exchange(mine, "row", 1, n_row)

    a00 = jnp.where(odd, other[0], mine[0])
    a10 = jnp.where(odd, mine[0], other[0])
    a11 = jnp.where(odd, mine[1], other[1])
    f0, w0 = first_factor(a00)
    w0, row_then, col_then = after(w0, grid_row, grid_col)
    ha = spread(upper, "row", row_then, n_row, row_bits)
    hb = spread(lower, "row", row_then, n_row, row_bits[::-1])
    rows = spread(column, "col", col_then, n_col, col_bits)
    rows_other = exchange(rows, "col", 1, n_col)
    f1, w, mixed, blocks = second_factor(a10, a11, w0, kernel)
    w, ha, hb = after(w, ha, hb)
    oa = exchange(ha, "row", 1, n_row)
    ob = exchange(hb, "row", 1, n_row)
    return settle(f0, f1, w, mixed, rows, rows_other, ha, hb, oa, ob, blocks)


def solution(mesh):
    in_specs = (P(None, "row", None, "col"),)
    out_specs = P(None, "row", None, "col")
    return jax.shard_map(shards, mesh=mesh, in_specs=in_specs, out_specs=out_specs, check_vma=False)
```

```python
import jax
import jax.numpy as jnp
from jax import lax
from jax.experimental import pallas as pl
from jax.experimental.pallas import tpu as pltpu
from jax.sharding import PartitionSpec as P

EXACT = lax.Precision.HIGHEST
SUB = 8
MIB = 1024 * 1024
VMEM = pl.BlockSpec(memory_space=pltpu.VMEM)
HBM = pl.BlockSpec(memory_space=pltpu.HBM)


def dot(a, b):
    return lax.dot_general(a, b, (((1,), (0,)), ((), ())), precision=EXACT, preferred_element_type=jnp.float32)


def dot_t(a, b):
    return lax.dot_general(a, b, (((1,), (1,)), ((), ())), precision=EXACT, preferred_element_type=jnp.float32)


def full(row):
    return jnp.broadcast_to(row, (SUB, row.shape[-1]))


def eliminate(s, sym, aug):
    n = s.shape[0]
    groups = n // SUB
    sub = lax.broadcasted_iota(jnp.int32, (SUB, n), 0)
    lane = lax.broadcasted_iota(jnp.int32, (SUB, n), 1)
    sym[...] = s.reshape(groups, SUB, n)
    rows = lax.broadcasted_iota(jnp.int32, (n, n), 0)
    cols = lax.broadcasted_iota(jnp.int32, (n, n), 1)
    aug[...] = jnp.where(rows == cols, 1.0, 0.0).reshape(groups, SUB, n)
    for g in range(groups):
        start = g * SUB
        left = groups - g
        rest = sym[g:]
        top = sym[g]
        top_aug = aug[g]
        spread = [jnp.broadcast_to(rest[:, :, start + j:start + j + 1], (left, SUB, n)) for j in range(SUB)]
        unit = {(i, j): full(spread[j][0, i:i + 1, :]) for j in range(SUB) for i in range(j, SUB)}
        scaled = []
        scaled_aug = []
        roots = jnp.zeros((SUB, n), jnp.float32)
        for k in range(SUB):
            pivot = unit[k, k]
            guess = pl.reciprocal(pivot, approx=True)
            rest_of = 2.0 - pivot * guess
            recip = guess * rest_of
            roots = jnp.where(sub == k, pivot, roots)
            for j in range(k + 1, SUB):
                unit[j, j] = unit[j, j] - (unit[j, k] * unit[j, k] * guess) * rest_of
                for i in range(j + 1, SUB):
                    unit[i, j] = unit[i, j] - (unit[i, k] * unit[j, k] * guess) * rest_of
            for j in range(k + 1, SUB):
                factor = unit[j, k] * recip
                spread[j] = spread[j] - spread[k] * factor[None]
            row = full(top[k:k + 1, :]) * recip
            row_aug = full(top_aug[k:k + 1, :]) * recip
            scaled.append(row)
            scaled_aug.append(row_aug)
            if k + 1 < SUB:
                below = jnp.where(sub > k, spread[k][0], 0.0)
                top = top - below * row
                top_aug = top_aug - below * row_aug
        root = lax.rsqrt(roots)
        sym[g] = jnp.where(lane >= start + sub, top * root, 0.0)
        aug[g] = top_aug * root
        if left > 1:
            low = rest[1:]
            low_aug = aug[g + 1:]
            for k in range(SUB):
                low = low - spread[k][1:] * scaled[k][None]
                low_aug = low_aug - spread[k][1:] * scaled_aug[k][None]
            sym[g + 1:] = low
            aug[g + 1:] = low_aug
    upper = sym[...].reshape(n, n)
    return upper.T, aug[...].reshape(n, n)


def is_odd_row():
    return lax.rem(lax.axis_index("row"), 2) == 1


def parts(x):
    high = x.astype(jnp.bfloat16)
    rest = x - high.astype(jnp.float32)
    middle = rest.astype(jnp.bfloat16)
    return high, middle, (rest - middle.astype(jnp.float32)).astype(jnp.bfloat16)


def dot_parts(a, b, dims=((1,), (0,))):
    total = None
    for i, j in ((2, 0), (0, 2), (1, 1), (1, 0), (0, 1), (0, 0)):
        term = lax.dot_general(a[i], b[j], (dims, ((), ())), preferred_element_type=jnp.float32)
        total = term if total is None else total + term
    return total


def estimate(flops, nbytes):
    return pl.CostEstimate(flops=flops, bytes_accessed=nbytes, transcendentals=0)


def corner_kernel(matrix_ref, block_ref, sem):
    copy = pltpu.make_async_copy(matrix_ref.at[0, :, 0, :], block_ref, sem)
    copy.start()
    copy.wait()


def corner_block(matrix):
    n = matrix.shape[1]
    return pl.pallas_call(
        corner_kernel,
        out_shape=jax.ShapeDtypeStruct((n, n), jnp.float32),
        in_specs=[HBM],
        out_specs=VMEM,
        scratch_shapes=[pltpu.SemaphoreType.DMA(())],
        compiler_params=pltpu.CompilerParams(vmem_limit_bytes=2 * MIB),
        cost_estimate=estimate(0, 3 * MIB),
        name="corner_block",
    )(matrix)


def panels_kernel(matrix_ref, column_ref, upper_ref, lower_ref, sems):
    local_cols, half, _ = upper_ref.shape
    copies = [pltpu.make_async_copy(matrix_ref.at[:, :, 0, :], column_ref, sems.at[0])]
    for j in range(local_cols):
        copies.append(pltpu.make_async_copy(matrix_ref.at[0, pl.ds(0, half), j, :], upper_ref.at[j], sems.at[1 + j]))
        copies.append(pltpu.make_async_copy(
            matrix_ref.at[0, pl.ds(half, half), j, :], lower_ref.at[j], sems.at[1 + local_cols + j]))
    for copy in copies:
        copy.start()
    for copy in copies:
        copy.wait()


def panels(matrix):
    local_rows, n, local_cols, _ = matrix.shape
    strip = jax.ShapeDtypeStruct((local_cols, n // 2, n), jnp.float32)
    return pl.pallas_call(
        panels_kernel,
        out_shape=[jax.ShapeDtypeStruct((local_rows, n, n), jnp.float32), strip, strip],
        in_specs=[HBM],
        out_specs=[VMEM] * 3,
        scratch_shapes=[pltpu.SemaphoreType.DMA((1 + 2 * local_cols,))],
        compiler_params=pltpu.CompilerParams(vmem_limit_bytes=4 * MIB),
        cost_estimate=estimate(0, 4 * MIB),
        name="panels",
    )(matrix)


def first_factor_kernel(a_ref, f_ref, w_ref, sym, aug):
    f_ref[...], w_ref[...] = eliminate(a_ref[...], sym, aug)


def first_factor(a):
    n = a.shape[1]
    square = jax.ShapeDtypeStruct((n, n), jnp.float32)
    return pl.pallas_call(
        first_factor_kernel,
        out_shape=[square, square],
        in_specs=[VMEM],
        out_specs=[VMEM, VMEM],
        scratch_shapes=[pltpu.VMEM((n // SUB, SUB, n), jnp.float32)] * 2,
        compiler_params=pltpu.CompilerParams(vmem_limit_bytes=4 * MIB),
        cost_estimate=estimate(8 * 10**9, 2 * MIB),
        name="first_factor",
    )(a)


def second_factor_kernel(low_ref, a_ref, w0_ref, matrix_ref, f_ref, w_ref, mixed_ref,
                         blocks_ref, sym, aug, sems):
    n = w0_ref.shape[0]
    local_cols = matrix_ref.shape[2]
    copies = [pltpu.make_async_copy(matrix_ref.at[:, :, j, :], blocks_ref.at[j], sems.at[j]) for j in range(local_cols)]
    for copy in copies:
        copy.start()
    odd = is_odd_row()
    w0 = w0_ref[...]
    cross = dot_t(low_ref[...], w0)
    f1, w1 = eliminate(a_ref[...] - dot_t(cross, cross), sym, aug)
    f_ref[...] = f1
    w10 = -dot(w1, dot(cross, w0))
    zero = jnp.zeros((n, n), jnp.float32)
    w_ref[:n, :n] = w0
    w_ref[:n, n:] = zero
    w_ref[n:, :n] = w10
    w_ref[n:, n:] = w1
    mixed_ref[:n, :n] = jnp.where(odd, zero, w0)
    mixed_ref[:n, n:] = jnp.where(odd, w0, zero)
    mixed_ref[n:, :n] = jnp.where(odd, w1, w10)
    mixed_ref[n:, n:] = jnp.where(odd, w10, w1)
    for copy in copies:
        copy.wait()


def second_factor(low, a, w0, matrix):
    local_rows, n, local_cols, _ = matrix.shape
    square = jax.ShapeDtypeStruct((n, n), jnp.float32)
    double = jax.ShapeDtypeStruct((2 * n, 2 * n), jnp.float32)
    blocks = jax.ShapeDtypeStruct((local_cols, local_rows, n, n), jnp.float32)
    return pl.pallas_call(
        second_factor_kernel,
        out_shape=[square, double, double, blocks],
        in_specs=[VMEM] * 3 + [HBM],
        out_specs=[VMEM] * 4,
        scratch_shapes=[pltpu.VMEM((n // SUB, SUB, n), jnp.float32)] * 2 + [pltpu.SemaphoreType.DMA((local_cols,))],
        compiler_params=pltpu.CompilerParams(vmem_limit_bytes=12 * MIB),
        cost_estimate=estimate(8 * 10**9, 4 * MIB),
        name="second_factor",
    )(low, a, w0, matrix)


def settle_kernel(f0_ref, f1_ref, w_ref, mixed_ref, rows_ref, rows_other_ref, ha_ref, hb_ref, oa_ref, ob_ref, blocks_ref,
                  out_ref, result, sems):
    grid_row = lax.axis_index("row")
    grid_col = lax.axis_index("col")
    n = f0_ref.shape[0]
    local_cols, local_rows, _, _ = blocks_ref.shape
    flat = local_rows * n
    own = rows_ref[...].reshape(flat, n)
    other = rows_other_ref[...].reshape(flat, n)
    swapped = lax.rem(grid_col, 2) == 1
    rows = jnp.concatenate([jnp.where(swapped, other, own), jnp.where(swapped, own, other)], axis=1)
    solved = dot_parts(parts(rows), parts(w_ref[...]), ((1,), (1,)))
    left = parts(solved)
    mixed = parts(mixed_ref[...])
    copies = []
    for j in range(0, local_cols, 2):
        pair = (j, j + 1)
        stacked = jnp.concatenate(
            [jnp.concatenate([ha_ref[b], hb_ref[b], oa_ref[b], ob_ref[b]], axis=0) for b in pair], axis=1)
        update = dot_parts(left, parts(dot_parts(mixed, parts(stacked))))
        for b in pair:
            part = update[:, (b - j) * n:(b - j + 1) * n].reshape(local_rows, n, n)
            result[b] = blocks_ref[b] - part
        if j == 0:
            @pl.when(grid_col == 0)
            def _():
                result[0] = solved[:, :n].reshape(local_rows, n, n)

            @pl.when(grid_col == 1)
            def _():
                result[0] = solved[:, n:].reshape(local_rows, n, n)

        @pl.when(grid_row <= 1)
        def _():
            for b in pair:
                if b > 0:
                    result[b, 0] = jnp.zeros((n, n), jnp.float32)
            if j == 0:
                @pl.when(grid_col > grid_row)
                def _():
                    result[0, 0] = jnp.zeros((n, n), jnp.float32)

                @pl.when((grid_row == 0) & (grid_col == 0))
                def _():
                    result[0, 0] = f0_ref[...]

                @pl.when((grid_row == 1) & (grid_col == 1))
                def _():
                    result[0, 0] = f1_ref[...]
        for b in pair:
            copy = pltpu.make_async_copy(result.at[b], out_ref.at[:, :, b, :], sems.at[b])
            copy.start()
            copies.append(copy)
    for copy in copies:
        copy.wait()


def settle(f0, f1, w, mixed, rows, rows_other, ha, hb, oa, ob, blocks):
    local_cols, local_rows, n, _ = blocks.shape
    return pl.pallas_call(
        settle_kernel,
        out_shape=jax.ShapeDtypeStruct((local_rows, n, local_cols, n), jnp.float32),
        in_specs=[VMEM] * 11,
        out_specs=HBM,
        scratch_shapes=[pltpu.VMEM(blocks.shape, jnp.float32), pltpu.SemaphoreType.DMA((local_cols,))],
        compiler_params=pltpu.CompilerParams(vmem_limit_bytes=32 * MIB),
        cost_estimate=estimate(4 * 10**9, 6 * MIB),
        name="settle",
    )(f0, f1, w, mixed, rows, rows_other, ha, hb, oa, ob, blocks)


def exchange(value, axis, mask, size):
    return lax.ppermute(value, axis, [(i, i ^ mask) for i in range(size)])


def bit_set(index, bit):
    return ((index >> bit) & 1) == 1


def spread(own, axis, index, size, bits):
    held = own
    for bit in bits:
        held = jnp.where(bit_set(index, bit), exchange(held, axis, 1 << bit, size), held)
    return held


def region(run, *values):
    shapes = jax.eval_shape(run, *values)

    def skip(*_):
        return jax.tree.map(lambda leaf: jnp.zeros(leaf.shape, leaf.dtype), shapes)

    everywhere = lax.axis_index("row") < lax.axis_size("row")
    return lax.cond(everywhere, run, skip, *values)


def after(value, *others):
    return lax.optimization_barrier((value,) + others)


def shards(kernel):
    grid_row = lax.axis_index("row")
    grid_col = lax.axis_index("col")
    n_row = lax.axis_size("row")
    n_col = lax.axis_size("col")
    row_bits = list(range(1, n_row.bit_length() - 1))
    col_bits = list(range(1, n_col.bit_length() - 1))
    odd = (grid_row % 2) == 1
    right = (grid_col % 2) == 1

    block = corner_block(kernel)
    column, upper, lower = panels(kernel)
    first_bit, last_bit = row_bits[0], row_bits[-1]
    moved = exchange(block, "row", 1 << first_bit, n_row)
    upper_moved = exchange(upper, "row", 1 << first_bit, n_row)
    column_moved = exchange(column, "col", 1 << col_bits[0], n_col)
    block = region(lambda new, old: jnp.where(bit_set(grid_row, first_bit), new, old), moved, block)

    block, lower = after(block, lower)
    moved = exchange(block, "row", 1 << row_bits[1], n_row)
    lower_moved = exchange(lower, "row", 1 << last_bit, n_row)

    def along_col(new, old):
        block = jnp.where(bit_set(grid_row, row_bits[1]), new, old)
        block = spread(block, "row", grid_row, n_row, row_bits[2:])
        return spread(block, "col", grid_col, n_col, col_bits)

    moved, block, upper_moved = after(moved, block, upper_moved)
    block = region(along_col, moved, block)

    block, row_then = after(block, grid_row)
    across = exchange(block, "col", 1, n_col)
    ha = jnp.where(bit_set(row_then, first_bit), upper_moved, upper)
    hb = jnp.where(bit_set(row_then, last_bit), lower_moved, lower)
    rows = jnp.where(bit_set(grid_col, col_bits[0]), column_moved, column)
    across, block, ha, hb, rows = after(across, block, ha, hb, rows)
    ha_moved = exchange(ha, "row", 1 << row_bits[1], n_row)
    hb_moved = exchange(hb, "row", 1 << row_bits[-2], n_row)

    def factor(across, block):
        mine = jnp.stack([jnp.where(right, across, block), jnp.where(right, block, across)])
        other = exchange(mine, "row", 1, n_row)
        a00 = jnp.where(odd, other[0], mine[0])
        a10 = jnp.where(odd, mine[0], other[0])
        a11 = jnp.where(odd, mine[1], other[1])
        f0, w0 = first_factor(a00)
        return a10, a11, f0, w0

    a10, a11, f0, w0 = region(factor, across, block)

    w0, row_then, col_then = after(w0, grid_row, grid_col)
    ha = jnp.where(bit_set(row_then, row_bits[1]), ha_moved, ha)
    ha = spread(ha, "row", row_then, n_row, row_bits[2:])
    hb = jnp.where(bit_set(row_then, row_bits[-2]), hb_moved, hb)
    hb = spread(hb, "row", row_then, n_row, row_bits[:-2][::-1])
    rows = spread(rows, "col", col_then, n_col, col_bits[1:])
    rows_other = exchange(rows, "col", 1, n_col)
    oa = exchange(ha, "row", 1, n_row)
    ob = exchange(hb, "row", 1, n_row)
    f1, w, mixed, blocks = second_factor(a10, a11, w0, kernel)
    return settle(f0, f1, w, mixed, rows, rows_other, ha, hb, oa, ob, blocks)


def solution(mesh):
    in_specs = (P(None, "row", None, "col"),)
    out_specs = P(None, "row", None, "col")
    return jax.shard_map(shards, mesh=mesh, in_specs=in_specs, out_specs=out_specs, check_vma=False)
```

```python
import jax
import jax.numpy as jnp
from jax import lax
from jax.experimental import pallas as pl
from jax.experimental.pallas import tpu as pltpu
from jax.sharding import PartitionSpec as P

EXACT = lax.Precision.HIGHEST
SUB = 8
MIB = 1024 * 1024
VMEM = pl.BlockSpec(memory_space=pltpu.VMEM)
HBM = pl.BlockSpec(memory_space=pltpu.HBM)


def dot(a, b):
    return lax.dot_general(a, b, (((1,), (0,)), ((), ())), precision=EXACT, preferred_element_type=jnp.float32)


def dot_t(a, b):
    return lax.dot_general(a, b, (((1,), (1,)), ((), ())), precision=EXACT, preferred_element_type=jnp.float32)


def full(row):
    return jnp.broadcast_to(row, (SUB, row.shape[-1]))


def eliminate(s, sym, aug):
    n = s.shape[0]
    groups = n // SUB
    sub = lax.broadcasted_iota(jnp.int32, (SUB, n), 0)
    lane = lax.broadcasted_iota(jnp.int32, (SUB, n), 1)
    sym[...] = s.reshape(groups, SUB, n)
    rows = lax.broadcasted_iota(jnp.int32, (n, n), 0)
    cols = lax.broadcasted_iota(jnp.int32, (n, n), 1)
    aug[...] = jnp.where(rows == cols, 1.0, 0.0).reshape(groups, SUB, n)
    for g in range(groups):
        start = g * SUB
        left = groups - g
        rest = sym[g:]
        top = sym[g]
        top_aug = aug[g]
        spread = [jnp.broadcast_to(rest[:, :, start + j:start + j + 1], (left, SUB, n)) for j in range(SUB)]
        unit = {(i, j): full(spread[j][0, i:i + 1, :]) for j in range(SUB) for i in range(j, SUB)}
        scaled = []
        scaled_aug = []
        roots = jnp.zeros((SUB, n), jnp.float32)
        for k in range(SUB):
            pivot = unit[k, k]
            guess = pl.reciprocal(pivot, approx=True)
            rest_of = 2.0 - pivot * guess
            recip = guess * rest_of
            roots = jnp.where(sub == k, pivot, roots)
            for j in range(k + 1, SUB):
                unit[j, j] = unit[j, j] - (unit[j, k] * unit[j, k] * guess) * rest_of
                for i in range(j + 1, SUB):
                    unit[i, j] = unit[i, j] - (unit[i, k] * unit[j, k] * guess) * rest_of
            for j in range(k + 1, SUB):
                factor = unit[j, k] * recip
                spread[j] = spread[j] - spread[k] * factor[None]
            row = full(top[k:k + 1, :]) * recip
            row_aug = full(top_aug[k:k + 1, :]) * recip
            scaled.append(row)
            scaled_aug.append(row_aug)
            if k + 1 < SUB:
                below = jnp.where(sub > k, spread[k][0], 0.0)
                top = top - below * row
                top_aug = top_aug - below * row_aug
        root = lax.rsqrt(roots)
        sym[g] = jnp.where(lane >= start + sub, top * root, 0.0)
        aug[g] = top_aug * root
        if left > 1:
            low = rest[1:]
            low_aug = aug[g + 1:]
            for k in range(SUB):
                low = low - spread[k][1:] * scaled[k][None]
                low_aug = low_aug - spread[k][1:] * scaled_aug[k][None]
            sym[g + 1:] = low
            aug[g + 1:] = low_aug
    upper = sym[...].reshape(n, n)
    return upper.T, aug[...].reshape(n, n)


def is_odd_row():
    return lax.rem(lax.axis_index("row"), 2) == 1


def parts(x):
    high = x.astype(jnp.bfloat16)
    rest = x - high.astype(jnp.float32)
    middle = rest.astype(jnp.bfloat16)
    return high, middle, (rest - middle.astype(jnp.float32)).astype(jnp.bfloat16)


def dot_parts(a, b, dims=((1,), (0,))):
    total = None
    for i, j in ((2, 0), (0, 2), (1, 1), (1, 0), (0, 1), (0, 0)):
        term = lax.dot_general(a[i], b[j], (dims, ((), ())), preferred_element_type=jnp.float32)
        total = term if total is None else total + term
    return total


def estimate(flops, nbytes):
    return pl.CostEstimate(flops=flops, bytes_accessed=nbytes, transcendentals=0)


def corner_kernel(matrix_ref, block_ref, sem):
    copy = pltpu.make_async_copy(matrix_ref.at[0, :, 0, :], block_ref, sem)
    copy.start()
    copy.wait()


def corner_block(matrix):
    n = matrix.shape[1]
    return pl.pallas_call(
        corner_kernel,
        out_shape=jax.ShapeDtypeStruct((n, n), jnp.float32),
        in_specs=[HBM],
        out_specs=VMEM,
        scratch_shapes=[pltpu.SemaphoreType.DMA(())],
        compiler_params=pltpu.CompilerParams(vmem_limit_bytes=2 * MIB),
        cost_estimate=estimate(0, 3 * MIB),
        name="corner_block",
    )(matrix)


def panels_kernel(matrix_ref, column_ref, upper_ref, lower_ref, sems):
    local_cols, half, _ = upper_ref.shape
    copies = [pltpu.make_async_copy(matrix_ref.at[:, :, 0, :], column_ref, sems.at[0])]
    for j in range(local_cols):
        copies.append(pltpu.make_async_copy(matrix_ref.at[0, pl.ds(0, half), j, :], upper_ref.at[j], sems.at[1 + j]))
        copies.append(pltpu.make_async_copy(
            matrix_ref.at[0, pl.ds(half, half), j, :], lower_ref.at[j], sems.at[1 + local_cols + j]))
    for copy in copies:
        copy.start()
    for copy in copies:
        copy.wait()


def panels(matrix):
    local_rows, n, local_cols, _ = matrix.shape
    strip = jax.ShapeDtypeStruct((local_cols, n // 2, n), jnp.float32)
    return pl.pallas_call(
        panels_kernel,
        out_shape=[jax.ShapeDtypeStruct((local_rows, n, n), jnp.float32), strip, strip],
        in_specs=[HBM],
        out_specs=[VMEM] * 3,
        scratch_shapes=[pltpu.SemaphoreType.DMA((1 + 2 * local_cols,))],
        compiler_params=pltpu.CompilerParams(vmem_limit_bytes=4 * MIB),
        cost_estimate=estimate(0, 4 * MIB),
        name="panels",
    )(matrix)


def first_factor_kernel(a_ref, f_ref, w_ref, sym, aug):
    f_ref[...], w_ref[...] = eliminate(a_ref[...], sym, aug)


def first_factor(a):
    n = a.shape[1]
    square = jax.ShapeDtypeStruct((n, n), jnp.float32)
    return pl.pallas_call(
        first_factor_kernel,
        out_shape=[square, square],
        in_specs=[VMEM],
        out_specs=[VMEM, VMEM],
        scratch_shapes=[pltpu.VMEM((n // SUB, SUB, n), jnp.float32)] * 2,
        compiler_params=pltpu.CompilerParams(vmem_limit_bytes=4 * MIB),
        cost_estimate=estimate(8 * 10**9, 2 * MIB),
        name="first_factor",
    )(a)


def second_factor_kernel(low_ref, a_ref, w0_ref, matrix_ref, f_ref, w_ref, mixed_ref,
                         blocks_ref, sym, aug, sems):
    n = w0_ref.shape[0]
    local_cols = matrix_ref.shape[2]
    copies = [pltpu.make_async_copy(matrix_ref.at[:, :, j, :], blocks_ref.at[j], sems.at[j]) for j in range(local_cols)]
    for copy in copies:
        copy.start()
    odd = is_odd_row()
    w0 = w0_ref[...]
    cross = dot_t(low_ref[...], w0)
    f1, w1 = eliminate(a_ref[...] - dot_t(cross, cross), sym, aug)
    f_ref[...] = f1
    w10 = -dot(w1, dot(cross, w0))
    zero = jnp.zeros((n, n), jnp.float32)
    w_ref[:n, :n] = w0
    w_ref[:n, n:] = zero
    w_ref[n:, :n] = w10
    w_ref[n:, n:] = w1
    mixed_ref[:n, :n] = jnp.where(odd, zero, w0)
    mixed_ref[:n, n:] = jnp.where(odd, w0, zero)
    mixed_ref[n:, :n] = jnp.where(odd, w1, w10)
    mixed_ref[n:, n:] = jnp.where(odd, w10, w1)
    for copy in copies:
        copy.wait()


def second_factor(low, a, w0, matrix):
    local_rows, n, local_cols, _ = matrix.shape
    square = jax.ShapeDtypeStruct((n, n), jnp.float32)
    double = jax.ShapeDtypeStruct((2 * n, 2 * n), jnp.float32)
    blocks = jax.ShapeDtypeStruct((local_cols, local_rows, n, n), jnp.float32)
    return pl.pallas_call(
        second_factor_kernel,
        out_shape=[square, double, double, blocks],
        in_specs=[VMEM] * 3 + [HBM],
        out_specs=[VMEM] * 4,
        scratch_shapes=[pltpu.VMEM((n // SUB, SUB, n), jnp.float32)] * 2 + [pltpu.SemaphoreType.DMA((local_cols,))],
        compiler_params=pltpu.CompilerParams(vmem_limit_bytes=12 * MIB),
        cost_estimate=estimate(8 * 10**9, 4 * MIB),
        name="second_factor",
    )(low, a, w0, matrix)


def settle_kernel(f0_ref, f1_ref, w_ref, mixed_ref, rows_ref, rows_other_ref, ha_ref, hb_ref, oa_ref, ob_ref, blocks_ref,
                  out_ref, result, sems):
    grid_row = lax.axis_index("row")
    grid_col = lax.axis_index("col")
    n = f0_ref.shape[0]
    local_cols, local_rows, _, _ = blocks_ref.shape
    flat = local_rows * n
    own = rows_ref[...].reshape(flat, n)
    other = rows_other_ref[...].reshape(flat, n)
    swapped = lax.rem(grid_col, 2) == 1
    rows = jnp.concatenate([jnp.where(swapped, other, own), jnp.where(swapped, own, other)], axis=1)
    solved = dot_parts(parts(rows), parts(w_ref[...]), ((1,), (1,)))
    left = parts(solved)
    mixed = parts(mixed_ref[...])
    copies = []
    for j in range(0, local_cols, 2):
        pair = (j, j + 1)
        stacked = jnp.concatenate(
            [jnp.concatenate([ha_ref[b], hb_ref[b], oa_ref[b], ob_ref[b]], axis=0) for b in pair], axis=1)
        update = dot_parts(left, parts(dot_parts(mixed, parts(stacked))))
        for b in pair:
            part = update[:, (b - j) * n:(b - j + 1) * n].reshape(local_rows, n, n)
            result[b] = blocks_ref[b] - part
        if j == 0:
            @pl.when(grid_col == 0)
            def _():
                result[0] = solved[:, :n].reshape(local_rows, n, n)

            @pl.when(grid_col == 1)
            def _():
                result[0] = solved[:, n:].reshape(local_rows, n, n)

        @pl.when(grid_row <= 1)
        def _():
            for b in pair:
                if b > 0:
                    result[b, 0] = jnp.zeros((n, n), jnp.float32)
            if j == 0:
                @pl.when(grid_col > grid_row)
                def _():
                    result[0, 0] = jnp.zeros((n, n), jnp.float32)

                @pl.when((grid_row == 0) & (grid_col == 0))
                def _():
                    result[0, 0] = f0_ref[...]

                @pl.when((grid_row == 1) & (grid_col == 1))
                def _():
                    result[0, 0] = f1_ref[...]
        for b in pair:
            copy = pltpu.make_async_copy(result.at[b], out_ref.at[:, :, b, :], sems.at[b])
            copy.start()
            copies.append(copy)
    for copy in copies:
        copy.wait()


def settle(f0, f1, w, mixed, rows, rows_other, ha, hb, oa, ob, blocks):
    local_cols, local_rows, n, _ = blocks.shape
    return pl.pallas_call(
        settle_kernel,
        out_shape=jax.ShapeDtypeStruct((local_rows, n, local_cols, n), jnp.float32),
        in_specs=[VMEM] * 11,
        out_specs=HBM,
        scratch_shapes=[pltpu.VMEM(blocks.shape, jnp.float32), pltpu.SemaphoreType.DMA((local_cols,))],
        compiler_params=pltpu.CompilerParams(vmem_limit_bytes=32 * MIB),
        cost_estimate=estimate(4 * 10**9, 6 * MIB),
        name="settle",
    )(f0, f1, w, mixed, rows, rows_other, ha, hb, oa, ob, blocks)


def exchange(value, axis, mask, size):
    return lax.ppermute(value, axis, [(i, i ^ mask) for i in range(size)])


def bit_set(index, bit):
    return ((index >> bit) & 1) == 1


def spread(own, axis, index, size, bits):
    held = own
    for bit in bits:
        held = jnp.where(bit_set(index, bit), exchange(held, axis, 1 << bit, size), held)
    return held


def region(run, *values):
    shapes = jax.eval_shape(run, *values)

    def skip(*_):
        return jax.tree.map(lambda leaf: jnp.zeros(leaf.shape, leaf.dtype), shapes)

    everywhere = lax.axis_index("row") < lax.axis_size("row")
    return lax.cond(everywhere, run, skip, *values)


def after(value, *others):
    return lax.optimization_barrier((value,) + others)


def shards(kernel):
    grid_row = lax.axis_index("row")
    grid_col = lax.axis_index("col")
    n_row = lax.axis_size("row")
    n_col = lax.axis_size("col")
    row_bits = list(range(1, n_row.bit_length() - 1))
    col_bits = list(range(1, n_col.bit_length() - 1))
    odd = (grid_row % 2) == 1
    right = (grid_col % 2) == 1

    block = corner_block(kernel)
    column, upper, lower = panels(kernel)
    first_bit, last_bit = row_bits[0], row_bits[-1]
    column_moved = exchange(column, "col", 1 << col_bits[0], n_col)
    moved = exchange(block, "row", 1 << first_bit, n_row)
    block = region(lambda new, old: jnp.where(bit_set(grid_row, first_bit), new, old), moved, block)

    block, upper, lower = after(block, upper, lower)
    moved = exchange(block, "row", 1 << row_bits[1], n_row)
    upper_moved = exchange(upper, "row", 1 << first_bit, n_row)
    lower_moved = exchange(lower, "row", 1 << last_bit, n_row)
    moved, block, column_moved = after(moved, block, column_moved)

    def along_col(new, old):
        block = jnp.where(bit_set(grid_row, row_bits[1]), new, old)
        block = spread(block, "row", grid_row, n_row, row_bits[2:])
        return spread(block, "col", grid_col, n_col, col_bits)

    block = region(along_col, moved, block)

    block, row_then = after(block, grid_row)
    ha = jnp.where(bit_set(row_then, first_bit), upper_moved, upper)
    hb = jnp.where(bit_set(row_then, last_bit), lower_moved, lower)
    block, ha, hb = after(block, ha, hb)
    across = exchange(block, "col", 1, n_col)
    mine = jnp.stack([jnp.where(right, across, block), jnp.where(right, block, across)])
    other = exchange(mine, "row", 1, n_row)
    ha_moved = exchange(ha, "row", 1 << row_bits[1], n_row)
    hb_moved = exchange(hb, "row", 1 << row_bits[-2], n_row)

    a00 = jnp.where(odd, other[0], mine[0])
    a10 = jnp.where(odd, mine[0], other[0])
    a11 = jnp.where(odd, mine[1], other[1])
    f0, w0 = first_factor(a00)

    w0, row_then, col_then = after(w0, grid_row, grid_col)
    ha = jnp.where(bit_set(row_then, row_bits[1]), ha_moved, ha)
    ha = spread(ha, "row", row_then, n_row, row_bits[2:])
    hb = jnp.where(bit_set(row_then, row_bits[-2]), hb_moved, hb)
    hb = spread(hb, "row", row_then, n_row, row_bits[:-2][::-1])
    rows = jnp.where(bit_set(col_then, col_bits[0]), column_moved, column)
    rows = spread(rows, "col", col_then, n_col, col_bits[1:])
    rows_other = exchange(rows, "col", 1, n_col)
    oa = exchange(ha, "row", 1, n_row)
    ob = exchange(hb, "row", 1, n_row)
    f1, w, mixed, blocks = second_factor(a10, a11, w0, kernel)
    return settle(f0, f1, w, mixed, rows, rows_other, ha, hb, oa, ob, blocks)


def solution(mesh):
    in_specs = (P(None, "row", None, "col"),)
    out_specs = P(None, "row", None, "col")
    return jax.shard_map(shards, mesh=mesh, in_specs=in_specs, out_specs=out_specs, check_vma=False)
```

```python
import jax
import jax.numpy as jnp
from jax import lax
from jax.experimental import pallas as pl
from jax.experimental.pallas import tpu as pltpu
from jax.sharding import PartitionSpec as P

EXACT = lax.Precision.HIGHEST
SUB = 8
MIB = 1024 * 1024
VMEM = pl.BlockSpec(memory_space=pltpu.VMEM)
HBM = pl.BlockSpec(memory_space=pltpu.HBM)


def dot(a, b):
    return lax.dot_general(a, b, (((1,), (0,)), ((), ())), precision=EXACT, preferred_element_type=jnp.float32)


def dot_t(a, b):
    return lax.dot_general(a, b, (((1,), (1,)), ((), ())), precision=EXACT, preferred_element_type=jnp.float32)


def full(row):
    return jnp.broadcast_to(row, (SUB, row.shape[-1]))


def eliminate(s, sym, aug):
    n = s.shape[0]
    groups = n // SUB
    sub = lax.broadcasted_iota(jnp.int32, (SUB, n), 0)
    lane = lax.broadcasted_iota(jnp.int32, (SUB, n), 1)
    sym[...] = s.reshape(groups, SUB, n)
    rows = lax.broadcasted_iota(jnp.int32, (n, n), 0)
    cols = lax.broadcasted_iota(jnp.int32, (n, n), 1)
    aug[...] = jnp.where(rows == cols, 1.0, 0.0).reshape(groups, SUB, n)
    for g in range(groups):
        start = g * SUB
        left = groups - g
        rest = sym[g:]
        top = sym[g]
        top_aug = aug[g]
        spread = [jnp.broadcast_to(rest[:, :, start + j:start + j + 1], (left, SUB, n)) for j in range(SUB)]
        unit = {(i, j): full(spread[j][0, i:i + 1, :]) for j in range(SUB) for i in range(j, SUB)}
        scaled = []
        scaled_aug = []
        roots = jnp.zeros((SUB, n), jnp.float32)
        for k in range(SUB):
            pivot = unit[k, k]
            guess = pl.reciprocal(pivot, approx=True)
            rest_of = 2.0 - pivot * guess
            recip = guess * rest_of
            roots = jnp.where(sub == k, pivot, roots)
            for j in range(k + 1, SUB):
                unit[j, j] = unit[j, j] - (unit[j, k] * unit[j, k] * guess) * rest_of
                for i in range(j + 1, SUB):
                    unit[i, j] = unit[i, j] - (unit[i, k] * unit[j, k] * guess) * rest_of
            for j in range(k + 1, SUB):
                factor = unit[j, k] * recip
                spread[j] = spread[j] - spread[k] * factor[None]
            row = full(top[k:k + 1, :]) * recip
            row_aug = full(top_aug[k:k + 1, :]) * recip
            scaled.append(row)
            scaled_aug.append(row_aug)
            if k + 1 < SUB:
                below = jnp.where(sub > k, spread[k][0], 0.0)
                top = top - below * row
                top_aug = top_aug - below * row_aug
        root = lax.rsqrt(roots)
        sym[g] = jnp.where(lane >= start + sub, top * root, 0.0)
        aug[g] = top_aug * root
        if left > 1:
            low = rest[1:]
            low_aug = aug[g + 1:]
            for k in range(SUB):
                low = low - spread[k][1:] * scaled[k][None]
                low_aug = low_aug - spread[k][1:] * scaled_aug[k][None]
            sym[g + 1:] = low
            aug[g + 1:] = low_aug
    upper = sym[...].reshape(n, n)
    return upper.T, aug[...].reshape(n, n)


def is_odd_row():
    return lax.rem(lax.axis_index("row"), 2) == 1


def parts(x):
    high = x.astype(jnp.bfloat16)
    rest = x - high.astype(jnp.float32)
    middle = rest.astype(jnp.bfloat16)
    return high, middle, (rest - middle.astype(jnp.float32)).astype(jnp.bfloat16)


def dot_parts(a, b, dims=((1,), (0,))):
    total = None
    for i, j in ((2, 0), (0, 2), (1, 1), (1, 0), (0, 1), (0, 0)):
        term = lax.dot_general(a[i], b[j], (dims, ((), ())), preferred_element_type=jnp.float32)
        total = term if total is None else total + term
    return total


def estimate(flops, nbytes):
    return pl.CostEstimate(flops=flops, bytes_accessed=nbytes, transcendentals=0)


def corner_kernel(matrix_ref, block_ref, sem):
    copy = pltpu.make_async_copy(matrix_ref.at[0, :, 0, :], block_ref, sem)
    copy.start()
    copy.wait()


def corner_block(matrix):
    n = matrix.shape[1]
    return pl.pallas_call(
        corner_kernel,
        out_shape=jax.ShapeDtypeStruct((n, n), jnp.float32),
        in_specs=[HBM],
        out_specs=VMEM,
        scratch_shapes=[pltpu.SemaphoreType.DMA(())],
        compiler_params=pltpu.CompilerParams(vmem_limit_bytes=2 * MIB),
        cost_estimate=estimate(0, 3 * MIB),
        name="corner_block",
    )(matrix)


def panels_kernel(matrix_ref, column_ref, upper_ref, lower_ref, sems):
    local_cols, half, _ = upper_ref.shape
    copies = [pltpu.make_async_copy(matrix_ref.at[:, :, 0, :], column_ref, sems.at[0])]
    for j in range(local_cols):
        copies.append(pltpu.make_async_copy(matrix_ref.at[0, pl.ds(0, half), j, :], upper_ref.at[j], sems.at[1 + j]))
        copies.append(pltpu.make_async_copy(
            matrix_ref.at[0, pl.ds(half, half), j, :], lower_ref.at[j], sems.at[1 + local_cols + j]))
    for copy in copies:
        copy.start()
    for copy in copies:
        copy.wait()


def panels(matrix):
    local_rows, n, local_cols, _ = matrix.shape
    strip = jax.ShapeDtypeStruct((local_cols, n // 2, n), jnp.float32)
    return pl.pallas_call(
        panels_kernel,
        out_shape=[jax.ShapeDtypeStruct((local_rows, n, n), jnp.float32), strip, strip],
        in_specs=[HBM],
        out_specs=[VMEM] * 3,
        scratch_shapes=[pltpu.SemaphoreType.DMA((1 + 2 * local_cols,))],
        compiler_params=pltpu.CompilerParams(vmem_limit_bytes=4 * MIB),
        cost_estimate=estimate(0, 4 * MIB),
        name="panels",
    )(matrix)


def first_factor_kernel(a_ref, f_ref, w_ref, sym, aug):
    f_ref[...], w_ref[...] = eliminate(a_ref[...], sym, aug)


def first_factor(a):
    n = a.shape[1]
    square = jax.ShapeDtypeStruct((n, n), jnp.float32)
    return pl.pallas_call(
        first_factor_kernel,
        out_shape=[square, square],
        in_specs=[VMEM],
        out_specs=[VMEM, VMEM],
        scratch_shapes=[pltpu.VMEM((n // SUB, SUB, n), jnp.float32)] * 2,
        compiler_params=pltpu.CompilerParams(vmem_limit_bytes=4 * MIB),
        cost_estimate=estimate(8 * 10**9, 2 * MIB),
        name="first_factor",
    )(a)


def second_factor_kernel(low_ref, a_ref, w0_ref, matrix_ref, f_ref, w_ref, mixed_ref,
                         blocks_ref, sym, aug, sems):
    n = w0_ref.shape[0]
    local_cols = matrix_ref.shape[2]
    copies = [pltpu.make_async_copy(matrix_ref.at[:, :, j, :], blocks_ref.at[j], sems.at[j]) for j in range(local_cols)]
    for copy in copies:
        copy.start()
    odd = is_odd_row()
    w0 = w0_ref[...]
    cross = dot_t(low_ref[...], w0)
    f1, w1 = eliminate(a_ref[...] - dot_t(cross, cross), sym, aug)
    f_ref[...] = f1
    w10 = -dot(w1, dot(cross, w0))
    zero = jnp.zeros((n, n), jnp.float32)
    w_ref[:n, :n] = w0
    w_ref[:n, n:] = zero
    w_ref[n:, :n] = w10
    w_ref[n:, n:] = w1
    mixed_ref[:n, :n] = jnp.where(odd, zero, w0)
    mixed_ref[:n, n:] = jnp.where(odd, w0, zero)
    mixed_ref[n:, :n] = jnp.where(odd, w1, w10)
    mixed_ref[n:, n:] = jnp.where(odd, w10, w1)
    for copy in copies:
        copy.wait()


def second_factor(low, a, w0, matrix):
    local_rows, n, local_cols, _ = matrix.shape
    square = jax.ShapeDtypeStruct((n, n), jnp.float32)
    double = jax.ShapeDtypeStruct((2 * n, 2 * n), jnp.float32)
    blocks = jax.ShapeDtypeStruct((local_cols, local_rows, n, n), jnp.float32)
    return pl.pallas_call(
        second_factor_kernel,
        out_shape=[square, double, double, blocks],
        in_specs=[VMEM] * 3 + [HBM],
        out_specs=[VMEM] * 4,
        scratch_shapes=[pltpu.VMEM((n // SUB, SUB, n), jnp.float32)] * 2 + [pltpu.SemaphoreType.DMA((local_cols,))],
        compiler_params=pltpu.CompilerParams(vmem_limit_bytes=12 * MIB),
        cost_estimate=estimate(8 * 10**9, 4 * MIB),
        name="second_factor",
    )(low, a, w0, matrix)


def settle_kernel(f0_ref, f1_ref, w_ref, mixed_ref, rows_ref, rows_other_ref, ha_ref, hb_ref, oa_ref, ob_ref, blocks_ref,
                  out_ref, result, sems):
    grid_row = lax.axis_index("row")
    grid_col = lax.axis_index("col")
    n = f0_ref.shape[0]
    local_cols, local_rows, _, _ = blocks_ref.shape
    flat = local_rows * n
    own = rows_ref[...].reshape(flat, n)
    other = rows_other_ref[...].reshape(flat, n)
    swapped = lax.rem(grid_col, 2) == 1
    rows = jnp.concatenate([jnp.where(swapped, other, own), jnp.where(swapped, own, other)], axis=1)
    solved = dot_parts(parts(rows), parts(w_ref[...]), ((1,), (1,)))
    left = parts(solved)
    mixed = parts(mixed_ref[...])
    copies = []
    for j in range(0, local_cols, 2):
        pair = (j, j + 1)
        stacked = jnp.concatenate(
            [jnp.concatenate([ha_ref[b], hb_ref[b], oa_ref[b], ob_ref[b]], axis=0) for b in pair], axis=1)
        update = dot_parts(left, parts(dot_parts(mixed, parts(stacked))))
        for b in pair:
            part = update[:, (b - j) * n:(b - j + 1) * n].reshape(local_rows, n, n)
            result[b] = blocks_ref[b] - part
        if j == 0:
            @pl.when(grid_col == 0)
            def _():
                result[0] = solved[:, :n].reshape(local_rows, n, n)

            @pl.when(grid_col == 1)
            def _():
                result[0] = solved[:, n:].reshape(local_rows, n, n)

        @pl.when(grid_row <= 1)
        def _():
            for b in pair:
                if b > 0:
                    result[b, 0] = jnp.zeros((n, n), jnp.float32)
            if j == 0:
                @pl.when(grid_col > grid_row)
                def _():
                    result[0, 0] = jnp.zeros((n, n), jnp.float32)

                @pl.when((grid_row == 0) & (grid_col == 0))
                def _():
                    result[0, 0] = f0_ref[...]

                @pl.when((grid_row == 1) & (grid_col == 1))
                def _():
                    result[0, 0] = f1_ref[...]
        for b in pair:
            copy = pltpu.make_async_copy(result.at[b], out_ref.at[:, :, b, :], sems.at[b])
            copy.start()
            copies.append(copy)
    for copy in copies:
        copy.wait()


def settle(f0, f1, w, mixed, rows, rows_other, ha, hb, oa, ob, blocks):
    local_cols, local_rows, n, _ = blocks.shape
    return pl.pallas_call(
        settle_kernel,
        out_shape=jax.ShapeDtypeStruct((local_rows, n, local_cols, n), jnp.float32),
        in_specs=[VMEM] * 11,
        out_specs=HBM,
        scratch_shapes=[pltpu.VMEM(blocks.shape, jnp.float32), pltpu.SemaphoreType.DMA((local_cols,))],
        compiler_params=pltpu.CompilerParams(vmem_limit_bytes=32 * MIB),
        cost_estimate=estimate(4 * 10**9, 6 * MIB),
        name="settle",
    )(f0, f1, w, mixed, rows, rows_other, ha, hb, oa, ob, blocks)


def exchange(value, axis, mask, size):
    return lax.ppermute(value, axis, [(i, i ^ mask) for i in range(size)])


def bit_set(index, bit):
    return ((index >> bit) & 1) == 1


def spread(own, axis, index, size, bits):
    held = own
    for bit in bits:
        held = jnp.where(bit_set(index, bit), exchange(held, axis, 1 << bit, size), held)
    return held


def region(run, *values):
    shapes = jax.eval_shape(run, *values)

    def skip(*_):
        return jax.tree.map(lambda leaf: jnp.zeros(leaf.shape, leaf.dtype), shapes)

    everywhere = lax.axis_index("row") < lax.axis_size("row")
    return lax.cond(everywhere, run, skip, *values)


def after(value, *others):
    return lax.optimization_barrier((value,) + others)


def shards(kernel):
    grid_row = lax.axis_index("row")
    grid_col = lax.axis_index("col")
    n_row = lax.axis_size("row")
    n_col = lax.axis_size("col")
    row_bits = list(range(1, n_row.bit_length() - 1))
    col_bits = list(range(1, n_col.bit_length() - 1))
    odd = (grid_row % 2) == 1
    right = (grid_col % 2) == 1

    block = corner_block(kernel)
    column, upper, lower = panels(kernel)
    first_bit, last_bit = row_bits[0], row_bits[-1]

    moved = exchange(block, "col", 1 << col_bits[0], n_col)
    upper_moved = exchange(upper, "row", 1 << first_bit, n_row)
    lower_moved = exchange(lower, "row", 1 << last_bit, n_row)

    def along_col(new, old):
        block = jnp.where(bit_set(grid_col, col_bits[0]), new, old)
        return spread(block, "col", grid_col, n_col, col_bits[1:])

    block = region(along_col, moved, block)
    across = exchange(block, "col", 1, n_col)
    ha = jnp.where(bit_set(grid_row, first_bit), upper_moved, upper)
    hb = jnp.where(bit_set(grid_row, last_bit), lower_moved, lower)
    across, block, ha, hb, column = after(across, block, ha, hb, column)

    pair = jnp.stack([jnp.where(right, across, block), jnp.where(right, block, across)])
    moved = exchange(pair, "row", 1 << first_bit, n_row)
    column_moved = exchange(column, "col", 1 << col_bits[0], n_col)

    def over_row(new, old):
        pair = jnp.where(bit_set(grid_row, first_bit), new, old)
        pair = spread(pair, "row", grid_row, n_row, row_bits[1:])
        return pair, exchange(pair, "row", 1, n_row)

    pair, other = region(over_row, moved, pair)
    pair, ha, hb = after(pair, ha, hb)
    ha_moved = exchange(ha, "row", 1 << row_bits[1], n_row)
    hb_moved = exchange(hb, "row", 1 << row_bits[-2], n_row)
    rows = jnp.where(bit_set(grid_col, col_bits[0]), column_moved, column)
    pair, other, rows = after(pair, other, rows)
    a00 = jnp.where(odd, other[0], pair[0])
    a10 = jnp.where(odd, pair[0], other[0])
    a11 = jnp.where(odd, pair[1], other[1])
    f0, w0 = first_factor(a00)

    w0, rows, row_then, col_then = after(w0, rows, grid_row, grid_col)
    ha = jnp.where(bit_set(row_then, row_bits[1]), ha_moved, ha)
    ha = spread(ha, "row", row_then, n_row, row_bits[2:])
    hb = jnp.where(bit_set(row_then, row_bits[-2]), hb_moved, hb)
    hb = spread(hb, "row", row_then, n_row, row_bits[:-2][::-1])
    rows = spread(rows, "col", col_then, n_col, col_bits[1:])
    rows_other = exchange(rows, "col", 1, n_col)
    oa = exchange(ha, "row", 1, n_row)
    ob = exchange(hb, "row", 1, n_row)
    f1, w, mixed, blocks = second_factor(a10, a11, w0, kernel)
    return settle(f0, f1, w, mixed, rows, rows_other, ha, hb, oa, ob, blocks)


def solution(mesh):
    in_specs = (P(None, "row", None, "col"),)
    out_specs = P(None, "row", None, "col")
    return jax.shard_map(shards, mesh=mesh, in_specs=in_specs, out_specs=out_specs, check_vma=False)
```

```python
import jax
import jax.numpy as jnp
from jax import lax
from jax.experimental import pallas as pl
from jax.experimental.pallas import tpu as pltpu
from jax.sharding import PartitionSpec as P

EXACT = lax.Precision.HIGHEST
SUB = 8
MIB = 1024 * 1024
VMEM = pl.BlockSpec(memory_space=pltpu.VMEM)
HBM = pl.BlockSpec(memory_space=pltpu.HBM)


def dot(a, b):
    return lax.dot_general(a, b, (((1,), (0,)), ((), ())), precision=EXACT, preferred_element_type=jnp.float32)


def dot_t(a, b):
    return lax.dot_general(a, b, (((1,), (1,)), ((), ())), precision=EXACT, preferred_element_type=jnp.float32)


def full(row):
    return jnp.broadcast_to(row, (SUB, row.shape[-1]))


def eliminate(s, extra, scratch):
    n = s.shape[0]
    groups = n // SUB
    sub = lax.broadcasted_iota(jnp.int32, (SUB, n), 0)
    lane = lax.broadcasted_iota(jnp.int32, (SUB, n), 1)
    rows = lax.broadcasted_iota(jnp.int32, (n, n), 0)
    cols = lax.broadcasted_iota(jnp.int32, (n, n), 1)
    for ref, value in zip(scratch, (s, jnp.where(rows == cols, 1.0, 0.0), extra)):
        ref[...] = value.reshape(groups, SUB, n)
    sides = range(len(scratch))
    for g in range(groups):
        start = g * SUB
        left = groups - g
        rest = scratch[0][g:]
        spread = [jnp.broadcast_to(rest[:, :, start + j:start + j + 1], (left, SUB, n)) for j in range(SUB)]
        unit = {(i, j): full(spread[j][0, i:i + 1, :]) for j in range(SUB) for i in range(j, SUB)}
        row = [[full(ref[g, k:k + 1, :]) for k in range(SUB)] for ref in scratch]
        scaled = [[] for _ in sides]
        tops = [None for _ in sides]
        for k in range(SUB):
            pivot = unit[k, k]
            guess = pl.reciprocal(pivot, approx=True)
            rest_of = 2.0 - pivot * guess
            recip = guess * rest_of
            root = lax.rsqrt(pivot)
            for j in range(k + 1, SUB):
                for i in range(j, SUB):
                    unit[i, j] = unit[i, j] - (unit[i, k] * unit[j, k] * guess) * rest_of
            factors = {j: unit[j, k] * recip for j in range(k + 1, SUB)}
            for j in range(k + 1, SUB):
                spread[j] = spread[j] - spread[k] * factors[j][None]
            for m in sides:
                for j in range(k + 1, SUB):
                    row[m][j] = row[m][j] - row[m][k] * factors[j]
                scaled[m].append(row[m][k] * recip)
                final = row[m][k] * root
                tops[m] = final if k == 0 else jnp.where(sub == k, final, tops[m])
        scratch[0][g] = jnp.where(lane >= start + sub, tops[0], 0.0)
        for m in sides[1:]:
            scratch[m][g] = tops[m]
        if left > 1:
            for m in sides:
                low = scratch[m][g + 1:]
                for k in range(SUB):
                    low = low - spread[k][1:] * scaled[m][k][None]
                scratch[m][g + 1:] = low
    upper, inverse, product = [ref[...].reshape(n, n) for ref in scratch]
    return upper.T, inverse, product


def is_odd_row():
    return lax.rem(lax.axis_index("row"), 2) == 1


def parts(x):
    high = x.astype(jnp.bfloat16)
    rest = x - high.astype(jnp.float32)
    middle = rest.astype(jnp.bfloat16)
    return high, middle, (rest - middle.astype(jnp.float32)).astype(jnp.bfloat16)


def dot_parts(a, b, dims=((1,), (0,))):
    total = None
    for i, j in ((2, 0), (0, 2), (1, 1), (1, 0), (0, 1), (0, 0)):
        term = lax.dot_general(a[i], b[j], (dims, ((), ())), preferred_element_type=jnp.float32)
        total = term if total is None else total + term
    return total


def estimate(flops, nbytes):
    return pl.CostEstimate(flops=flops, bytes_accessed=nbytes, transcendentals=0)


def corner_kernel(matrix_ref, block_ref, sem):
    copy = pltpu.make_async_copy(matrix_ref.at[0, :, 0, :], block_ref, sem)
    copy.start()
    copy.wait()


def corner_block(matrix):
    n = matrix.shape[1]
    return pl.pallas_call(
        corner_kernel,
        out_shape=jax.ShapeDtypeStruct((n, n), jnp.float32),
        in_specs=[HBM],
        out_specs=VMEM,
        scratch_shapes=[pltpu.SemaphoreType.DMA(())],
        compiler_params=pltpu.CompilerParams(vmem_limit_bytes=2 * MIB),
        cost_estimate=estimate(0, 3 * MIB),
        name="corner_block",
    )(matrix)


def panels_kernel(matrix_ref, column_ref, upper_ref, lower_ref, sems):
    local_cols, half, _ = upper_ref.shape
    copies = [pltpu.make_async_copy(matrix_ref.at[:, :, 0, :], column_ref, sems.at[0])]
    for j in range(local_cols):
        copies.append(pltpu.make_async_copy(matrix_ref.at[0, pl.ds(0, half), j, :], upper_ref.at[j], sems.at[1 + j]))
        copies.append(pltpu.make_async_copy(
            matrix_ref.at[0, pl.ds(half, half), j, :], lower_ref.at[j], sems.at[1 + local_cols + j]))
    for copy in copies:
        copy.start()
    for copy in copies:
        copy.wait()


def panels(matrix):
    local_rows, n, local_cols, _ = matrix.shape
    strip = jax.ShapeDtypeStruct((local_cols, n // 2, n), jnp.float32)
    return pl.pallas_call(
        panels_kernel,
        out_shape=[jax.ShapeDtypeStruct((local_rows, n, n), jnp.float32), strip, strip],
        in_specs=[HBM],
        out_specs=[VMEM] * 3,
        scratch_shapes=[pltpu.SemaphoreType.DMA((1 + 2 * local_cols,))],
        compiler_params=pltpu.CompilerParams(vmem_limit_bytes=4 * MIB),
        cost_estimate=estimate(0, 4 * MIB),
        name="panels",
    )(matrix)


def first_factor_kernel(a_ref, side_ref, f_ref, w_ref, cross_ref, *scratch):
    f_ref[...], w_ref[...], cross_ref[...] = eliminate(a_ref[...], side_ref[...], scratch)


def elimination_scratch(n):
    return [pltpu.VMEM((n // SUB, SUB, n), jnp.float32)] * 3


def first_factor(a, side):
    n = a.shape[1]
    square = jax.ShapeDtypeStruct((n, n), jnp.float32)
    return pl.pallas_call(
        first_factor_kernel,
        out_shape=[square] * 3,
        in_specs=[VMEM] * 2,
        out_specs=[VMEM] * 3,
        scratch_shapes=elimination_scratch(n),
        compiler_params=pltpu.CompilerParams(vmem_limit_bytes=4 * MIB),
        cost_estimate=estimate(8 * 10**9, 2 * MIB),
        name="first_factor",
    )(a, side)


def second_factor_kernel(a_ref, cross_ref, w0_ref, matrix_ref, f_ref, w_ref, mixed_ref, blocks_ref, *scratch):
    n = w0_ref.shape[0]
    local_cols = matrix_ref.shape[2]
    sems = scratch[-1]
    copies = [pltpu.make_async_copy(matrix_ref.at[:, :, j, :], blocks_ref.at[j], sems.at[j]) for j in range(local_cols)]
    for copy in copies:
        copy.start()
    odd = is_odd_row()
    w0 = w0_ref[...]
    cross = cross_ref[...]
    both = dot(cross.T, jnp.concatenate([cross, w0], axis=1))
    f1, w1, w10 = eliminate(a_ref[...] - both[:, :n], -both[:, n:], scratch[:-1])
    f_ref[...] = f1
    zero = jnp.zeros((n, n), jnp.float32)
    w_ref[:n, :n] = w0
    w_ref[:n, n:] = zero
    w_ref[n:, :n] = w10
    w_ref[n:, n:] = w1
    mixed_ref[:n, :n] = jnp.where(odd, zero, w0)
    mixed_ref[:n, n:] = jnp.where(odd, w0, zero)
    mixed_ref[n:, :n] = jnp.where(odd, w1, w10)
    mixed_ref[n:, n:] = jnp.where(odd, w10, w1)
    for copy in copies:
        copy.wait()


def second_factor(a, cross, w0, matrix):
    local_rows, n, local_cols, _ = matrix.shape
    square = jax.ShapeDtypeStruct((n, n), jnp.float32)
    double = jax.ShapeDtypeStruct((2 * n, 2 * n), jnp.float32)
    blocks = jax.ShapeDtypeStruct((local_cols, local_rows, n, n), jnp.float32)
    return pl.pallas_call(
        second_factor_kernel,
        out_shape=[square, double, double, blocks],
        in_specs=[VMEM] * 3 + [HBM],
        out_specs=[VMEM] * 4,
        scratch_shapes=elimination_scratch(n) + [pltpu.SemaphoreType.DMA((local_cols,))],
        compiler_params=pltpu.CompilerParams(vmem_limit_bytes=12 * MIB),
        cost_estimate=estimate(8 * 10**9, 4 * MIB),
        name="second_factor",
    )(a, cross, w0, matrix)


def settle_kernel(f0_ref, f1_ref, w_ref, mixed_ref, rows_ref, rows_other_ref, ha_ref, hb_ref, oa_ref, ob_ref, blocks_ref,
                  out_ref, result, sems):
    grid_row = lax.axis_index("row")
    grid_col = lax.axis_index("col")
    n = f0_ref.shape[0]
    local_cols, local_rows, _, _ = blocks_ref.shape
    flat = local_rows * n
    own = rows_ref[...].reshape(flat, n)
    other = rows_other_ref[...].reshape(flat, n)
    swapped = lax.rem(grid_col, 2) == 1
    rows = jnp.concatenate([jnp.where(swapped, other, own), jnp.where(swapped, own, other)], axis=1)
    solved = dot_parts(parts(rows), parts(w_ref[...]), ((1,), (1,)))
    left = parts(solved)
    mixed = parts(mixed_ref[...])
    copies = []
    for j in range(0, local_cols, 2):
        pair = (j, j + 1)
        stacked = jnp.concatenate(
            [jnp.concatenate([ha_ref[b], hb_ref[b], oa_ref[b], ob_ref[b]], axis=0) for b in pair], axis=1)
        update = dot_parts(left, parts(dot_parts(mixed, parts(stacked))))
        for b in pair:
            part = update[:, (b - j) * n:(b - j + 1) * n].reshape(local_rows, n, n)
            result[b] = blocks_ref[b] - part
        if j == 0:
            @pl.when(grid_col == 0)
            def _():
                result[0] = solved[:, :n].reshape(local_rows, n, n)

            @pl.when(grid_col == 1)
            def _():
                result[0] = solved[:, n:].reshape(local_rows, n, n)

        @pl.when(grid_row <= 1)
        def _():
            for b in pair:
                if b > 0:
                    result[b, 0] = jnp.zeros((n, n), jnp.float32)
            if j == 0:
                @pl.when(grid_col > grid_row)
                def _():
                    result[0, 0] = jnp.zeros((n, n), jnp.float32)

                @pl.when((grid_row == 0) & (grid_col == 0))
                def _():
                    result[0, 0] = f0_ref[...]

                @pl.when((grid_row == 1) & (grid_col == 1))
                def _():
                    result[0, 0] = f1_ref[...]
        for b in pair:
            copy = pltpu.make_async_copy(result.at[b], out_ref.at[:, :, b, :], sems.at[b])
            copy.start()
            copies.append(copy)
    for copy in copies:
        copy.wait()


def settle(f0, f1, w, mixed, rows, rows_other, ha, hb, oa, ob, blocks):
    local_cols, local_rows, n, _ = blocks.shape
    return pl.pallas_call(
        settle_kernel,
        out_shape=jax.ShapeDtypeStruct((local_rows, n, local_cols, n), jnp.float32),
        in_specs=[VMEM] * 11,
        out_specs=HBM,
        scratch_shapes=[pltpu.VMEM(blocks.shape, jnp.float32), pltpu.SemaphoreType.DMA((local_cols,))],
        compiler_params=pltpu.CompilerParams(vmem_limit_bytes=32 * MIB),
        cost_estimate=estimate(4 * 10**9, 6 * MIB),
        name="settle",
    )(f0, f1, w, mixed, rows, rows_other, ha, hb, oa, ob, blocks)


def exchange(value, axis, mask, size):
    return lax.ppermute(value, axis, [(i, i ^ mask) for i in range(size)])


def bit_set(index, bit):
    return ((index >> bit) & 1) == 1


def spread(own, axis, index, size, bits):
    held = own
    for bit in bits:
        held = jnp.where(bit_set(index, bit), exchange(held, axis, 1 << bit, size), held)
    return held


def region(run, *values):
    shapes = jax.eval_shape(run, *values)

    def skip(*_):
        return jax.tree.map(lambda leaf: jnp.zeros(leaf.shape, leaf.dtype), shapes)

    everywhere = lax.axis_index("row") < lax.axis_size("row")
    return lax.cond(everywhere, run, skip, *values)


def after(value, *others):
    return lax.optimization_barrier((value,) + others)


def shards(kernel):
    grid_row = lax.axis_index("row")
    grid_col = lax.axis_index("col")
    n_row = lax.axis_size("row")
    n_col = lax.axis_size("col")
    row_bits = list(range(1, n_row.bit_length() - 1))
    col_bits = list(range(1, n_col.bit_length() - 1))
    odd = (grid_row % 2) == 1
    right = (grid_col % 2) == 1

    block = corner_block(kernel)
    block, kernel_then = after(block, kernel)
    column, upper, lower = panels(kernel_then)
    first_bit, last_bit = row_bits[0], row_bits[-1]

    moved = exchange(block, "col", 1 << col_bits[0], n_col)
    upper_moved = exchange(upper, "row", 1 << first_bit, n_row)
    lower_moved = exchange(lower, "row", 1 << last_bit, n_row)

    def along_col(new, old):
        block = jnp.where(bit_set(grid_col, col_bits[0]), new, old)
        return spread(block, "col", grid_col, n_col, col_bits[1:])

    block = region(along_col, moved, block)
    across = exchange(block, "col", 1, n_col)
    ha = jnp.where(bit_set(grid_row, first_bit), upper_moved, upper)
    hb = jnp.where(bit_set(grid_row, last_bit), lower_moved, lower)
    across, block, ha, hb, column = after(across, block, ha, hb, column)

    pair = jnp.stack([jnp.where(right, across, block), jnp.where(right, block, across)])
    pair, column = after(pair, column)
    moved = exchange(pair, "row", 1 << first_bit, n_row)
    column_moved = exchange(column, "col", 1 << col_bits[0], n_col)

    def over_row(new, old):
        pair = jnp.where(bit_set(grid_row, first_bit), new, old)
        pair = spread(pair, "row", grid_row, n_row, row_bits[1:])
        return pair, exchange(pair, "row", 1, n_row)

    pair, other = region(over_row, moved, pair)
    pair, ha, hb = after(pair, ha, hb)
    ha_moved = exchange(ha, "row", 1 << row_bits[1], n_row)
    hb_moved = exchange(hb, "row", 1 << row_bits[-2], n_row)
    rows = jnp.where(bit_set(grid_col, col_bits[0]), column_moved, column)
    pair, other, rows = after(pair, other, rows)
    a00 = jnp.where(odd, other[0], pair[0])
    a01 = jnp.where(odd, other[1], pair[1])
    a11 = jnp.where(odd, pair[1], other[1])
    f0, w0, cross = first_factor(a00, a01)

    w0, rows, row_then, col_then = after(w0, rows, grid_row, grid_col)
    ha = jnp.where(bit_set(row_then, row_bits[1]), ha_moved, ha)
    ha = spread(ha, "row", row_then, n_row, row_bits[2:])
    hb = jnp.where(bit_set(row_then, row_bits[-2]), hb_moved, hb)
    hb = spread(hb, "row", row_then, n_row, row_bits[:-2][::-1])
    rows = spread(rows, "col", col_then, n_col, col_bits[1:])
    rows_other = exchange(rows, "col", 1, n_col)
    oa = exchange(ha, "row", 1, n_row)
    ob = exchange(hb, "row", 1, n_row)
    f1, w, mixed, blocks = second_factor(a11, cross, w0, kernel)
    return settle(f0, f1, w, mixed, rows, rows_other, ha, hb, oa, ob, blocks)


def solution(mesh):
    in_specs = (P(None, "row", None, "col"),)
    out_specs = P(None, "row", None, "col")
    return jax.shard_map(shards, mesh=mesh, in_specs=in_specs, out_specs=out_specs, check_vma=False)
```

```python
import jax
import jax.numpy as jnp
from jax import lax
from jax.experimental import pallas as pl
from jax.experimental.pallas import tpu as pltpu
from jax.sharding import PartitionSpec as P

EXACT = lax.Precision.HIGHEST
SUB = 8
PANEL = 4
MIB = 1024 * 1024
VMEM = pl.BlockSpec(memory_space=pltpu.VMEM)
HBM = pl.BlockSpec(memory_space=pltpu.HBM)


def dot(a, b):
    return lax.dot_general(a, b, (((1,), (0,)), ((), ())), precision=EXACT, preferred_element_type=jnp.float32)


def dot_t(a, b):
    return lax.dot_general(a, b, (((1,), (1,)), ((), ())), precision=EXACT, preferred_element_type=jnp.float32)


def full(row):
    return jnp.broadcast_to(row, (SUB, row.shape[-1]))


def eliminate(s, extra, scratch):
    n = s.shape[0]
    groups = n // SUB
    sub = lax.broadcasted_iota(jnp.int32, (SUB, n), 0)
    lane = lax.broadcasted_iota(jnp.int32, (SUB, n), 1)
    rows = lax.broadcasted_iota(jnp.int32, (n, n), 0)
    cols = lax.broadcasted_iota(jnp.int32, (n, n), 1)
    for ref, value in zip(scratch, (s, jnp.where(rows == cols, 1.0, 0.0), extra)):
        ref[...] = value.reshape(groups, SUB, n)
    sides = range(len(scratch))
    for g in range(groups):
        start = g * SUB
        until = (g // PANEL + 1) * PANEL
        left = until - g
        rest = scratch[0][g:until]
        spread = [jnp.broadcast_to(rest[:, :, start + j:start + j + 1], (left, SUB, n)) for j in range(SUB)]
        unit = {(i, j): full(spread[j][0, i:i + 1, :]) for j in range(SUB) for i in range(j, SUB)}
        row = [[full(ref[g, k:k + 1, :]) for k in range(SUB)] for ref in scratch]
        scaled = [[] for _ in sides]
        tops = [None for _ in sides]
        for k in range(SUB):
            pivot = unit[k, k]
            guess = pl.reciprocal(pivot, approx=True)
            rest_of = 2.0 - pivot * guess
            recip = guess * rest_of
            root = lax.rsqrt(pivot)
            for j in range(k + 1, SUB):
                for i in range(j, SUB):
                    unit[i, j] = unit[i, j] - (unit[i, k] * unit[j, k] * guess) * rest_of
            factors = {j: unit[j, k] * recip for j in range(k + 1, SUB)}
            for j in range(k + 1, SUB):
                spread[j] = spread[j] - spread[k] * factors[j][None]
            for m in sides:
                for j in range(k + 1, SUB):
                    row[m][j] = row[m][j] - row[m][k] * factors[j]
                scaled[m].append(row[m][k] * recip)
                final = row[m][k] * root
                tops[m] = final if k == 0 else jnp.where(sub == k, final, tops[m])
        scratch[0][g] = jnp.where(lane >= start + sub, tops[0], 0.0)
        for m in sides[1:]:
            scratch[m][g] = tops[m]
        if left > 1:
            for m in sides:
                low = scratch[m][g + 1:until]
                for k in range(SUB):
                    low = low - spread[k][1:] * scaled[m][k][None]
                scratch[m][g + 1:until] = low
        elif until < groups:
            done = [ref[until - PANEL:until].reshape(PANEL * SUB, n) for ref in scratch]
            update = lax.dot_general(
                done[0], jnp.concatenate(done, axis=1), (((0,), (0,)), ((), ())), precision=EXACT,
                preferred_element_type=jnp.float32)
            for m in sides:
                part = update[until * SUB:, m * n:(m + 1) * n]
                scratch[m][until:] = scratch[m][until:] - part.reshape(groups - until, SUB, n)
    upper, inverse, product = [ref[...].reshape(n, n) for ref in scratch]
    return upper.T, inverse, product


def is_odd_row():
    return lax.rem(lax.axis_index("row"), 2) == 1


def parts(x):
    high = x.astype(jnp.bfloat16)
    rest = x - high.astype(jnp.float32)
    middle = rest.astype(jnp.bfloat16)
    return high, middle, (rest - middle.astype(jnp.float32)).astype(jnp.bfloat16)


def dot_parts(a, b, dims=((1,), (0,))):
    total = None
    for i, j in ((2, 0), (0, 2), (1, 1), (1, 0), (0, 1), (0, 0)):
        term = lax.dot_general(a[i], b[j], (dims, ((), ())), preferred_element_type=jnp.float32)
        total = term if total is None else total + term
    return total


def estimate(flops, nbytes):
    return pl.CostEstimate(flops=flops, bytes_accessed=nbytes, transcendentals=0)


def corner_kernel(matrix_ref, block_ref, sem):
    copy = pltpu.make_async_copy(matrix_ref.at[0, :, 0, :], block_ref, sem)
    copy.start()
    copy.wait()


def corner_block(matrix):
    n = matrix.shape[1]
    return pl.pallas_call(
        corner_kernel,
        out_shape=jax.ShapeDtypeStruct((n, n), jnp.float32),
        in_specs=[HBM],
        out_specs=VMEM,
        scratch_shapes=[pltpu.SemaphoreType.DMA(())],
        compiler_params=pltpu.CompilerParams(vmem_limit_bytes=2 * MIB),
        cost_estimate=estimate(0, 3 * MIB),
        name="corner_block",
    )(matrix)


def panels_kernel(matrix_ref, column_ref, upper_ref, lower_ref, sems):
    local_cols, half, _ = upper_ref.shape
    copies = [pltpu.make_async_copy(matrix_ref.at[pl.ds(1, column_ref.shape[0]), :, 0, :], column_ref, sems.at[0])]
    for j in range(local_cols):
        copies.append(pltpu.make_async_copy(matrix_ref.at[0, pl.ds(0, half), j, :], upper_ref.at[j], sems.at[1 + j]))
        copies.append(pltpu.make_async_copy(
            matrix_ref.at[0, pl.ds(half, half), j, :], lower_ref.at[j], sems.at[1 + local_cols + j]))
    for copy in copies:
        copy.start()
    for copy in copies:
        copy.wait()


def panels(matrix):
    local_rows, n, local_cols, _ = matrix.shape
    strip = jax.ShapeDtypeStruct((local_cols, n // 2, n), jnp.float32)
    return pl.pallas_call(
        panels_kernel,
        out_shape=[jax.ShapeDtypeStruct((local_rows - 1, n, n), jnp.float32), strip, strip],
        in_specs=[HBM],
        out_specs=[VMEM] * 3,
        scratch_shapes=[pltpu.SemaphoreType.DMA((1 + 2 * local_cols,))],
        compiler_params=pltpu.CompilerParams(vmem_limit_bytes=4 * MIB),
        cost_estimate=estimate(0, 4 * MIB),
        name="panels",
    )(matrix)


def first_factor_kernel(a_ref, side_ref, f_ref, w_ref, cross_ref, *scratch):
    f_ref[...], w_ref[...], cross_ref[...] = eliminate(a_ref[...], side_ref[...], scratch)


def elimination_scratch(n):
    return [pltpu.VMEM((n // SUB, SUB, n), jnp.float32)] * 3


def first_factor(a, side):
    n = a.shape[1]
    square = jax.ShapeDtypeStruct((n, n), jnp.float32)
    return pl.pallas_call(
        first_factor_kernel,
        out_shape=[square] * 3,
        in_specs=[VMEM] * 2,
        out_specs=[VMEM] * 3,
        scratch_shapes=elimination_scratch(n),
        compiler_params=pltpu.CompilerParams(vmem_limit_bytes=4 * MIB),
        cost_estimate=estimate(8 * 10**9, 2 * MIB),
        name="first_factor",
    )(a, side)


def second_factor_kernel(a_ref, cross_ref, w0_ref, matrix_ref, f_ref, w_ref, mixed_ref, blocks_ref, *scratch):
    n = w0_ref.shape[0]
    local_cols = matrix_ref.shape[2]
    sems = scratch[-1]
    copies = [pltpu.make_async_copy(matrix_ref.at[:, :, j, :], blocks_ref.at[j], sems.at[j]) for j in range(local_cols)]
    for copy in copies:
        copy.start()
    odd = is_odd_row()
    w0 = w0_ref[...]
    cross = cross_ref[...]
    both = dot(cross.T, jnp.concatenate([cross, w0], axis=1))
    f1, w1, w10 = eliminate(a_ref[...] - both[:, :n], -both[:, n:], scratch[:-1])
    f_ref[...] = f1
    zero = jnp.zeros((n, n), jnp.float32)
    w_ref[:n, :n] = w0
    w_ref[:n, n:] = zero
    w_ref[n:, :n] = w10
    w_ref[n:, n:] = w1
    mixed_ref[:n, :n] = jnp.where(odd, zero, w0)
    mixed_ref[:n, n:] = jnp.where(odd, w0, zero)
    mixed_ref[n:, :n] = jnp.where(odd, w1, w10)
    mixed_ref[n:, n:] = jnp.where(odd, w10, w1)
    for copy in copies:
        copy.wait()


def second_factor(a, cross, w0, matrix):
    local_rows, n, local_cols, _ = matrix.shape
    square = jax.ShapeDtypeStruct((n, n), jnp.float32)
    double = jax.ShapeDtypeStruct((2 * n, 2 * n), jnp.float32)
    blocks = jax.ShapeDtypeStruct((local_cols, local_rows, n, n), jnp.float32)
    return pl.pallas_call(
        second_factor_kernel,
        out_shape=[square, double, double, blocks],
        in_specs=[VMEM] * 3 + [HBM],
        out_specs=[VMEM] * 4,
        scratch_shapes=elimination_scratch(n) + [pltpu.SemaphoreType.DMA((local_cols,))],
        compiler_params=pltpu.CompilerParams(vmem_limit_bytes=12 * MIB),
        cost_estimate=estimate(8 * 10**9, 4 * MIB),
        name="second_factor",
    )(a, cross, w0, matrix)


def settle_kernel(f0_ref, f1_ref, w_ref, mixed_ref, first_ref, rows_ref, rows_other_ref, ha_ref, hb_ref, oa_ref, ob_ref,
                  blocks_ref, out_ref, result, sems):
    grid_row = lax.axis_index("row")
    grid_col = lax.axis_index("col")
    n = f0_ref.shape[0]
    local_cols, local_rows, _, _ = blocks_ref.shape
    flat = (local_rows - 1) * n
    own = rows_ref[...].reshape(flat, n)
    other = rows_other_ref[...].reshape(flat, n)
    swapped = lax.rem(grid_col, 2) == 1
    rows = jnp.concatenate([
        jnp.concatenate([first_ref[0], jnp.where(swapped, other, own)], axis=0),
        jnp.concatenate([first_ref[1], jnp.where(swapped, own, other)], axis=0)], axis=1)
    solved = dot_parts(parts(rows), parts(w_ref[...]), ((1,), (1,)))
    left = parts(solved)
    mixed = parts(mixed_ref[...])
    copies = []
    for j in range(0, local_cols, 2):
        pair = (j, j + 1)
        stacked = jnp.concatenate(
            [jnp.concatenate([ha_ref[b], hb_ref[b], oa_ref[b], ob_ref[b]], axis=0) for b in pair], axis=1)
        update = dot_parts(left, parts(dot_parts(mixed, parts(stacked))))
        for b in pair:
            part = update[:, (b - j) * n:(b - j + 1) * n].reshape(local_rows, n, n)
            result[b] = blocks_ref[b] - part
        if j == 0:
            @pl.when(grid_col == 0)
            def _():
                result[0] = solved[:, :n].reshape(local_rows, n, n)

            @pl.when(grid_col == 1)
            def _():
                result[0] = solved[:, n:].reshape(local_rows, n, n)

        @pl.when(grid_row <= 1)
        def _():
            for b in pair:
                if b > 0:
                    result[b, 0] = jnp.zeros((n, n), jnp.float32)
            if j == 0:
                @pl.when(grid_col > grid_row)
                def _():
                    result[0, 0] = jnp.zeros((n, n), jnp.float32)

                @pl.when((grid_row == 0) & (grid_col == 0))
                def _():
                    result[0, 0] = f0_ref[...]

                @pl.when((grid_row == 1) & (grid_col == 1))
                def _():
                    result[0, 0] = f1_ref[...]
        for b in pair:
            copy = pltpu.make_async_copy(result.at[b], out_ref.at[:, :, b, :], sems.at[b])
            copy.start()
            copies.append(copy)
    for copy in copies:
        copy.wait()


def settle(f0, f1, w, mixed, first_rows, rows, rows_other, ha, hb, oa, ob, blocks):
    local_cols, local_rows, n, _ = blocks.shape
    return pl.pallas_call(
        settle_kernel,
        out_shape=jax.ShapeDtypeStruct((local_rows, n, local_cols, n), jnp.float32),
        in_specs=[VMEM] * 12,
        out_specs=HBM,
        scratch_shapes=[pltpu.VMEM(blocks.shape, jnp.float32), pltpu.SemaphoreType.DMA((local_cols,))],
        compiler_params=pltpu.CompilerParams(vmem_limit_bytes=32 * MIB),
        cost_estimate=estimate(4 * 10**9, 6 * MIB),
        name="settle",
    )(f0, f1, w, mixed, first_rows, rows, rows_other, ha, hb, oa, ob, blocks)


def exchange(value, axis, mask, size):
    return lax.ppermute(value, axis, [(i, i ^ mask) for i in range(size)])


def bit_set(index, bit):
    return ((index >> bit) & 1) == 1


def spread(own, axis, index, size, bits):
    held = own
    for bit in bits:
        held = jnp.where(bit_set(index, bit), exchange(held, axis, 1 << bit, size), held)
    return held


def region(run, *values):
    shapes = jax.eval_shape(run, *values)

    def skip(*_):
        return jax.tree.map(lambda leaf: jnp.zeros(leaf.shape, leaf.dtype), shapes)

    everywhere = lax.axis_index("row") < lax.axis_size("row")
    return lax.cond(everywhere, run, skip, *values)


def after(value, *others):
    return lax.optimization_barrier((value,) + others)


def shards(kernel):
    grid_row = lax.axis_index("row")
    grid_col = lax.axis_index("col")
    n_row = lax.axis_size("row")
    n_col = lax.axis_size("col")
    row_bits = list(range(1, n_row.bit_length() - 1))
    col_bits = list(range(1, n_col.bit_length() - 1))
    odd = (grid_row % 2) == 1
    right = (grid_col % 2) == 1

    block = corner_block(kernel)
    column, upper, lower = panels(kernel)
    first_bit, last_bit = row_bits[0], row_bits[-1]

    moved = exchange(block, "col", 1 << col_bits[0], n_col)
    upper_moved = exchange(upper, "row", 1 << first_bit, n_row)
    lower_moved = exchange(lower, "row", 1 << last_bit, n_row)

    def along_col(new, old):
        block = jnp.where(bit_set(grid_col, col_bits[0]), new, old)
        return spread(block, "col", grid_col, n_col, col_bits[1:])

    block = region(along_col, moved, block)
    across = exchange(block, "col", 1, n_col)
    ha = jnp.where(bit_set(grid_row, first_bit), upper_moved, upper)
    hb = jnp.where(bit_set(grid_row, last_bit), lower_moved, lower)
    across, block, ha, hb, column = after(across, block, ha, hb, column)

    pair = jnp.stack([jnp.where(right, across, block), jnp.where(right, block, across)])
    first_rows = pair
    moved = exchange(pair, "row", 1 << first_bit, n_row)
    column_moved = exchange(column, "col", 1 << col_bits[0], n_col)
    pair = jnp.where(bit_set(grid_row, first_bit), moved, pair)
    pair = spread(pair, "row", grid_row, n_row, row_bits[1:])
    pair, ha, hb = after(pair, ha, hb)
    ha_moved = exchange(ha, "row", 1 << row_bits[1], n_row)
    hb_moved = exchange(hb, "row", 1 << row_bits[-2], n_row)
    rows = jnp.where(bit_set(grid_col, col_bits[0]), column_moved, column)
    pair, rows = after(pair, rows)
    other = exchange(pair, "row", 1, n_row)

    a00 = jnp.where(odd, other[0], pair[0])
    a01 = jnp.where(odd, other[1], pair[1])
    a11 = jnp.where(odd, pair[1], other[1])
    f0, w0, cross = first_factor(a00, a01)

    w0, rows, row_then, col_then = after(w0, rows, grid_row, grid_col)
    ha = jnp.where(bit_set(row_then, row_bits[1]), ha_moved, ha)
    ha = spread(ha, "row", row_then, n_row, row_bits[2:])
    hb = jnp.where(bit_set(row_then, row_bits[-2]), hb_moved, hb)
    hb = spread(hb, "row", row_then, n_row, row_bits[:-2][::-1])
    rows = spread(rows, "col", col_then, n_col, col_bits[1:])
    rows_other = exchange(rows, "col", 1, n_col)
    oa = exchange(ha, "row", 1, n_row)
    ob = exchange(hb, "row", 1, n_row)
    f1, w, mixed, blocks = second_factor(a11, cross, w0, kernel)
    return settle(f0, f1, w, mixed, first_rows, rows, rows_other, ha, hb, oa, ob, blocks)


def solution(mesh):
    in_specs = (P(None, "row", None, "col"),)
    out_specs = P(None, "row", None, "col")
    return jax.shard_map(shards, mesh=mesh, in_specs=in_specs, out_specs=out_specs, check_vma=False)
```

```python
import functools

import jax
import jax.numpy as jnp
from jax import lax
from jax.experimental import pallas as pl
from jax.experimental.pallas import tpu as pltpu
from jax.sharding import PartitionSpec as P

SUB = 8
PANEL = 4
MIB = 1024 * 1024
VMEM = pl.BlockSpec(memory_space=pltpu.VMEM)
HBM = pl.BlockSpec(memory_space=pltpu.HBM)


def parts(x):
    high = x.astype(jnp.bfloat16)
    rest = x - high.astype(jnp.float32)
    middle = rest.astype(jnp.bfloat16)
    return high, middle, (rest - middle.astype(jnp.float32)).astype(jnp.bfloat16)


def dot_over_rows(a, b):
    a, b = parts(a), parts(b)
    lhs = jnp.concatenate([a[2], a[0], a[1], a[1], a[0], a[0]], axis=0)
    rhs = jnp.concatenate([b[0], b[2], b[1], b[0], b[1], b[0]], axis=0)
    return lax.dot_general(lhs, rhs, (((0,), (0,)), ((), ())), preferred_element_type=jnp.float32)


def full(row):
    return jnp.broadcast_to(row, (SUB, row.shape[-1]))


def eliminate(s, extra, scratch):
    n = s.shape[0]
    groups = n // SUB
    sub = lax.broadcasted_iota(jnp.int32, (SUB, n), 0)
    lane = lax.broadcasted_iota(jnp.int32, (SUB, n), 1)
    rows = lax.broadcasted_iota(jnp.int32, (n, n), 0)
    cols = lax.broadcasted_iota(jnp.int32, (n, n), 1)
    for ref, value in zip(scratch, (s, jnp.where(rows == cols, 1.0, 0.0), extra)):
        ref[...] = value.reshape(groups, SUB, n)
    sides = range(len(scratch))
    for g in range(groups):
        start = g * SUB
        until = (g // PANEL + 1) * PANEL
        left = until - g
        rest = scratch[0][g:until]
        spread = [jnp.broadcast_to(rest[:, :, start + j:start + j + 1], (left, SUB, n)) for j in range(SUB)]
        unit = {(i, j): full(spread[j][0, i:i + 1, :]) for j in range(SUB) for i in range(j, SUB)}
        row = [[full(ref[g, k:k + 1, :]) for k in range(SUB)] for ref in scratch]
        scaled = [[] for _ in sides]
        tops = [None for _ in sides]
        for k in range(SUB):
            pivot = unit[k, k]
            guess = pl.reciprocal(pivot, approx=True)
            rest_of = 2.0 - pivot * guess
            recip = guess * rest_of
            root = lax.rsqrt(pivot)
            for j in range(k + 1, SUB):
                for i in range(j, SUB):
                    unit[i, j] = unit[i, j] - (unit[i, k] * unit[j, k] * guess) * rest_of
            factors = {j: unit[j, k] * recip for j in range(k + 1, SUB)}
            for j in range(k + 1, SUB):
                spread[j] = spread[j] - spread[k] * factors[j][None]
            for m in sides:
                for j in range(k + 1, SUB):
                    row[m][j] = row[m][j] - row[m][k] * factors[j]
                scaled[m].append(row[m][k] * recip)
                final = row[m][k] * root
                tops[m] = final if k == 0 else jnp.where(sub == k, final, tops[m])
        scratch[0][g] = jnp.where(lane >= start + sub, tops[0], 0.0)
        for m in sides[1:]:
            scratch[m][g] = tops[m]
        if left > 1:
            for m in sides:
                low = scratch[m][g + 1:until]
                for k in range(SUB):
                    low = low - spread[k][1:] * scaled[m][k][None]
                scratch[m][g + 1:until] = low
        elif until < groups:
            done = [ref[until - PANEL:until].reshape(PANEL * SUB, n) for ref in scratch]
            update = dot_over_rows(done[0], jnp.concatenate(done, axis=1))
            for m in sides:
                part = update[until * SUB:, m * n:(m + 1) * n]
                scratch[m][until:] = scratch[m][until:] - part.reshape(groups - until, SUB, n)
    upper, inverse, product = [ref[...].reshape(n, n) for ref in scratch]
    return upper.T, inverse, product


def is_odd_row():
    return lax.rem(lax.axis_index("row"), 2) == 1


def dot_parts(a, b, dims=((1,), (0,))):
    total = None
    for i, j in ((2, 0), (0, 2), (1, 1), (1, 0), (0, 1), (0, 0)):
        term = lax.dot_general(a[i], b[j], (dims, ((), ())), preferred_element_type=jnp.float32)
        total = term if total is None else total + term
    return total


def estimate(flops, nbytes):
    return pl.CostEstimate(flops=flops, bytes_accessed=nbytes, transcendentals=0)


def corner_kernel(matrix_ref, block_ref, sem):
    copy = pltpu.make_async_copy(matrix_ref.at[0, :, 0, :], block_ref, sem)
    copy.start()
    copy.wait()


def corner_block(matrix):
    n = matrix.shape[1]
    return pl.pallas_call(
        corner_kernel,
        out_shape=jax.ShapeDtypeStruct((n, n), jnp.float32),
        in_specs=[HBM],
        out_specs=VMEM,
        scratch_shapes=[pltpu.SemaphoreType.DMA(())],
        compiler_params=pltpu.CompilerParams(vmem_limit_bytes=2 * MIB),
        cost_estimate=estimate(0, 3 * MIB),
        name="corner_block",
    )(matrix)


def panels_kernel(matrix_ref, column_ref, upper_ref, lower_ref, sems):
    local_cols, half, _ = upper_ref.shape
    copies = [pltpu.make_async_copy(matrix_ref.at[pl.ds(1, column_ref.shape[0]), :, 0, :], column_ref, sems.at[0])]
    for j in range(local_cols):
        copies.append(pltpu.make_async_copy(matrix_ref.at[0, pl.ds(0, half), j, :], upper_ref.at[j], sems.at[1 + j]))
        copies.append(pltpu.make_async_copy(
            matrix_ref.at[0, pl.ds(half, half), j, :], lower_ref.at[j], sems.at[1 + local_cols + j]))
    for copy in copies:
        copy.start()
    for copy in copies:
        copy.wait()


def panels(matrix):
    local_rows, n, local_cols, _ = matrix.shape
    strip = jax.ShapeDtypeStruct((local_cols, n // 2, n), jnp.float32)
    return pl.pallas_call(
        panels_kernel,
        out_shape=[jax.ShapeDtypeStruct((local_rows - 1, n, n), jnp.float32), strip, strip],
        in_specs=[HBM],
        out_specs=[VMEM] * 3,
        scratch_shapes=[pltpu.SemaphoreType.DMA((1 + 2 * local_cols,))],
        compiler_params=pltpu.CompilerParams(vmem_limit_bytes=4 * MIB),
        cost_estimate=estimate(0, 4 * MIB),
        name="panels",
    )(matrix)


def pick_kernel(bit, new_ref, old_ref, out_ref):
    out_ref[...] = jnp.where(bit_set(lax.axis_index("col"), bit), new_ref[...], old_ref[...])


def pick(new, old, bit):
    return pl.pallas_call(
        functools.partial(pick_kernel, bit),
        out_shape=jax.ShapeDtypeStruct(old.shape, old.dtype),
        in_specs=[VMEM] * 2,
        out_specs=VMEM,
        compiler_params=pltpu.CompilerParams(vmem_limit_bytes=2 * MIB),
        cost_estimate=estimate(8 * 10**9, 2 * MIB),
        name="pick",
    )(new, old)


def pack_kernel(across_ref, block_ref, both_ref, message_ref):
    n = block_ref.shape[0]
    odd = is_odd_row()
    right = bit_set(lax.axis_index("col"), 0)
    across, block = across_ref[...], block_ref[...]
    left_block = jnp.where(right, across, block)
    right_block = jnp.where(right, block, across)
    both_ref[0] = left_block
    both_ref[1] = right_block
    message_ref[:n] = jnp.where(odd, right_block, left_block)
    message_ref[n:] = jnp.where(odd, left_block.T[n // 2:], right_block[:n // 2])


def pack(across, block):
    n = block.shape[0]
    return pl.pallas_call(
        pack_kernel,
        out_shape=[jax.ShapeDtypeStruct((2, n, n), jnp.float32), jax.ShapeDtypeStruct((n + n // 2, n), jnp.float32)],
        in_specs=[VMEM] * 2,
        out_specs=[VMEM] * 2,
        compiler_params=pltpu.CompilerParams(vmem_limit_bytes=2 * MIB),
        cost_estimate=estimate(1000, 1000),
        name="pack",
    )(across, block)


def first_factor_kernel(a_ref, side_ref, f_ref, w_ref, cross_ref, *scratch):
    f_ref[...], w_ref[...], cross_ref[...] = eliminate(a_ref[...], side_ref[...], scratch)


def elimination_scratch(n):
    return [pltpu.VMEM((n // SUB, SUB, n), jnp.float32)] * 3


def first_factor(a, side):
    n = a.shape[1]
    square = jax.ShapeDtypeStruct((n, n), jnp.float32)
    return pl.pallas_call(
        first_factor_kernel,
        out_shape=[square] * 3,
        in_specs=[VMEM] * 2,
        out_specs=[VMEM] * 3,
        scratch_shapes=elimination_scratch(n),
        compiler_params=pltpu.CompilerParams(vmem_limit_bytes=4 * MIB),
        cost_estimate=estimate(8 * 10**9, 2 * MIB),
        name="first_factor",
    )(a, side)


def second_factor_kernel(a_ref, cross_ref, w0_ref, matrix_ref, f_ref, w_ref, mixed_ref, blocks_ref, *scratch):
    n = w0_ref.shape[0]
    local_cols = matrix_ref.shape[2]
    sems = scratch[-1]
    copies = [pltpu.make_async_copy(matrix_ref.at[:, :, j, :], blocks_ref.at[j], sems.at[j]) for j in range(local_cols)]
    for copy in copies:
        copy.start()
    odd = is_odd_row()
    w0 = w0_ref[...]
    cross = cross_ref[...]
    both = dot_over_rows(cross, jnp.concatenate([cross, w0], axis=1))
    f1, w1, w10 = eliminate(a_ref[...] - both[:, :n], -both[:, n:], scratch[:-1])
    f_ref[...] = f1
    zero = jnp.zeros((n, n), jnp.float32)
    w_ref[:n, :n] = w0
    w_ref[:n, n:] = zero
    w_ref[n:, :n] = w10
    w_ref[n:, n:] = w1
    mixed_ref[:n, :n] = jnp.where(odd, zero, w0)
    mixed_ref[:n, n:] = jnp.where(odd, w0, zero)
    mixed_ref[n:, :n] = jnp.where(odd, w1, w10)
    mixed_ref[n:, n:] = jnp.where(odd, w10, w1)
    for copy in copies:
        copy.wait()


def second_factor(a, cross, w0, matrix):
    local_rows, n, local_cols, _ = matrix.shape
    square = jax.ShapeDtypeStruct((n, n), jnp.float32)
    double = jax.ShapeDtypeStruct((2 * n, 2 * n), jnp.float32)
    blocks = jax.ShapeDtypeStruct((local_cols, local_rows, n, n), jnp.float32)
    return pl.pallas_call(
        second_factor_kernel,
        out_shape=[square, double, double, blocks],
        in_specs=[VMEM] * 3 + [HBM],
        out_specs=[VMEM] * 4,
        scratch_shapes=elimination_scratch(n) + [pltpu.SemaphoreType.DMA((local_cols,))],
        compiler_params=pltpu.CompilerParams(vmem_limit_bytes=12 * MIB),
        cost_estimate=estimate(8 * 10**9, 4 * MIB),
        name="second_factor",
    )(a, cross, w0, matrix)


def settle_kernel(f0_ref, f1_ref, w_ref, mixed_ref, first_ref, rows_ref, rows_other_ref, ha_ref, hb_ref, oa_ref, ob_ref,
                  blocks_ref, out_ref, result, sems):
    grid_row = lax.axis_index("row")
    grid_col = lax.axis_index("col")
    n = f0_ref.shape[0]
    local_cols, local_rows, _, _ = blocks_ref.shape
    flat = (local_rows - 1) * n
    own = rows_ref[...].reshape(flat, n)
    other = rows_other_ref[...].reshape(flat, n)
    swapped = lax.rem(grid_col, 2) == 1
    rows = jnp.concatenate([
        jnp.concatenate([first_ref[0], jnp.where(swapped, other, own)], axis=0),
        jnp.concatenate([first_ref[1], jnp.where(swapped, own, other)], axis=0)], axis=1)
    solved = dot_parts(parts(rows), parts(w_ref[...]), ((1,), (1,)))
    left = parts(solved)
    mixed = parts(mixed_ref[...])
    copies = []
    for j in range(0, local_cols, 2):
        pair = (j, j + 1)
        stacked = jnp.concatenate(
            [jnp.concatenate([ha_ref[b], hb_ref[b], oa_ref[b], ob_ref[b]], axis=0) for b in pair], axis=1)
        update = dot_parts(left, parts(dot_parts(mixed, parts(stacked))))
        for b in pair:
            part = update[:, (b - j) * n:(b - j + 1) * n].reshape(local_rows, n, n)
            result[b] = blocks_ref[b] - part
        if j == 0:
            @pl.when(grid_col == 0)
            def _():
                result[0] = solved[:, :n].reshape(local_rows, n, n)

            @pl.when(grid_col == 1)
            def _():
                result[0] = solved[:, n:].reshape(local_rows, n, n)

        @pl.when(grid_row <= 1)
        def _():
            for b in pair:
                if b > 0:
                    result[b, 0] = jnp.zeros((n, n), jnp.float32)
            if j == 0:
                @pl.when(grid_col > grid_row)
                def _():
                    result[0, 0] = jnp.zeros((n, n), jnp.float32)

                @pl.when((grid_row == 0) & (grid_col == 0))
                def _():
                    result[0, 0] = f0_ref[...]

                @pl.when((grid_row == 1) & (grid_col == 1))
                def _():
                    result[0, 0] = f1_ref[...]
        for b in pair:
            copy = pltpu.make_async_copy(result.at[b], out_ref.at[:, :, b, :], sems.at[b])
            copy.start()
            copies.append(copy)
    for copy in copies:
        copy.wait()


def settle(f0, f1, w, mixed, first_rows, rows, rows_other, ha, hb, oa, ob, blocks):
    local_cols, local_rows, n, _ = blocks.shape
    return pl.pallas_call(
        settle_kernel,
        out_shape=jax.ShapeDtypeStruct((local_rows, n, local_cols, n), jnp.float32),
        in_specs=[VMEM] * 12,
        out_specs=HBM,
        scratch_shapes=[pltpu.VMEM(blocks.shape, jnp.float32), pltpu.SemaphoreType.DMA((local_cols,))],
        compiler_params=pltpu.CompilerParams(vmem_limit_bytes=32 * MIB),
        cost_estimate=estimate(4 * 10**9, 6 * MIB),
        name="settle",
    )(f0, f1, w, mixed, first_rows, rows, rows_other, ha, hb, oa, ob, blocks)


def exchange(value, axis, mask, size):
    return lax.ppermute(value, axis, [(i, i ^ mask) for i in range(size)])


def bit_set(index, bit):
    return ((index >> bit) & 1) == 1


def spread(own, axis, index, size, bits):
    held = own
    for bit in bits:
        held = jnp.where(bit_set(index, bit), exchange(held, axis, 1 << bit, size), held)
    return held


def after(value, *others):
    return lax.optimization_barrier((value,) + others)


def shards(kernel):
    grid_row = lax.axis_index("row")
    grid_col = lax.axis_index("col")
    n_row = lax.axis_size("row")
    n_col = lax.axis_size("col")
    row_bits = list(range(1, n_row.bit_length() - 1))
    col_bits = list(range(1, n_col.bit_length() - 1))
    odd = (grid_row % 2) == 1

    block = corner_block(kernel)
    column, upper, lower = panels(kernel)
    first_bit, last_bit = row_bits[0], row_bits[-1]

    moved = exchange(block, "col", 1 << col_bits[0], n_col)
    upper_moved = exchange(upper, "row", 1 << first_bit, n_row)
    lower_moved = exchange(lower, "row", 1 << last_bit, n_row)

    block = pick(moved, block, col_bits[0])
    block = spread(block, "col", grid_col, n_col, col_bits[1:])
    across = exchange(block, "col", 1, n_col)
    ha = jnp.where(bit_set(grid_row, first_bit), upper_moved, upper)
    hb = jnp.where(bit_set(grid_row, last_bit), lower_moved, lower)
    across, block, ha, hb, column = after(across, block, ha, hb, column)

    first_rows, pair = pack(across, block)
    moved = exchange(pair, "row", 1 << first_bit, n_row)
    column_moved = exchange(column, "col", 1 << col_bits[0], n_col)
    pair = jnp.where(bit_set(grid_row, first_bit), moved, pair)
    moved = exchange(pair, "row", 1 << row_bits[1], n_row)
    rows = jnp.where(bit_set(grid_col, col_bits[0]), column_moved, column)
    moved, pair, rows, ha, hb = after(moved, pair, rows, ha, hb)
    pair = jnp.where(bit_set(grid_row, row_bits[1]), moved, pair)
    pair = spread(pair, "row", grid_row, n_row, row_bits[2:])
    ha_moved = exchange(ha, "row", 1 << row_bits[1], n_row)
    hb_moved = exchange(hb, "row", 1 << row_bits[-2], n_row)
    other = exchange(pair, "row", 1, n_row)

    n = block.shape[0]
    a00 = jnp.where(odd, other[:n], pair[:n])
    a11 = jnp.where(odd, pair[:n], other[:n])
    a01 = jnp.concatenate([jnp.where(odd, other[n:], pair[n:]), jnp.where(odd, pair[n:], other[n:])], axis=0)
    f0, w0, cross = first_factor(a00, a01)

    w0, rows, row_then, col_then = after(w0, rows, grid_row, grid_col)
    ha = jnp.where(bit_set(row_then, row_bits[1]), ha_moved, ha)
    ha = spread(ha, "row", row_then, n_row, row_bits[2:])
    hb = jnp.where(bit_set(row_then, row_bits[-2]), hb_moved, hb)
    hb = spread(hb, "row", row_then, n_row, row_bits[:-2][::-1])
    rows = spread(rows, "col", col_then, n_col, col_bits[1:])
    rows_other = exchange(rows, "col", 1, n_col)
    oa = exchange(ha, "row", 1, n_row)
    ob = exchange(hb, "row", 1, n_row)
    f1, w, mixed, blocks = second_factor(a11, cross, w0, kernel)
    return settle(f0, f1, w, mixed, first_rows, rows, rows_other, ha, hb, oa, ob, blocks)


def solution(mesh):
    in_specs = (P(None, "row", None, "col"),)
    out_specs = P(None, "row", None, "col")
    return jax.shard_map(shards, mesh=mesh, in_specs=in_specs, out_specs=out_specs, check_vma=False)
```

```python
import jax
import jax.numpy as jnp
from jax import lax
from jax.experimental import pallas as pl
from jax.experimental.pallas import tpu as pltpu
from jax.sharding import PartitionSpec as P

SUB = 8
PANEL = 4
MIB = 1024 * 1024
VMEM = pl.BlockSpec(memory_space=pltpu.VMEM)
HBM = pl.BlockSpec(memory_space=pltpu.HBM)


def parts(x):
    high = x.astype(jnp.bfloat16)
    rest = x - high.astype(jnp.float32)
    middle = rest.astype(jnp.bfloat16)
    return high, middle, (rest - middle.astype(jnp.float32)).astype(jnp.bfloat16)


def dot_over_rows(a, b):
    a, b = parts(a), parts(b)
    lhs = jnp.concatenate([a[2], a[0], a[1], a[1], a[0], a[0]], axis=0)
    rhs = jnp.concatenate([b[0], b[2], b[1], b[0], b[1], b[0]], axis=0)
    return lax.dot_general(lhs, rhs, (((0,), (0,)), ((), ())), preferred_element_type=jnp.float32)


def full(row):
    return jnp.broadcast_to(row, (SUB, row.shape[-1]))


def eliminate(s, extra, scratch):
    n = s.shape[0]
    groups = n // SUB
    sub = lax.broadcasted_iota(jnp.int32, (SUB, n), 0)
    lane = lax.broadcasted_iota(jnp.int32, (SUB, n), 1)
    rows = lax.broadcasted_iota(jnp.int32, (n, n), 0)
    cols = lax.broadcasted_iota(jnp.int32, (n, n), 1)
    for ref, value in zip(scratch, (s, jnp.where(rows == cols, 1.0, 0.0), extra)):
        ref[...] = value.reshape(groups, SUB, n)
    sides = range(len(scratch))
    for g in range(groups):
        start = g * SUB
        until = (g // PANEL + 1) * PANEL
        left = until - g
        rest = scratch[0][g:until]
        spread = [jnp.broadcast_to(rest[:, :, start + j:start + j + 1], (left, SUB, n)) for j in range(SUB)]
        unit = {(i, j): full(spread[j][0, i:i + 1, :]) for j in range(SUB) for i in range(j, SUB)}
        row = [[full(ref[g, k:k + 1, :]) for k in range(SUB)] for ref in scratch]
        scaled = [[] for _ in sides]
        tops = [None for _ in sides]
        for k in range(SUB):
            pivot = unit[k, k]
            guess = pl.reciprocal(pivot, approx=True)
            rest_of = 2.0 - pivot * guess
            recip = guess * rest_of
            root = lax.rsqrt(pivot)
            for j in range(k + 1, SUB):
                for i in range(j, SUB):
                    unit[i, j] = unit[i, j] - (unit[i, k] * unit[j, k] * guess) * rest_of
            factors = {j: unit[j, k] * recip for j in range(k + 1, SUB)}
            for j in range(k + 1, SUB):
                spread[j] = spread[j] - spread[k] * factors[j][None]
            for m in sides:
                for j in range(k + 1, SUB):
                    row[m][j] = row[m][j] - row[m][k] * factors[j]
                scaled[m].append(row[m][k] * recip)
                final = row[m][k] * root
                tops[m] = final if k == 0 else jnp.where(sub == k, final, tops[m])
        scratch[0][g] = jnp.where(lane >= start + sub, tops[0], 0.0)
        for m in sides[1:]:
            scratch[m][g] = tops[m]
        if left > 1:
            for m in sides:
                low = scratch[m][g + 1:until]
                for k in range(SUB):
                    low = low - spread[k][1:] * scaled[m][k][None]
                scratch[m][g + 1:until] = low
        elif until < groups:
            done = [ref[until - PANEL:until].reshape(PANEL * SUB, n) for ref in scratch]
            update = dot_over_rows(done[0], jnp.concatenate(done, axis=1))
            for m in sides:
                part = update[until * SUB:, m * n:(m + 1) * n]
                scratch[m][until:] = scratch[m][until:] - part.reshape(groups - until, SUB, n)
    upper, inverse, product = [ref[...].reshape(n, n) for ref in scratch]
    return upper.T, inverse, product


def is_odd_row():
    return lax.rem(lax.axis_index("row"), 2) == 1


def dot_parts(a, b, dims=((1,), (0,))):
    total = None
    for i, j in ((2, 0), (0, 2), (1, 1), (1, 0), (0, 1), (0, 0)):
        term = lax.dot_general(a[i], b[j], (dims, ((), ())), preferred_element_type=jnp.float32)
        total = term if total is None else total + term
    return total


def estimate(flops, nbytes):
    return pl.CostEstimate(flops=flops, bytes_accessed=nbytes, transcendentals=0)


def corner_kernel(matrix_ref, block_ref, sem):
    copy = pltpu.make_async_copy(matrix_ref.at[0, :, 0, :], block_ref, sem)
    copy.start()
    copy.wait()


def corner_block(matrix):
    n = matrix.shape[1]
    return pl.pallas_call(
        corner_kernel,
        out_shape=jax.ShapeDtypeStruct((n, n), jnp.float32),
        in_specs=[HBM],
        out_specs=VMEM,
        scratch_shapes=[pltpu.SemaphoreType.DMA(())],
        compiler_params=pltpu.CompilerParams(vmem_limit_bytes=2 * MIB),
        cost_estimate=estimate(0, 3 * MIB),
        name="corner_block",
    )(matrix)


def panels_kernel(matrix_ref, column_ref, upper_ref, lower_ref, sems):
    local_cols, half, _ = upper_ref.shape
    copies = [pltpu.make_async_copy(matrix_ref.at[pl.ds(1, column_ref.shape[0]), :, 0, :], column_ref, sems.at[0])]
    for j in range(local_cols):
        copies.append(pltpu.make_async_copy(matrix_ref.at[0, pl.ds(0, half), j, :], upper_ref.at[j], sems.at[1 + j]))
        copies.append(pltpu.make_async_copy(
            matrix_ref.at[0, pl.ds(half, half), j, :], lower_ref.at[j], sems.at[1 + local_cols + j]))
    for copy in copies:
        copy.start()
    for copy in copies:
        copy.wait()


def panels(matrix):
    local_rows, n, local_cols, _ = matrix.shape
    strip = jax.ShapeDtypeStruct((local_cols, n // 2, n), jnp.float32)
    return pl.pallas_call(
        panels_kernel,
        out_shape=[jax.ShapeDtypeStruct((local_rows - 1, n, n), jnp.float32), strip, strip],
        in_specs=[HBM],
        out_specs=[VMEM] * 3,
        scratch_shapes=[pltpu.SemaphoreType.DMA((1 + 2 * local_cols,))],
        compiler_params=pltpu.CompilerParams(vmem_limit_bytes=4 * MIB),
        cost_estimate=estimate(0, 4 * MIB),
        name="panels",
    )(matrix)


def pack_kernel(across_ref, block_ref, both_ref, message_ref):
    n = block_ref.shape[0]
    odd = is_odd_row()
    right = bit_set(lax.axis_index("col"), 0)
    across, block = across_ref[...], block_ref[...]
    left_block = jnp.where(right, across, block)
    right_block = jnp.where(right, block, across)
    both_ref[0] = left_block
    both_ref[1] = right_block
    message_ref[:n] = jnp.where(odd, right_block, left_block)
    message_ref[n:] = jnp.where(odd, left_block.T[n // 2:], right_block[:n // 2])


def pack(across, block):
    n = block.shape[0]
    return pl.pallas_call(
        pack_kernel,
        out_shape=[jax.ShapeDtypeStruct((2, n, n), jnp.float32), jax.ShapeDtypeStruct((n + n // 2, n), jnp.float32)],
        in_specs=[VMEM] * 2,
        out_specs=[VMEM] * 2,
        compiler_params=pltpu.CompilerParams(vmem_limit_bytes=2 * MIB),
        cost_estimate=estimate(1000, 1000),
        name="pack",
    )(across, block)


def first_factor_kernel(a_ref, side_ref, f_ref, w_ref, cross_ref, *scratch):
    f_ref[...], w_ref[...], cross_ref[...] = eliminate(a_ref[...], side_ref[...], scratch)


def elimination_scratch(n):
    return [pltpu.VMEM((n // SUB, SUB, n), jnp.float32)] * 3


def first_factor(a, side):
    n = a.shape[1]
    square = jax.ShapeDtypeStruct((n, n), jnp.float32)
    return pl.pallas_call(
        first_factor_kernel,
        out_shape=[square] * 3,
        in_specs=[VMEM] * 2,
        out_specs=[VMEM] * 3,
        scratch_shapes=elimination_scratch(n),
        compiler_params=pltpu.CompilerParams(vmem_limit_bytes=4 * MIB),
        cost_estimate=estimate(8 * 10**9, 2 * MIB),
        name="first_factor",
    )(a, side)


def second_factor_kernel(a_ref, cross_ref, w0_ref, matrix_ref, f_ref, w_ref, mixed_ref, blocks_ref, *scratch):
    n = w0_ref.shape[0]
    local_cols = matrix_ref.shape[2]
    sems = scratch[-1]
    copies = [pltpu.make_async_copy(matrix_ref.at[:, :, j, :], blocks_ref.at[j], sems.at[j]) for j in range(local_cols)]
    for copy in copies:
        copy.start()
    odd = is_odd_row()
    w0 = w0_ref[...]
    cross = cross_ref[...]
    both = dot_over_rows(cross, jnp.concatenate([cross, w0], axis=1))
    f1, w1, w10 = eliminate(a_ref[...] - both[:, :n], -both[:, n:], scratch[:-1])
    f_ref[...] = f1
    zero = jnp.zeros((n, n), jnp.float32)
    w_ref[:n, :n] = w0
    w_ref[:n, n:] = zero
    w_ref[n:, :n] = w10
    w_ref[n:, n:] = w1
    mixed_ref[:n, :n] = jnp.where(odd, zero, w0)
    mixed_ref[:n, n:] = jnp.where(odd, w0, zero)
    mixed_ref[n:, :n] = jnp.where(odd, w1, w10)
    mixed_ref[n:, n:] = jnp.where(odd, w10, w1)
    for copy in copies:
        copy.wait()


def second_factor(a, cross, w0, matrix):
    local_rows, n, local_cols, _ = matrix.shape
    square = jax.ShapeDtypeStruct((n, n), jnp.float32)
    double = jax.ShapeDtypeStruct((2 * n, 2 * n), jnp.float32)
    blocks = jax.ShapeDtypeStruct((local_cols, local_rows, n, n), jnp.float32)
    return pl.pallas_call(
        second_factor_kernel,
        out_shape=[square, double, double, blocks],
        in_specs=[VMEM] * 3 + [HBM],
        out_specs=[VMEM] * 4,
        scratch_shapes=elimination_scratch(n) + [pltpu.SemaphoreType.DMA((local_cols,))],
        compiler_params=pltpu.CompilerParams(vmem_limit_bytes=12 * MIB),
        cost_estimate=estimate(8 * 10**9, 4 * MIB),
        name="second_factor",
    )(a, cross, w0, matrix)


def settle_kernel(f0_ref, f1_ref, w_ref, mixed_ref, first_ref, rows_ref, rows_other_ref, ha_ref, hb_ref, oa_ref, ob_ref,
                  blocks_ref, out_ref, result, sems):
    grid_row = lax.axis_index("row")
    grid_col = lax.axis_index("col")
    n = f0_ref.shape[0]
    local_cols, local_rows, _, _ = blocks_ref.shape
    flat = (local_rows - 1) * n
    own = rows_ref[...].reshape(flat, n)
    other = rows_other_ref[...].reshape(flat, n)
    swapped = lax.rem(grid_col, 2) == 1
    rows = jnp.concatenate([
        jnp.concatenate([first_ref[0], jnp.where(swapped, other, own)], axis=0),
        jnp.concatenate([first_ref[1], jnp.where(swapped, own, other)], axis=0)], axis=1)
    solved = dot_parts(parts(rows), parts(w_ref[...]), ((1,), (1,)))
    left = parts(solved)
    mixed = parts(mixed_ref[...])
    copies = []
    for j in range(0, local_cols, 2):
        pair = (j, j + 1)
        stacked = jnp.concatenate(
            [jnp.concatenate([ha_ref[b], hb_ref[b], oa_ref[b], ob_ref[b]], axis=0) for b in pair], axis=1)
        update = dot_parts(left, parts(dot_parts(mixed, parts(stacked))))
        for b in pair:
            part = update[:, (b - j) * n:(b - j + 1) * n].reshape(local_rows, n, n)
            result[b] = blocks_ref[b] - part
        if j == 0:
            @pl.when(grid_col == 0)
            def _():
                result[0] = solved[:, :n].reshape(local_rows, n, n)

            @pl.when(grid_col == 1)
            def _():
                result[0] = solved[:, n:].reshape(local_rows, n, n)

        @pl.when(grid_row <= 1)
        def _():
            for b in pair:
                if b > 0:
                    result[b, 0] = jnp.zeros((n, n), jnp.float32)
            if j == 0:
                @pl.when(grid_col > grid_row)
                def _():
                    result[0, 0] = jnp.zeros((n, n), jnp.float32)

                @pl.when((grid_row == 0) & (grid_col == 0))
                def _():
                    result[0, 0] = f0_ref[...]

                @pl.when((grid_row == 1) & (grid_col == 1))
                def _():
                    result[0, 0] = f1_ref[...]
        for b in pair:
            copy = pltpu.make_async_copy(result.at[b], out_ref.at[:, :, b, :], sems.at[b])
            copy.start()
            copies.append(copy)
    for copy in copies:
        copy.wait()


def settle(f0, f1, w, mixed, first_rows, rows, rows_other, ha, hb, oa, ob, blocks):
    local_cols, local_rows, n, _ = blocks.shape
    return pl.pallas_call(
        settle_kernel,
        out_shape=jax.ShapeDtypeStruct((local_rows, n, local_cols, n), jnp.float32),
        in_specs=[VMEM] * 12,
        out_specs=HBM,
        scratch_shapes=[pltpu.VMEM(blocks.shape, jnp.float32), pltpu.SemaphoreType.DMA((local_cols,))],
        compiler_params=pltpu.CompilerParams(vmem_limit_bytes=32 * MIB),
        cost_estimate=estimate(4 * 10**9, 6 * MIB),
        name="settle",
    )(f0, f1, w, mixed, first_rows, rows, rows_other, ha, hb, oa, ob, blocks)


def exchange(value, axis, mask, size):
    return lax.ppermute(value, axis, [(i, i ^ mask) for i in range(size)])


def bit_set(index, bit):
    return ((index >> bit) & 1) == 1


def spread(own, axis, index, size, bits):
    held = own
    for bit in bits:
        held = jnp.where(bit_set(index, bit), exchange(held, axis, 1 << bit, size), held)
    return held


def region(run, *values):
    shapes = jax.eval_shape(run, *values)

    def skip(*_):
        return jax.tree.map(lambda leaf: jnp.zeros(leaf.shape, leaf.dtype), shapes)

    everywhere = lax.axis_index("row") < lax.axis_size("row")
    return lax.cond(everywhere, run, skip, *values)


def after(value, *others):
    return lax.optimization_barrier((value,) + others)


def shards(kernel):
    grid_row = lax.axis_index("row")
    grid_col = lax.axis_index("col")
    n_row = lax.axis_size("row")
    n_col = lax.axis_size("col")
    row_bits = list(range(1, n_row.bit_length() - 1))
    col_bits = list(range(1, n_col.bit_length() - 1))
    odd = (grid_row % 2) == 1

    block = corner_block(kernel)
    column, upper, lower = panels(kernel)
    first_bit, last_bit = row_bits[0], row_bits[-1]

    moved = exchange(block, "col", 1 << col_bits[0], n_col)
    upper_moved = exchange(upper, "row", 1 << first_bit, n_row)
    lower_moved = exchange(lower, "row", 1 << last_bit, n_row)

    def along_col(new, old):
        block = jnp.where(bit_set(grid_col, col_bits[0]), new, old)
        return spread(block, "col", grid_col, n_col, col_bits[1:])

    block = region(along_col, moved, block)
    across = exchange(block, "col", 1, n_col)
    ha = jnp.where(bit_set(grid_row, first_bit), upper_moved, upper)
    hb = jnp.where(bit_set(grid_row, last_bit), lower_moved, lower)
    across, block, ha, hb, column = after(across, block, ha, hb, column)

    first_rows, pair = pack(across, block)
    moved = exchange(pair, "row", 1 << first_bit, n_row)
    column_moved = exchange(column, "col", 1 << col_bits[0], n_col)
    pair = jnp.where(bit_set(grid_row, first_bit), moved, pair)
    moved = exchange(pair, "row", 1 << row_bits[1], n_row)
    rows = jnp.where(bit_set(grid_col, col_bits[0]), column_moved, column)
    moved, pair, rows, ha, hb = after(moved, pair, rows, ha, hb)
    pair = jnp.where(bit_set(grid_row, row_bits[1]), moved, pair)
    pair = spread(pair, "row", grid_row, n_row, row_bits[2:])
    ha_moved = exchange(ha, "row", 1 << row_bits[1], n_row)
    hb_moved = exchange(hb, "row", 1 << row_bits[-2], n_row)
    other = exchange(pair, "row", 1, n_row)

    n = block.shape[0]
    a00 = jnp.where(odd, other[:n], pair[:n])
    a11 = jnp.where(odd, pair[:n], other[:n])
    a01 = jnp.concatenate([jnp.where(odd, other[n:], pair[n:]), jnp.where(odd, pair[n:], other[n:])], axis=0)
    f0, w0, cross = first_factor(a00, a01)

    w0, rows, row_then, col_then = after(w0, rows, grid_row, grid_col)
    ha = jnp.where(bit_set(row_then, row_bits[1]), ha_moved, ha)
    ha = spread(ha, "row", row_then, n_row, row_bits[2:])
    hb = jnp.where(bit_set(row_then, row_bits[-2]), hb_moved, hb)
    hb = spread(hb, "row", row_then, n_row, row_bits[:-2][::-1])
    rows = spread(rows, "col", col_then, n_col, col_bits[1:])
    rows_other = exchange(rows, "col", 1, n_col)
    oa = exchange(ha, "row", 1, n_row)
    ob = exchange(hb, "row", 1, n_row)
    f1, w, mixed, blocks = second_factor(a11, cross, w0, kernel)
    return settle(f0, f1, w, mixed, first_rows, rows, rows_other, ha, hb, oa, ob, blocks)


def solution(mesh):
    in_specs = (P(None, "row", None, "col"),)
    out_specs = P(None, "row", None, "col")
    return jax.shard_map(shards, mesh=mesh, in_specs=in_specs, out_specs=out_specs, check_vma=False)
```

```python
import jax
import jax.numpy as jnp
from jax import lax
from jax.experimental import pallas as pl
from jax.experimental.pallas import tpu as pltpu
from jax.sharding import PartitionSpec as P

SUB = 8
PANEL = 4
MIB = 1024 * 1024
VMEM = pl.BlockSpec(memory_space=pltpu.VMEM)
HBM = pl.BlockSpec(memory_space=pltpu.HBM)


def parts(x):
    high = x.astype(jnp.bfloat16)
    rest = x - high.astype(jnp.float32)
    middle = rest.astype(jnp.bfloat16)
    return high, middle, (rest - middle.astype(jnp.float32)).astype(jnp.bfloat16)


def dot_over_rows(a, b):
    a, b = parts(a), parts(b)
    lhs = jnp.concatenate([a[2], a[0], a[1], a[1], a[0], a[0]], axis=0)
    rhs = jnp.concatenate([b[0], b[2], b[1], b[0], b[1], b[0]], axis=0)
    return lax.dot_general(lhs, rhs, (((0,), (0,)), ((), ())), preferred_element_type=jnp.float32)


def full(row):
    return jnp.broadcast_to(row, (SUB, row.shape[-1]))


def eliminate(s, extra, scratch):
    n = s.shape[0]
    groups = n // SUB
    sub = lax.broadcasted_iota(jnp.int32, (SUB, n), 0)
    lane = lax.broadcasted_iota(jnp.int32, (SUB, n), 1)
    rows = lax.broadcasted_iota(jnp.int32, (n, n), 0)
    cols = lax.broadcasted_iota(jnp.int32, (n, n), 1)
    for ref, value in zip(scratch, (s, jnp.where(rows == cols, 1.0, 0.0), extra)):
        ref[...] = value.reshape(groups, SUB, n)
    sides = range(len(scratch))
    for g in range(groups):
        start = g * SUB
        until = (g // PANEL + 1) * PANEL
        left = until - g
        rest = scratch[0][g:until]
        spread = [jnp.broadcast_to(rest[:, :, start + j:start + j + 1], (left, SUB, n)) for j in range(SUB)]
        unit = {(i, j): full(spread[j][0, i:i + 1, :]) for j in range(SUB) for i in range(j, SUB)}
        row = [[full(ref[g, k:k + 1, :]) for k in range(SUB)] for ref in scratch]
        scaled = [[] for _ in sides]
        tops = [None for _ in sides]
        for k in range(SUB):
            pivot = unit[k, k]
            guess = pl.reciprocal(pivot, approx=True)
            rest_of = 2.0 - pivot * guess
            recip = guess * rest_of
            root = lax.rsqrt(pivot)
            for j in range(k + 1, SUB):
                for i in range(j, SUB):
                    unit[i, j] = unit[i, j] - (unit[i, k] * unit[j, k] * guess) * rest_of
            factors = {j: unit[j, k] * recip for j in range(k + 1, SUB)}
            for j in range(k + 1, SUB):
                spread[j] = spread[j] - spread[k] * factors[j][None]
            for m in sides:
                for j in range(k + 1, SUB):
                    row[m][j] = row[m][j] - row[m][k] * factors[j]
                scaled[m].append(row[m][k] * recip)
                final = row[m][k] * root
                tops[m] = final if k == 0 else jnp.where(sub == k, final, tops[m])
        scratch[0][g] = jnp.where(lane >= start + sub, tops[0], 0.0)
        for m in sides[1:]:
            scratch[m][g] = tops[m]
        if left > 1:
            for m in sides:
                low = scratch[m][g + 1:until]
                for k in range(SUB):
                    low = low - spread[k][1:] * scaled[m][k][None]
                scratch[m][g + 1:until] = low
        elif until < groups:
            done = [ref[until - PANEL:until].reshape(PANEL * SUB, n) for ref in scratch]
            update = dot_over_rows(done[0], jnp.concatenate(done, axis=1))
            for m in sides:
                part = update[until * SUB:, m * n:(m + 1) * n]
                scratch[m][until:] = scratch[m][until:] - part.reshape(groups - until, SUB, n)
    upper, inverse, product = [ref[...].reshape(n, n) for ref in scratch]
    return upper.T, inverse, product


def is_odd_row():
    return lax.rem(lax.axis_index("row"), 2) == 1


def stacked(a):
    return jnp.concatenate(parts(a)[::-1], axis=0)


def dot_parts(a, b, dims=((1,), (0,))):
    m = a.shape[0] // 3
    high, middle, low = [
        lax.dot_general(a[i * m:], b[i], (dims, ((), ())), preferred_element_type=jnp.float32) for i in range(3)]
    small = high[:m] + middle[:m] + low
    return small + (high[m:2 * m] + middle[m:]) + high[2 * m:]


def estimate(flops, nbytes):
    return pl.CostEstimate(flops=flops, bytes_accessed=nbytes, transcendentals=0)


def corner_kernel(matrix_ref, block_ref, sem):
    copy = pltpu.make_async_copy(matrix_ref.at[0, :, 0, :], block_ref, sem)
    copy.start()
    copy.wait()


def corner_block(matrix):
    n = matrix.shape[1]
    return pl.pallas_call(
        corner_kernel,
        out_shape=jax.ShapeDtypeStruct((n, n), jnp.float32),
        in_specs=[HBM],
        out_specs=VMEM,
        scratch_shapes=[pltpu.SemaphoreType.DMA(())],
        compiler_params=pltpu.CompilerParams(vmem_limit_bytes=2 * MIB),
        cost_estimate=estimate(0, 3 * MIB),
        name="corner_block",
    )(matrix)


def panels_kernel(matrix_ref, column_ref, upper_ref, lower_ref, sems):
    local_cols, half, _ = upper_ref.shape
    copies = [pltpu.make_async_copy(matrix_ref.at[pl.ds(1, column_ref.shape[0]), :, 0, :], column_ref, sems.at[0])]
    for j in range(local_cols):
        copies.append(pltpu.make_async_copy(matrix_ref.at[0, pl.ds(0, half), j, :], upper_ref.at[j], sems.at[1 + j]))
        copies.append(pltpu.make_async_copy(
            matrix_ref.at[0, pl.ds(half, half), j, :], lower_ref.at[j], sems.at[1 + local_cols + j]))
    for copy in copies:
        copy.start()
    for copy in copies:
        copy.wait()


def panels(matrix):
    local_rows, n, local_cols, _ = matrix.shape
    strip = jax.ShapeDtypeStruct((local_cols, n // 2, n), jnp.float32)
    return pl.pallas_call(
        panels_kernel,
        out_shape=[jax.ShapeDtypeStruct((local_rows - 1, n, n), jnp.float32), strip, strip],
        in_specs=[HBM],
        out_specs=[VMEM] * 3,
        scratch_shapes=[pltpu.SemaphoreType.DMA((1 + 2 * local_cols,))],
        compiler_params=pltpu.CompilerParams(vmem_limit_bytes=4 * MIB),
        cost_estimate=estimate(0, 4 * MIB),
        name="panels",
    )(matrix)


def pack_kernel(across_ref, block_ref, both_ref, message_ref):
    n = block_ref.shape[0]
    odd = is_odd_row()
    right = bit_set(lax.axis_index("col"), 0)
    across, block = across_ref[...], block_ref[...]
    left_block = jnp.where(right, across, block)
    right_block = jnp.where(right, block, across)
    both_ref[0] = left_block
    both_ref[1] = right_block
    message_ref[:n] = jnp.where(odd, right_block, left_block)
    message_ref[n:] = jnp.where(odd, left_block.T[n // 2:], right_block[:n // 2])


def pack(across, block):
    n = block.shape[0]
    return pl.pallas_call(
        pack_kernel,
        out_shape=[jax.ShapeDtypeStruct((2, n, n), jnp.float32), jax.ShapeDtypeStruct((n + n // 2, n), jnp.float32)],
        in_specs=[VMEM] * 2,
        out_specs=[VMEM] * 2,
        compiler_params=pltpu.CompilerParams(vmem_limit_bytes=2 * MIB),
        cost_estimate=estimate(1000, 1000),
        name="pack",
    )(across, block)


def first_factor_kernel(a_ref, side_ref, f_ref, w_ref, cross_ref, *scratch):
    f_ref[...], w_ref[...], cross_ref[...] = eliminate(a_ref[...], side_ref[...], scratch)


def elimination_scratch(n):
    return [pltpu.VMEM((n // SUB, SUB, n), jnp.float32)] * 3


def first_factor(a, side):
    n = a.shape[1]
    square = jax.ShapeDtypeStruct((n, n), jnp.float32)
    return pl.pallas_call(
        first_factor_kernel,
        out_shape=[square] * 3,
        in_specs=[VMEM] * 2,
        out_specs=[VMEM] * 3,
        scratch_shapes=elimination_scratch(n),
        compiler_params=pltpu.CompilerParams(vmem_limit_bytes=4 * MIB),
        cost_estimate=estimate(8 * 10**9, 2 * MIB),
        name="first_factor",
    )(a, side)


def second_factor_kernel(a_ref, cross_ref, w0_ref, matrix_ref, f_ref, w_ref, mixed_ref, blocks_ref, *scratch):
    n = w0_ref.shape[0]
    local_cols = matrix_ref.shape[2]
    sems = scratch[-1]
    copies = [pltpu.make_async_copy(matrix_ref.at[:, :, j, :], blocks_ref.at[j], sems.at[j]) for j in range(local_cols)]
    for copy in copies:
        copy.start()
    odd = is_odd_row()
    w0 = w0_ref[...]
    cross = cross_ref[...]
    both = dot_over_rows(cross, jnp.concatenate([cross, w0], axis=1))
    f1, w1, w10 = eliminate(a_ref[...] - both[:, :n], -both[:, n:], scratch[:-1])
    f_ref[...] = f1
    zero = jnp.zeros((n, n), jnp.float32)
    w_ref[:n, :n] = w0
    w_ref[:n, n:] = zero
    w_ref[n:, :n] = w10
    w_ref[n:, n:] = w1
    mixed_ref[:n, :n] = jnp.where(odd, zero, w0)
    mixed_ref[:n, n:] = jnp.where(odd, w0, zero)
    mixed_ref[n:, :n] = jnp.where(odd, w1, w10)
    mixed_ref[n:, n:] = jnp.where(odd, w10, w1)
    for copy in copies:
        copy.wait()


def second_factor(a, cross, w0, matrix):
    local_rows, n, local_cols, _ = matrix.shape
    square = jax.ShapeDtypeStruct((n, n), jnp.float32)
    double = jax.ShapeDtypeStruct((2 * n, 2 * n), jnp.float32)
    blocks = jax.ShapeDtypeStruct((local_cols, local_rows, n, n), jnp.float32)
    return pl.pallas_call(
        second_factor_kernel,
        out_shape=[square, double, double, blocks],
        in_specs=[VMEM] * 3 + [HBM],
        out_specs=[VMEM] * 4,
        scratch_shapes=elimination_scratch(n) + [pltpu.SemaphoreType.DMA((local_cols,))],
        compiler_params=pltpu.CompilerParams(vmem_limit_bytes=12 * MIB),
        cost_estimate=estimate(8 * 10**9, 4 * MIB),
        name="second_factor",
    )(a, cross, w0, matrix)


def settle_kernel(f0_ref, f1_ref, w_ref, mixed_ref, first_ref, rows_ref, rows_other_ref, ha_ref, hb_ref, oa_ref, ob_ref,
                  blocks_ref, out_ref, result, sems):
    grid_row = lax.axis_index("row")
    grid_col = lax.axis_index("col")
    n = f0_ref.shape[0]
    local_cols, local_rows, _, _ = blocks_ref.shape
    flat = (local_rows - 1) * n
    own = rows_ref[...].reshape(flat, n)
    other = rows_other_ref[...].reshape(flat, n)
    swapped = lax.rem(grid_col, 2) == 1
    rows = jnp.concatenate([
        jnp.concatenate([first_ref[0], jnp.where(swapped, other, own)], axis=0),
        jnp.concatenate([first_ref[1], jnp.where(swapped, own, other)], axis=0)], axis=1)
    solved = dot_parts(stacked(rows), parts(w_ref[...]), ((1,), (1,)))
    left = stacked(solved)
    mixed = stacked(mixed_ref[...])
    copies = []
    for j in range(0, local_cols, 2):
        pair = (j, j + 1)
        tops = jnp.concatenate(
            [jnp.concatenate([ha_ref[b], hb_ref[b], oa_ref[b], ob_ref[b]], axis=0) for b in pair], axis=1)
        update = dot_parts(left, parts(dot_parts(mixed, parts(tops))))
        for b in pair:
            part = update[:, (b - j) * n:(b - j + 1) * n].reshape(local_rows, n, n)
            result[b] = blocks_ref[b] - part
        if j == 0:
            @pl.when(grid_col == 0)
            def _():
                result[0] = solved[:, :n].reshape(local_rows, n, n)

            @pl.when(grid_col == 1)
            def _():
                result[0] = solved[:, n:].reshape(local_rows, n, n)

        @pl.when(grid_row <= 1)
        def _():
            for b in pair:
                if b > 0:
                    result[b, 0] = jnp.zeros((n, n), jnp.float32)
            if j == 0:
                @pl.when(grid_col > grid_row)
                def _():
                    result[0, 0] = jnp.zeros((n, n), jnp.float32)

                @pl.when((grid_row == 0) & (grid_col == 0))
                def _():
                    result[0, 0] = f0_ref[...]

                @pl.when((grid_row == 1) & (grid_col == 1))
                def _():
                    result[0, 0] = f1_ref[...]
        for b in pair:
            copy = pltpu.make_async_copy(result.at[b], out_ref.at[:, :, b, :], sems.at[b])
            copy.start()
            copies.append(copy)
    for copy in copies:
        copy.wait()


def settle(f0, f1, w, mixed, first_rows, rows, rows_other, ha, hb, oa, ob, blocks):
    local_cols, local_rows, n, _ = blocks.shape
    return pl.pallas_call(
        settle_kernel,
        out_shape=jax.ShapeDtypeStruct((local_rows, n, local_cols, n), jnp.float32),
        in_specs=[VMEM] * 12,
        out_specs=HBM,
        scratch_shapes=[pltpu.VMEM(blocks.shape, jnp.float32), pltpu.SemaphoreType.DMA((local_cols,))],
        compiler_params=pltpu.CompilerParams(vmem_limit_bytes=32 * MIB),
        cost_estimate=estimate(4 * 10**9, 6 * MIB),
        name="settle",
    )(f0, f1, w, mixed, first_rows, rows, rows_other, ha, hb, oa, ob, blocks)


def exchange(value, axis, mask, size):
    return lax.ppermute(value, axis, [(i, i ^ mask) for i in range(size)])


def bit_set(index, bit):
    return ((index >> bit) & 1) == 1


def spread(own, axis, index, size, bits):
    held = own
    for bit in bits:
        held = jnp.where(bit_set(index, bit), exchange(held, axis, 1 << bit, size), held)
    return held


def region(run, *values):
    shapes = jax.eval_shape(run, *values)

    def skip(*_):
        return jax.tree.map(lambda leaf: jnp.zeros(leaf.shape, leaf.dtype), shapes)

    everywhere = lax.axis_index("row") < lax.axis_size("row")
    return lax.cond(everywhere, run, skip, *values)


def after(value, *others):
    return lax.optimization_barrier((value,) + others)


def shards(kernel):
    grid_row = lax.axis_index("row")
    grid_col = lax.axis_index("col")
    n_row = lax.axis_size("row")
    n_col = lax.axis_size("col")
    row_bits = list(range(1, n_row.bit_length() - 1))
    col_bits = list(range(1, n_col.bit_length() - 1))
    odd = (grid_row % 2) == 1

    block = corner_block(kernel)
    column, upper, lower = panels(kernel)
    first_bit, last_bit = row_bits[0], row_bits[-1]

    moved = exchange(block, "col", 1 << col_bits[0], n_col)
    upper_moved = exchange(upper, "row", 1 << first_bit, n_row)
    lower_moved = exchange(lower, "row", 1 << last_bit, n_row)

    def along_col(new, old):
        block = jnp.where(bit_set(grid_col, col_bits[0]), new, old)
        return spread(block, "col", grid_col, n_col, col_bits[1:])

    block = region(along_col, moved, block)
    across = exchange(block, "col", 1, n_col)
    ha = jnp.where(bit_set(grid_row, first_bit), upper_moved, upper)
    hb = jnp.where(bit_set(grid_row, last_bit), lower_moved, lower)
    across, block, ha, hb, column = after(across, block, ha, hb, column)

    first_rows, pair = pack(across, block)
    moved = exchange(pair, "row", 1 << first_bit, n_row)
    column_moved = exchange(column, "col", 1 << col_bits[0], n_col)
    pair = jnp.where(bit_set(grid_row, first_bit), moved, pair)
    moved = exchange(pair, "row", 1 << row_bits[1], n_row)
    rows = jnp.where(bit_set(grid_col, col_bits[0]), column_moved, column)
    moved, pair, rows, ha, hb = after(moved, pair, rows, ha, hb)
    pair = jnp.where(bit_set(grid_row, row_bits[1]), moved, pair)
    pair = spread(pair, "row", grid_row, n_row, row_bits[2:])
    ha_moved = exchange(ha, "row", 1 << row_bits[1], n_row)
    hb_moved = exchange(hb, "row", 1 << row_bits[-2], n_row)
    other = exchange(pair, "row", 1, n_row)

    n = block.shape[0]
    a00 = jnp.where(odd, other[:n], pair[:n])
    a11 = jnp.where(odd, pair[:n], other[:n])
    a01 = jnp.concatenate([jnp.where(odd, other[n:], pair[n:]), jnp.where(odd, pair[n:], other[n:])], axis=0)
    f0, w0, cross = first_factor(a00, a01)

    rows = spread(rows, "col", grid_col, n_col, col_bits[1:])
    rows_other = exchange(rows, "col", 1, n_col)
    w0, row_then = after(w0, grid_row)
    ha = jnp.where(bit_set(row_then, row_bits[1]), ha_moved, ha)
    ha = spread(ha, "row", row_then, n_row, row_bits[2:])
    hb = jnp.where(bit_set(row_then, row_bits[-2]), hb_moved, hb)
    hb = spread(hb, "row", row_then, n_row, row_bits[:-2][::-1])
    oa = exchange(ha, "row", 1, n_row)
    ob = exchange(hb, "row", 1, n_row)
    a11, rows_other = after(a11, rows_other)
    f1, w, mixed, blocks = second_factor(a11, cross, w0, kernel)
    return settle(f0, f1, w, mixed, first_rows, rows, rows_other, ha, hb, oa, ob, blocks)


def solution(mesh):
    in_specs = (P(None, "row", None, "col"),)
    out_specs = P(None, "row", None, "col")
    return jax.shard_map(shards, mesh=mesh, in_specs=in_specs, out_specs=out_specs, check_vma=False)
```

```python
import jax
import jax.numpy as jnp
from jax import lax
from jax.experimental import pallas as pl
from jax.experimental.pallas import tpu as pltpu
from jax.sharding import PartitionSpec as P

SUB = 8
PANEL = 4
MIB = 1024 * 1024
VMEM = pl.BlockSpec(memory_space=pltpu.VMEM)
HBM = pl.BlockSpec(memory_space=pltpu.HBM)


def parts(x):
    high = x.astype(jnp.bfloat16)
    rest = x - high.astype(jnp.float32)
    middle = rest.astype(jnp.bfloat16)
    return high, middle, (rest - middle.astype(jnp.float32)).astype(jnp.bfloat16)


def dot_over_rows(a, b):
    a, b = parts(a), parts(b)
    lhs = jnp.concatenate([a[2], a[0], a[1], a[1], a[0], a[0]], axis=0)
    rhs = jnp.concatenate([b[0], b[2], b[1], b[0], b[1], b[0]], axis=0)
    return lax.dot_general(lhs, rhs, (((0,), (0,)), ((), ())), preferred_element_type=jnp.float32)


def full(row):
    return jnp.broadcast_to(row, (SUB, row.shape[-1]))


def eliminate(s, extra, scratch):
    n = s.shape[0]
    groups = n // SUB
    sub = lax.broadcasted_iota(jnp.int32, (SUB, n), 0)
    lane = lax.broadcasted_iota(jnp.int32, (SUB, n), 1)
    rows = lax.broadcasted_iota(jnp.int32, (n, n), 0)
    cols = lax.broadcasted_iota(jnp.int32, (n, n), 1)
    for ref, value in zip(scratch, (s, jnp.where(rows == cols, 1.0, 0.0), extra)):
        ref[...] = value.reshape(groups, SUB, n)
    sides = range(len(scratch))
    for g in range(groups):
        start = g * SUB
        until = (g // PANEL + 1) * PANEL
        left = until - g
        rest = scratch[0][g:until]
        spread = [jnp.broadcast_to(rest[:, :, start + j:start + j + 1], (left, SUB, n)) for j in range(SUB)]
        unit = {(i, j): full(spread[j][0, i:i + 1, :]) for j in range(SUB) for i in range(j, SUB)}
        row = [[full(ref[g, k:k + 1, :]) for k in range(SUB)] for ref in scratch]
        scaled = [[] for _ in sides]
        tops = [None for _ in sides]
        for k in range(SUB):
            pivot = unit[k, k]
            guess = pl.reciprocal(pivot, approx=True)
            rest_of = 2.0 - pivot * guess
            recip = guess * rest_of
            root = lax.rsqrt(pivot)
            for j in range(k + 1, SUB):
                for i in range(j, SUB):
                    unit[i, j] = unit[i, j] - (unit[i, k] * unit[j, k] * guess) * rest_of
            factors = {j: unit[j, k] * recip for j in range(k + 1, SUB)}
            for j in range(k + 1, SUB):
                spread[j] = spread[j] - spread[k] * factors[j][None]
            for m in sides:
                for j in range(k + 1, SUB):
                    row[m][j] = row[m][j] - row[m][k] * factors[j]
                scaled[m].append(row[m][k] * recip)
                final = row[m][k] * root
                tops[m] = final if k == 0 else jnp.where(sub == k, final, tops[m])
        scratch[0][g] = jnp.where(lane >= start + sub, tops[0], 0.0)
        for m in sides[1:]:
            scratch[m][g] = tops[m]
        if left > 1:
            for m in sides:
                low = scratch[m][g + 1:until]
                for k in range(SUB):
                    low = low - spread[k][1:] * scaled[m][k][None]
                scratch[m][g + 1:until] = low
        elif until < groups:
            done = [ref[until - PANEL:until].reshape(PANEL * SUB, n) for ref in scratch]
            update = dot_over_rows(done[0], jnp.concatenate(done, axis=1))
            for m in sides:
                part = update[until * SUB:, m * n:(m + 1) * n]
                scratch[m][until:] = scratch[m][until:] - part.reshape(groups - until, SUB, n)
    upper, inverse, product = [ref[...].reshape(n, n) for ref in scratch]
    return upper.T, inverse, product


def is_odd_row():
    return lax.rem(lax.axis_index("row"), 2) == 1


def stacked(a):
    return jnp.concatenate(parts(a)[::-1], axis=0)


def dot_parts(a, b, dims=((1,), (0,))):
    m = a.shape[0] // 3
    high, middle, low = [
        lax.dot_general(a[i * m:], b[i], (dims, ((), ())), preferred_element_type=jnp.float32) for i in range(3)]
    small = high[:m] + middle[:m] + low
    return small + (high[m:2 * m] + middle[m:]) + high[2 * m:]


def estimate(flops, nbytes):
    return pl.CostEstimate(flops=flops, bytes_accessed=nbytes, transcendentals=0)


def corner_kernel(matrix_ref, block_ref, sem):
    copy = pltpu.make_async_copy(matrix_ref.at[0, :, 0, :], block_ref, sem)
    copy.start()
    copy.wait()


def corner_block(matrix):
    n = matrix.shape[1]
    return pl.pallas_call(
        corner_kernel,
        out_shape=jax.ShapeDtypeStruct((n, n), jnp.float32),
        in_specs=[HBM],
        out_specs=VMEM,
        scratch_shapes=[pltpu.SemaphoreType.DMA(())],
        compiler_params=pltpu.CompilerParams(vmem_limit_bytes=2 * MIB),
        cost_estimate=estimate(0, 3 * MIB),
        name="corner_block",
    )(matrix)


def panels_kernel(matrix_ref, column_ref, upper_ref, lower_ref, sems):
    local_cols, half, _ = upper_ref.shape
    copies = [pltpu.make_async_copy(matrix_ref.at[pl.ds(1, column_ref.shape[0]), :, 0, :], column_ref, sems.at[0])]
    for j in range(local_cols):
        copies.append(pltpu.make_async_copy(matrix_ref.at[0, pl.ds(0, half), j, :], upper_ref.at[j], sems.at[1 + j]))
        copies.append(pltpu.make_async_copy(
            matrix_ref.at[0, pl.ds(half, half), j, :], lower_ref.at[j], sems.at[1 + local_cols + j]))
    for copy in copies:
        copy.start()
    for copy in copies:
        copy.wait()


def panels(matrix):
    local_rows, n, local_cols, _ = matrix.shape
    strip = jax.ShapeDtypeStruct((local_cols, n // 2, n), jnp.float32)
    return pl.pallas_call(
        panels_kernel,
        out_shape=[jax.ShapeDtypeStruct((local_rows - 1, n, n), jnp.float32), strip, strip],
        in_specs=[HBM],
        out_specs=[VMEM] * 3,
        scratch_shapes=[pltpu.SemaphoreType.DMA((1 + 2 * local_cols,))],
        compiler_params=pltpu.CompilerParams(vmem_limit_bytes=4 * MIB),
        cost_estimate=estimate(0, 4 * MIB),
        name="panels",
    )(matrix)


def pack_kernel(across_ref, block_ref, both_ref, message_ref):
    n = block_ref.shape[0]
    odd = is_odd_row()
    right = bit_set(lax.axis_index("col"), 0)
    across, block = across_ref[...], block_ref[...]
    left_block = jnp.where(right, across, block)
    right_block = jnp.where(right, block, across)
    both_ref[0] = left_block
    both_ref[1] = right_block
    message_ref[:n] = jnp.where(odd, right_block, left_block)
    message_ref[n:] = jnp.where(odd, left_block.T[n // 2:], right_block[:n // 2])


def pack(across, block):
    n = block.shape[0]
    return pl.pallas_call(
        pack_kernel,
        out_shape=[jax.ShapeDtypeStruct((2, n, n), jnp.float32), jax.ShapeDtypeStruct((n + n // 2, n), jnp.float32)],
        in_specs=[VMEM] * 2,
        out_specs=[VMEM] * 2,
        compiler_params=pltpu.CompilerParams(vmem_limit_bytes=2 * MIB),
        cost_estimate=estimate(1000, 1000),
        name="pack",
    )(across, block)


def first_factor_kernel(a_ref, side_ref, f_ref, w_ref, cross_ref, *scratch):
    f_ref[...], w_ref[...], cross_ref[...] = eliminate(a_ref[...], side_ref[...], scratch)


def elimination_scratch(n):
    return [pltpu.VMEM((n // SUB, SUB, n), jnp.float32)] * 3


def first_factor(a, side):
    n = a.shape[1]
    square = jax.ShapeDtypeStruct((n, n), jnp.float32)
    return pl.pallas_call(
        first_factor_kernel,
        out_shape=[square] * 3,
        in_specs=[VMEM] * 2,
        out_specs=[VMEM] * 3,
        scratch_shapes=elimination_scratch(n),
        compiler_params=pltpu.CompilerParams(vmem_limit_bytes=4 * MIB),
        cost_estimate=estimate(8 * 10**9, 2 * MIB),
        name="first_factor",
    )(a, side)


def second_factor_kernel(a_ref, cross_ref, w0_ref, matrix_ref, f_ref, w_ref, mixed_ref, blocks_ref, *scratch):
    n = w0_ref.shape[0]
    local_cols = matrix_ref.shape[2]
    sems = scratch[-1]
    copies = [pltpu.make_async_copy(matrix_ref.at[:, :, j, :], blocks_ref.at[j], sems.at[j]) for j in range(local_cols)]
    for copy in copies:
        copy.start()
    odd = is_odd_row()
    w0 = w0_ref[...]
    cross = cross_ref[...]
    both = dot_over_rows(cross, jnp.concatenate([cross, w0], axis=1))
    f1, w1, w10 = eliminate(a_ref[...] - both[:, :n], -both[:, n:], scratch[:-1])
    f_ref[...] = f1
    zero = jnp.zeros((n, n), jnp.float32)
    w_ref[:n, :n] = w0
    w_ref[:n, n:] = zero
    w_ref[n:, :n] = w10
    w_ref[n:, n:] = w1
    mixed_ref[:n, :n] = jnp.where(odd, zero, w0)
    mixed_ref[:n, n:] = jnp.where(odd, w0, zero)
    mixed_ref[n:, :n] = jnp.where(odd, w1, w10)
    mixed_ref[n:, n:] = jnp.where(odd, w10, w1)
    for copy in copies:
        copy.wait()


def second_factor(a, cross, w0, matrix):
    local_rows, n, local_cols, _ = matrix.shape
    square = jax.ShapeDtypeStruct((n, n), jnp.float32)
    double = jax.ShapeDtypeStruct((2 * n, 2 * n), jnp.float32)
    blocks = jax.ShapeDtypeStruct((local_cols, local_rows, n, n), jnp.float32)
    return pl.pallas_call(
        second_factor_kernel,
        out_shape=[square, double, double, blocks],
        in_specs=[VMEM] * 3 + [HBM],
        out_specs=[VMEM] * 4,
        scratch_shapes=elimination_scratch(n) + [pltpu.SemaphoreType.DMA((local_cols,))],
        compiler_params=pltpu.CompilerParams(vmem_limit_bytes=12 * MIB),
        cost_estimate=estimate(8 * 10**9, 4 * MIB),
        name="second_factor",
    )(a, cross, w0, matrix)


def settle_kernel(f0_ref, f1_ref, w_ref, mixed_ref, first_ref, rows_ref, rows_other_ref, ha_ref, hb_ref, oa_ref, ob_ref,
                  blocks_ref, out_ref, result, sems):
    grid_row = lax.axis_index("row")
    grid_col = lax.axis_index("col")
    n = f0_ref.shape[0]
    local_cols, local_rows, _, _ = blocks_ref.shape
    flat = (local_rows - 1) * n
    own = rows_ref[...].reshape(flat, n)
    other = rows_other_ref[...].reshape(flat, n)
    swapped = lax.rem(grid_col, 2) == 1
    rows = jnp.concatenate([
        jnp.concatenate([first_ref[0], jnp.where(swapped, other, own)], axis=0),
        jnp.concatenate([first_ref[1], jnp.where(swapped, own, other)], axis=0)], axis=1)
    solved = dot_parts(stacked(rows), parts(w_ref[...]), ((1,), (1,)))
    left = stacked(solved)
    mixed = stacked(mixed_ref[...])
    copies = []
    for j in range(0, local_cols, 2):
        pair = (j, j + 1)
        tops = jnp.concatenate(
            [jnp.concatenate([ha_ref[b], hb_ref[b], oa_ref[b], ob_ref[b]], axis=0) for b in pair], axis=1)
        update = dot_parts(left, parts(dot_parts(mixed, parts(tops))))
        for b in pair:
            part = update[:, (b - j) * n:(b - j + 1) * n].reshape(local_rows, n, n)
            result[b] = blocks_ref[b] - part
        if j == 0:
            @pl.when(grid_col == 0)
            def _():
                result[0] = solved[:, :n].reshape(local_rows, n, n)

            @pl.when(grid_col == 1)
            def _():
                result[0] = solved[:, n:].reshape(local_rows, n, n)

        @pl.when(grid_row <= 1)
        def _():
            for b in pair:
                if b > 0:
                    result[b, 0] = jnp.zeros((n, n), jnp.float32)
            if j == 0:
                @pl.when(grid_col > grid_row)
                def _():
                    result[0, 0] = jnp.zeros((n, n), jnp.float32)

                @pl.when((grid_row == 0) & (grid_col == 0))
                def _():
                    result[0, 0] = f0_ref[...]

                @pl.when((grid_row == 1) & (grid_col == 1))
                def _():
                    result[0, 0] = f1_ref[...]
        for b in pair:
            copy = pltpu.make_async_copy(result.at[b], out_ref.at[:, :, b, :], sems.at[b])
            copy.start()
            copies.append(copy)
    for copy in copies:
        copy.wait()


def settle(f0, f1, w, mixed, first_rows, rows, rows_other, ha, hb, oa, ob, blocks):
    local_cols, local_rows, n, _ = blocks.shape
    return pl.pallas_call(
        settle_kernel,
        out_shape=jax.ShapeDtypeStruct((local_rows, n, local_cols, n), jnp.float32),
        in_specs=[VMEM] * 12,
        out_specs=HBM,
        scratch_shapes=[pltpu.VMEM(blocks.shape, jnp.float32), pltpu.SemaphoreType.DMA((local_cols,))],
        compiler_params=pltpu.CompilerParams(vmem_limit_bytes=32 * MIB),
        cost_estimate=estimate(4 * 10**9, 6 * MIB),
        name="settle",
    )(f0, f1, w, mixed, first_rows, rows, rows_other, ha, hb, oa, ob, blocks)


def exchange(value, axis, mask, size):
    return lax.ppermute(value, axis, [(i, i ^ mask) for i in range(size)])


def bit_set(index, bit):
    return ((index >> bit) & 1) == 1


def spread(own, axis, index, size, bits):
    held = own
    for bit in bits:
        held = jnp.where(bit_set(index, bit), exchange(held, axis, 1 << bit, size), held)
    return held


def region(run, *values):
    shapes = jax.eval_shape(run, *values)

    def skip(*_):
        return jax.tree.map(lambda leaf: jnp.zeros(leaf.shape, leaf.dtype), shapes)

    everywhere = lax.axis_index("row") < lax.axis_size("row")
    return lax.cond(everywhere, run, skip, *values)


def after(value, *others):
    return lax.optimization_barrier((value,) + others)


def shards(kernel):
    grid_row = lax.axis_index("row")
    grid_col = lax.axis_index("col")
    n_row = lax.axis_size("row")
    n_col = lax.axis_size("col")
    row_bits = list(range(1, n_row.bit_length() - 1))
    col_bits = list(range(1, n_col.bit_length() - 1))
    odd = (grid_row % 2) == 1

    block = corner_block(kernel)
    column, upper, lower = panels(kernel)
    first_bit, last_bit = row_bits[0], row_bits[-1]

    moved = exchange(block, "col", 1 << col_bits[0], n_col)
    upper_moved = exchange(upper, "row", 1 << first_bit, n_row)
    lower_moved = exchange(lower, "row", 1 << last_bit, n_row)

    def along_col(new, old):
        block = jnp.where(bit_set(grid_col, col_bits[0]), new, old)
        return spread(block, "col", grid_col, n_col, col_bits[1:])

    block = region(along_col, moved, block)
    across = exchange(block, "col", 1, n_col)
    ha = jnp.where(bit_set(grid_row, first_bit), upper_moved, upper)
    hb = jnp.where(bit_set(grid_row, last_bit), lower_moved, lower)
    across, block, ha, hb, column = after(across, block, ha, hb, column)

    first_rows, pair = pack(across, block)
    moved = exchange(pair, "row", 1 << first_bit, n_row)
    column_moved = exchange(column, "col", 1 << col_bits[0], n_col)
    pair = jnp.where(bit_set(grid_row, first_bit), moved, pair)
    pair, ha, hb = after(pair, ha, hb)
    moved = exchange(pair, "row", 1 << row_bits[1], n_row)
    ha_moved = exchange(ha, "row", 1 << row_bits[1], n_row)
    hb_moved = exchange(hb, "row", 1 << row_bits[-2], n_row)
    rows = jnp.where(bit_set(grid_col, col_bits[0]), column_moved, column)
    moved, pair, rows = after(moved, pair, rows)
    pair = jnp.where(bit_set(grid_row, row_bits[1]), moved, pair)
    pair = spread(pair, "row", grid_row, n_row, row_bits[2:])
    other = exchange(pair, "row", 1, n_row)
    ha = jnp.where(bit_set(grid_row, row_bits[1]), ha_moved, ha)
    hb = jnp.where(bit_set(grid_row, row_bits[-2]), hb_moved, hb)
    other, pair, ha, hb = after(other, pair, ha, hb)

    n = block.shape[0]
    a00 = jnp.where(odd, other[:n], pair[:n])
    a11 = jnp.where(odd, pair[:n], other[:n])
    a01 = jnp.concatenate([jnp.where(odd, other[n:], pair[n:]), jnp.where(odd, pair[n:], other[n:])], axis=0)
    f0, w0, cross = first_factor(a00, a01)

    rows = spread(rows, "col", grid_col, n_col, col_bits[1:])
    rows_other = exchange(rows, "col", 1, n_col)
    w0, row_then, ha, hb = after(w0, grid_row, ha, hb)
    ha = spread(ha, "row", row_then, n_row, row_bits[2:])
    hb = spread(hb, "row", row_then, n_row, row_bits[:-2][::-1])
    oa = exchange(ha, "row", 1, n_row)
    ob = exchange(hb, "row", 1, n_row)
    a11, rows_other = after(a11, rows_other)
    f1, w, mixed, blocks = second_factor(a11, cross, w0, kernel)
    return settle(f0, f1, w, mixed, first_rows, rows, rows_other, ha, hb, oa, ob, blocks)


def solution(mesh):
    in_specs = (P(None, "row", None, "col"),)
    out_specs = P(None, "row", None, "col")
    return jax.shard_map(shards, mesh=mesh, in_specs=in_specs, out_specs=out_specs, check_vma=False)
```

```python
import jax
import jax.numpy as jnp
from jax import lax
from jax.experimental import pallas as pl
from jax.experimental.pallas import tpu as pltpu
from jax.sharding import PartitionSpec as P

SUB = 8
PANEL = 4
MIB = 1024 * 1024
VMEM = pl.BlockSpec(memory_space=pltpu.VMEM)
HBM = pl.BlockSpec(memory_space=pltpu.HBM)


def parts(x):
    high = x.astype(jnp.bfloat16)
    rest = x - high.astype(jnp.float32)
    middle = rest.astype(jnp.bfloat16)
    return high, middle, (rest - middle.astype(jnp.float32)).astype(jnp.bfloat16)


def dot_over_rows(a, b):
    a, b = parts(a), parts(b)
    lhs = jnp.concatenate([a[2], a[0], a[1], a[1], a[0], a[0]], axis=0)
    rhs = jnp.concatenate([b[0], b[2], b[1], b[0], b[1], b[0]], axis=0)
    return lax.dot_general(lhs, rhs, (((0,), (0,)), ((), ())), preferred_element_type=jnp.float32)


def wide(a):
    a = parts(a)
    return jnp.concatenate([a[2], a[0], a[1], a[1], a[0], a[0]], axis=1)


def tall(b):
    b = parts(b)
    return jnp.concatenate([b[0], b[2], b[1], b[0], b[1], b[0]], axis=0)


def times(a, b):
    return jnp.dot(a, b, preferred_element_type=jnp.float32)


def panel_rows(panel, first_ref, rows_ref, rows_other_ref):
    n = rows_ref.shape[-1]
    flat = rows_ref.shape[0] * n
    here = lax.rem(lax.axis_index("col"), 2) == panel
    rest = jnp.where(here, rows_ref[...].reshape(flat, n), rows_other_ref[...].reshape(flat, n))
    return jnp.concatenate([first_ref[panel], rest], axis=0)


def full(row):
    return jnp.broadcast_to(row, (SUB, row.shape[-1]))


def eliminate(s, extra, scratch, beside=()):
    n = s.shape[0]
    groups = n // SUB
    sub = lax.broadcasted_iota(jnp.int32, (SUB, n), 0)
    lane = lax.broadcasted_iota(jnp.int32, (SUB, n), 1)
    rows = lax.broadcasted_iota(jnp.int32, (n, n), 0)
    cols = lax.broadcasted_iota(jnp.int32, (n, n), 1)
    for ref, value in zip(scratch, (s, jnp.where(rows == cols, 1.0, 0.0), extra)):
        ref[...] = value.reshape(groups, SUB, n)
    sides = range(len(scratch))
    for g in range(groups):
        start = g * SUB
        until = (g // PANEL + 1) * PANEL
        left = until - g
        rest = scratch[0][g:until]
        spread = [jnp.broadcast_to(rest[:, :, start + j:start + j + 1], (left, SUB, n)) for j in range(SUB)]
        unit = {(i, j): full(spread[j][0, i:i + 1, :]) for j in range(SUB) for i in range(j, SUB)}
        row = [[full(ref[g, k:k + 1, :]) for k in range(SUB)] for ref in scratch]
        scaled = [[] for _ in sides]
        tops = [None for _ in sides]
        for k in range(SUB):
            pivot = unit[k, k]
            guess = pl.reciprocal(pivot, approx=True)
            rest_of = 2.0 - pivot * guess
            recip = guess * rest_of
            root = lax.rsqrt(pivot)
            for j in range(k + 1, SUB):
                for i in range(j, SUB):
                    unit[i, j] = unit[i, j] - (unit[i, k] * unit[j, k] * guess) * rest_of
            factors = {j: unit[j, k] * recip for j in range(k + 1, SUB)}
            for j in range(k + 1, SUB):
                spread[j] = spread[j] - spread[k] * factors[j][None]
            for m in sides:
                for j in range(k + 1, SUB):
                    row[m][j] = row[m][j] - row[m][k] * factors[j]
                scaled[m].append(row[m][k] * recip)
                final = row[m][k] * root
                tops[m] = final if k == 0 else jnp.where(sub == k, final, tops[m])
        scratch[0][g] = jnp.where(lane >= start + sub, tops[0], 0.0)
        for m in sides[1:]:
            scratch[m][g] = tops[m]
        if left > 1:
            for m in sides:
                low = scratch[m][g + 1:until]
                for k in range(SUB):
                    low = low - spread[k][1:] * scaled[m][k][None]
                scratch[m][g + 1:until] = low
        elif until < groups:
            done = [ref[until - PANEL:until].reshape(PANEL * SUB, n) for ref in scratch]
            update = dot_over_rows(done[0], jnp.concatenate(done, axis=1))
            for m in sides:
                part = update[until * SUB:, m * n:(m + 1) * n]
                scratch[m][until:] = scratch[m][until:] - part.reshape(groups - until, SUB, n)
        if g < len(beside):
            beside[g]()
    upper, inverse, product = [ref[...].reshape(n, n) for ref in scratch]
    return upper.T, inverse, product


def is_odd_row():
    return lax.rem(lax.axis_index("row"), 2) == 1


def stacked(a):
    return jnp.concatenate(parts(a)[::-1], axis=0)


def dot_parts(a, b, dims=((1,), (0,))):
    m = a.shape[0] // 3
    high, middle, low = [
        lax.dot_general(a[i * m:], b[i], (dims, ((), ())), preferred_element_type=jnp.float32) for i in range(3)]
    small = high[:m] + middle[:m] + low
    return small + (high[m:2 * m] + middle[m:]) + high[2 * m:]


def estimate(flops, nbytes):
    return pl.CostEstimate(flops=flops, bytes_accessed=nbytes, transcendentals=0)


def corner_kernel(matrix_ref, block_ref, sem):
    copy = pltpu.make_async_copy(matrix_ref.at[0, :, 0, :], block_ref, sem)
    copy.start()
    copy.wait()


def corner_block(matrix):
    n = matrix.shape[1]
    return pl.pallas_call(
        corner_kernel,
        out_shape=jax.ShapeDtypeStruct((n, n), jnp.float32),
        in_specs=[HBM],
        out_specs=VMEM,
        scratch_shapes=[pltpu.SemaphoreType.DMA(())],
        compiler_params=pltpu.CompilerParams(vmem_limit_bytes=2 * MIB),
        cost_estimate=estimate(0, 3 * MIB),
        name="corner_block",
    )(matrix)


def panels_kernel(matrix_ref, column_ref, upper_ref, lower_ref, sems):
    local_cols, half, _ = upper_ref.shape
    copies = [pltpu.make_async_copy(matrix_ref.at[pl.ds(1, column_ref.shape[0]), :, 0, :], column_ref, sems.at[0])]
    for j in range(local_cols):
        copies.append(pltpu.make_async_copy(matrix_ref.at[0, pl.ds(0, half), j, :], upper_ref.at[j], sems.at[1 + j]))
        copies.append(pltpu.make_async_copy(
            matrix_ref.at[0, pl.ds(half, half), j, :], lower_ref.at[j], sems.at[1 + local_cols + j]))
    for copy in copies:
        copy.start()
    for copy in copies:
        copy.wait()


def panels(matrix):
    local_rows, n, local_cols, _ = matrix.shape
    strip = jax.ShapeDtypeStruct((local_cols, n // 2, n), jnp.float32)
    return pl.pallas_call(
        panels_kernel,
        out_shape=[jax.ShapeDtypeStruct((local_rows - 1, n, n), jnp.float32), strip, strip],
        in_specs=[HBM],
        out_specs=[VMEM] * 3,
        scratch_shapes=[pltpu.SemaphoreType.DMA((1 + 2 * local_cols,))],
        compiler_params=pltpu.CompilerParams(vmem_limit_bytes=4 * MIB),
        cost_estimate=estimate(0, 4 * MIB),
        name="panels",
    )(matrix)


def pack_kernel(across_ref, block_ref, both_ref, message_ref):
    n = block_ref.shape[0]
    odd = is_odd_row()
    right = bit_set(lax.axis_index("col"), 0)
    across, block = across_ref[...], block_ref[...]
    left_block = jnp.where(right, across, block)
    right_block = jnp.where(right, block, across)
    both_ref[0] = left_block
    both_ref[1] = right_block
    message_ref[:n] = jnp.where(odd, right_block, left_block)
    message_ref[n:] = jnp.where(odd, left_block.T[n // 2:], right_block[:n // 2])


def pack(across, block):
    n = block.shape[0]
    return pl.pallas_call(
        pack_kernel,
        out_shape=[jax.ShapeDtypeStruct((2, n, n), jnp.float32), jax.ShapeDtypeStruct((n + n // 2, n), jnp.float32)],
        in_specs=[VMEM] * 2,
        out_specs=[VMEM] * 2,
        compiler_params=pltpu.CompilerParams(vmem_limit_bytes=2 * MIB),
        cost_estimate=estimate(1000, 1000),
        name="pack",
    )(across, block)


def first_factor_kernel(a_ref, side_ref, f_ref, w_ref, cross_ref, *scratch):
    f_ref[...], w_ref[...], cross_ref[...] = eliminate(a_ref[...], side_ref[...], scratch)


def elimination_scratch(n):
    return [pltpu.VMEM((n // SUB, SUB, n), jnp.float32)] * 3


def first_factor(a, side):
    n = a.shape[1]
    square = jax.ShapeDtypeStruct((n, n), jnp.float32)
    return pl.pallas_call(
        first_factor_kernel,
        out_shape=[square] * 3,
        in_specs=[VMEM] * 2,
        out_specs=[VMEM] * 3,
        scratch_shapes=elimination_scratch(n),
        compiler_params=pltpu.CompilerParams(vmem_limit_bytes=4 * MIB),
        cost_estimate=estimate(8 * 10**9, 2 * MIB),
        name="first_factor",
    )(a, side)


def second_factor_kernel(a_ref, cross_ref, w0_ref, first_ref, rows_ref, rows_other_ref, ha_ref, hb_ref, oa_ref, ob_ref, matrix_ref,
                         f_ref, low_ref, mixed_ref, solved_ref, blocks_ref, left, right, sems, *scratch):
    n = w0_ref.shape[0]
    local_cols = matrix_ref.shape[2]
    local_rows = matrix_ref.shape[0]
    copies = [pltpu.make_async_copy(matrix_ref.at[:, :, j, :], blocks_ref.at[j], sems.at[j]) for j in range(local_cols)]
    for copy in copies:
        copy.start()
    odd = is_odd_row()
    w0 = w0_ref[...]
    cross = cross_ref[...]

    def solve_rows():
        solved = times(wide(panel_rows(0, first_ref, rows_ref, rows_other_ref)), tall(w0.T))
        solved_ref[...] = solved
        left[...] = wide(solved)

    def solve_top(j):
        def step():
            top = jnp.concatenate([
                jnp.concatenate([jnp.where(odd, oa_ref[b], ha_ref[b]), jnp.where(odd, ob_ref[b], hb_ref[b])], axis=0)
                for b in (j, j + 1)], axis=1)
            right[...] = tall(times(wide(w0), tall(top)))
        return step

    def update(j, i):
        def step():
            if i == 0:
                copies[j].wait()
                copies[j + 1].wait()
            change = times(left[i * n:(i + 2) * n], right[...])
            for b in range(2):
                part = change[:, b * n:(b + 1) * n].reshape(2, n, n)
                blocks_ref[j + b, i:i + 2] = blocks_ref[j + b, i:i + 2] - part
        return step

    steps = [solve_rows]
    for j in range(0, local_cols, 2):
        steps.append(solve_top(j))
        steps.extend(update(j, i) for i in range(0, local_rows, 2))

    both = dot_over_rows(cross, jnp.concatenate([cross, w0], axis=1))
    groups = n // SUB
    each = -(-len(steps) // groups)

    def several(some):
        def run():
            for step in some:
                step()
        return run

    beside = [several(steps[at:at + each]) for at in range(0, len(steps), each)]
    f1, w1, w10 = eliminate(a_ref[...] - both[:, :n], -both[:, n:], scratch, beside)
    f_ref[...] = f1
    low_ref[:, :n] = w10
    low_ref[:, n:] = w1
    mixed_ref[:, :n] = jnp.where(odd, w1, w10)
    mixed_ref[:, n:] = jnp.where(odd, w10, w1)


def second_factor(a, cross, w0, first_rows, rows, rows_other, ha, hb, oa, ob, matrix):
    local_rows, n, local_cols, _ = matrix.shape
    square = jax.ShapeDtypeStruct((n, n), jnp.float32)
    half = jax.ShapeDtypeStruct((n, 2 * n), jnp.float32)
    solved = jax.ShapeDtypeStruct((local_rows * n, n), jnp.float32)
    blocks = jax.ShapeDtypeStruct((local_cols, local_rows, n, n), jnp.float32)
    return pl.pallas_call(
        second_factor_kernel,
        out_shape=[square, half, half, solved, blocks],
        in_specs=[VMEM] * 10 + [HBM],
        out_specs=[VMEM] * 5,
        scratch_shapes=[
            pltpu.VMEM((local_rows * n, 6 * n), jnp.bfloat16),
            pltpu.VMEM((6 * n, 2 * n), jnp.bfloat16),
            pltpu.SemaphoreType.DMA((local_cols,)),
        ] + elimination_scratch(n),
        compiler_params=pltpu.CompilerParams(vmem_limit_bytes=20 * MIB),
        cost_estimate=estimate(8 * 10**9, 4 * MIB),
        name="second_factor",
    )(a, cross, w0, first_rows, rows, rows_other, ha, hb, oa, ob, matrix)


def settle_kernel(f0_ref, f1_ref, low_ref, mixed_ref, solved_ref, first_ref, rows_ref, rows_other_ref, ha_ref, hb_ref, oa_ref, ob_ref,
                  blocks_ref, out_ref, result, sems):
    grid_row = lax.axis_index("row")
    grid_col = lax.axis_index("col")
    n = f0_ref.shape[0]
    local_cols, local_rows, _, _ = blocks_ref.shape
    rows = jnp.concatenate([panel_rows(p, first_ref, rows_ref, rows_other_ref) for p in range(2)], axis=1)
    solved = dot_parts(stacked(rows), parts(low_ref[...]), ((1,), (1,)))
    left = wide(solved)
    mixed = stacked(mixed_ref[...])
    copies = []
    for j in range(0, local_cols, 2):
        pair = (j, j + 1)
        tops = jnp.concatenate(
            [jnp.concatenate([ha_ref[b], hb_ref[b], oa_ref[b], ob_ref[b]], axis=0) for b in pair], axis=1)
        update = times(left, tall(dot_parts(mixed, parts(tops))))
        for b in pair:
            part = update[:, (b - j) * n:(b - j + 1) * n].reshape(local_rows, n, n)
            result[b] = blocks_ref[b] - part
        if j == 0:
            @pl.when(grid_col == 0)
            def _():
                result[0] = solved_ref[...].reshape(local_rows, n, n)

            @pl.when(grid_col == 1)
            def _():
                result[0] = solved.reshape(local_rows, n, n)

        @pl.when(grid_row <= 1)
        def _():
            for b in pair:
                if b > 0:
                    result[b, 0] = jnp.zeros((n, n), jnp.float32)
            if j == 0:
                @pl.when(grid_col > grid_row)
                def _():
                    result[0, 0] = jnp.zeros((n, n), jnp.float32)

                @pl.when((grid_row == 0) & (grid_col == 0))
                def _():
                    result[0, 0] = f0_ref[...]

                @pl.when((grid_row == 1) & (grid_col == 1))
                def _():
                    result[0, 0] = f1_ref[...]
        for b in pair:
            copy = pltpu.make_async_copy(result.at[b], out_ref.at[:, :, b, :], sems.at[b])
            copy.start()
            copies.append(copy)
    for copy in copies:
        copy.wait()


def settle(f0, f1, low, mixed, solved, first_rows, rows, rows_other, ha, hb, oa, ob, blocks):
    local_cols, local_rows, n, _ = blocks.shape
    return pl.pallas_call(
        settle_kernel,
        out_shape=jax.ShapeDtypeStruct((local_rows, n, local_cols, n), jnp.float32),
        in_specs=[VMEM] * 13,
        out_specs=HBM,
        scratch_shapes=[pltpu.VMEM(blocks.shape, jnp.float32), pltpu.SemaphoreType.DMA((local_cols,))],
        compiler_params=pltpu.CompilerParams(vmem_limit_bytes=32 * MIB),
        cost_estimate=estimate(4 * 10**9, 6 * MIB),
        name="settle",
    )(f0, f1, low, mixed, solved, first_rows, rows, rows_other, ha, hb, oa, ob, blocks)


def exchange(value, axis, mask, size):
    return lax.ppermute(value, axis, [(i, i ^ mask) for i in range(size)])


def bit_set(index, bit):
    return ((index >> bit) & 1) == 1


def spread(own, axis, index, size, bits):
    held = own
    for bit in bits:
        held = jnp.where(bit_set(index, bit), exchange(held, axis, 1 << bit, size), held)
    return held


def region(run, *values):
    shapes = jax.eval_shape(run, *values)

    def skip(*_):
        return jax.tree.map(lambda leaf: jnp.zeros(leaf.shape, leaf.dtype), shapes)

    everywhere = lax.axis_index("row") < lax.axis_size("row")
    return lax.cond(everywhere, run, skip, *values)


def after(value, *others):
    return lax.optimization_barrier((value,) + others)


def shards(kernel):
    grid_row = lax.axis_index("row")
    grid_col = lax.axis_index("col")
    n_row = lax.axis_size("row")
    n_col = lax.axis_size("col")
    row_bits = list(range(1, n_row.bit_length() - 1))
    col_bits = list(range(1, n_col.bit_length() - 1))
    odd = (grid_row % 2) == 1

    block = corner_block(kernel)
    column, upper, lower = panels(kernel)
    first_bit, last_bit = row_bits[0], row_bits[-1]

    moved = exchange(block, "col", 1 << col_bits[0], n_col)
    upper_moved = exchange(upper, "row", 1 << first_bit, n_row)
    lower_moved = exchange(lower, "row", 1 << last_bit, n_row)

    def along_col(new, old):
        block = jnp.where(bit_set(grid_col, col_bits[0]), new, old)
        return spread(block, "col", grid_col, n_col, col_bits[1:])

    block = region(along_col, moved, block)
    across = exchange(block, "col", 1, n_col)
    ha = jnp.where(bit_set(grid_row, first_bit), upper_moved, upper)
    hb = jnp.where(bit_set(grid_row, last_bit), lower_moved, lower)
    across, block, ha, hb, column = after(across, block, ha, hb, column)

    first_rows, pair = pack(across, block)
    moved = exchange(pair, "row", 1 << first_bit, n_row)
    column_moved = exchange(column, "col", 1 << col_bits[0], n_col)
    pair = jnp.where(bit_set(grid_row, first_bit), moved, pair)
    pair, ha, hb = after(pair, ha, hb)
    moved = exchange(pair, "row", 1 << row_bits[1], n_row)
    ha_moved = exchange(ha, "row", 1 << row_bits[1], n_row)
    hb_moved = exchange(hb, "row", 1 << row_bits[-2], n_row)
    rows = jnp.where(bit_set(grid_col, col_bits[0]), column_moved, column)
    moved, pair, rows = after(moved, pair, rows)
    pair = jnp.where(bit_set(grid_row, row_bits[1]), moved, pair)
    pair = spread(pair, "row", grid_row, n_row, row_bits[2:])
    other = exchange(pair, "row", 1, n_row)
    ha = jnp.where(bit_set(grid_row, row_bits[1]), ha_moved, ha)
    hb = jnp.where(bit_set(grid_row, row_bits[-2]), hb_moved, hb)
    ha = spread(ha, "row", grid_row, n_row, row_bits[2:])
    hb = spread(hb, "row", grid_row, n_row, row_bits[:-2][::-1])
    other, pair, ha, hb = after(other, pair, ha, hb)
    oa = exchange(ha, "row", 1, n_row)
    ob = exchange(hb, "row", 1, n_row)

    n = block.shape[0]
    a00 = jnp.where(odd, other[:n], pair[:n])
    a11 = jnp.where(odd, pair[:n], other[:n])
    a01 = jnp.concatenate([jnp.where(odd, other[n:], pair[n:]), jnp.where(odd, pair[n:], other[n:])], axis=0)
    f0, w0, cross = first_factor(a00, a01)

    rows = spread(rows, "col", grid_col, n_col, col_bits[1:])
    rows_other = exchange(rows, "col", 1, n_col)
    f1, low, mixed, solved, blocks = second_factor(a11, cross, w0, first_rows, rows, rows_other, ha, hb, oa, ob, kernel)
    return settle(f0, f1, low, mixed, solved, first_rows, rows, rows_other, ha, hb, oa, ob, blocks)


def solution(mesh):
    in_specs = (P(None, "row", None, "col"),)
    out_specs = P(None, "row", None, "col")
    return jax.shard_map(shards, mesh=mesh, in_specs=in_specs, out_specs=out_specs, check_vma=False)
```

```python
import jax
import jax.numpy as jnp
from jax import lax
from jax.experimental import pallas as pl
from jax.experimental.pallas import tpu as pltpu
from jax.sharding import PartitionSpec as P

SUB = 8
PANEL = 4
MIB = 1024 * 1024
VMEM = pl.BlockSpec(memory_space=pltpu.VMEM)
HBM = pl.BlockSpec(memory_space=pltpu.HBM)


def parts(x):
    high = x.astype(jnp.bfloat16)
    rest = x - high.astype(jnp.float32)
    middle = rest.astype(jnp.bfloat16)
    return high, middle, (rest - middle.astype(jnp.float32)).astype(jnp.bfloat16)


def dot_over_rows(a, b):
    a, b = parts(a), parts(b)
    lhs = jnp.concatenate([a[2], a[0], a[1], a[1], a[0], a[0]], axis=0)
    rhs = jnp.concatenate([b[0], b[2], b[1], b[0], b[1], b[0]], axis=0)
    return lax.dot_general(lhs, rhs, (((0,), (0,)), ((), ())), preferred_element_type=jnp.float32)


def wide(a):
    a = parts(a)
    return jnp.concatenate([a[2], a[0], a[1], a[1], a[0], a[0]], axis=1)


def tall(b):
    b = parts(b)
    return jnp.concatenate([b[0], b[2], b[1], b[0], b[1], b[0]], axis=0)


def times(a, b):
    return jnp.dot(a, b, preferred_element_type=jnp.float32)


def panel_rows(panel, first_ref, rows_ref, rows_other_ref):
    n = rows_ref.shape[-1]
    flat = rows_ref.shape[0] * n
    here = lax.rem(lax.axis_index("col"), 2) == panel
    rest = jnp.where(here, rows_ref[...].reshape(flat, n), rows_other_ref[...].reshape(flat, n))
    return jnp.concatenate([first_ref[panel], rest], axis=0)


def full(row):
    return jnp.broadcast_to(row, (SUB, row.shape[-1]))


def eliminate(s, extra, scratch, beside=()):
    n = s.shape[0]
    groups = n // SUB
    sub = lax.broadcasted_iota(jnp.int32, (SUB, n), 0)
    lane = lax.broadcasted_iota(jnp.int32, (SUB, n), 1)
    rows = lax.broadcasted_iota(jnp.int32, (n, n), 0)
    cols = lax.broadcasted_iota(jnp.int32, (n, n), 1)
    for ref, value in zip(scratch, [s, jnp.where(rows == cols, 1.0, 0.0)] + list(extra)):
        ref[...] = value.reshape(groups, SUB, n)
    sides = range(len(scratch))
    for g in range(groups):
        start = g * SUB
        until = (g // PANEL + 1) * PANEL
        left = until - g
        rest = scratch[0][g:until]
        spread = [jnp.broadcast_to(rest[:, :, start + j:start + j + 1], (left, SUB, n)) for j in range(SUB)]
        unit = {(i, j): full(spread[j][0, i:i + 1, :]) for j in range(SUB) for i in range(j, SUB)}
        row = [[full(ref[g, k:k + 1, :]) for k in range(SUB)] for ref in scratch]
        scaled = [[] for _ in sides]
        tops = [None for _ in sides]
        for k in range(SUB):
            pivot = unit[k, k]
            guess = pl.reciprocal(pivot, approx=True)
            rest_of = 2.0 - pivot * guess
            recip = guess * rest_of
            root = lax.rsqrt(pivot)
            for j in range(k + 1, SUB):
                for i in range(j, SUB):
                    unit[i, j] = unit[i, j] - (unit[i, k] * unit[j, k] * guess) * rest_of
            factors = {j: unit[j, k] * recip for j in range(k + 1, SUB)}
            for j in range(k + 1, SUB):
                spread[j] = spread[j] - spread[k] * factors[j][None]
            for m in sides:
                for j in range(k + 1, SUB):
                    row[m][j] = row[m][j] - row[m][k] * factors[j]
                scaled[m].append(row[m][k] * recip)
                final = row[m][k] * root
                tops[m] = final if k == 0 else jnp.where(sub == k, final, tops[m])
        scratch[0][g] = jnp.where(lane >= start + sub, tops[0], 0.0)
        for m in sides[1:]:
            scratch[m][g] = tops[m]
        if left > 1:
            for m in sides:
                low = scratch[m][g + 1:until]
                for k in range(SUB):
                    low = low - spread[k][1:] * scaled[m][k][None]
                scratch[m][g + 1:until] = low
        elif until < groups:
            done = [ref[until - PANEL:until].reshape(PANEL * SUB, n) for ref in scratch]
            update = dot_over_rows(done[0], jnp.concatenate(done, axis=1))
            for m in sides:
                part = update[until * SUB:, m * n:(m + 1) * n]
                scratch[m][until:] = scratch[m][until:] - part.reshape(groups - until, SUB, n)
        if g < len(beside):
            beside[g]()
    upper, *others = [ref[...].reshape(n, n) for ref in scratch]
    return [upper.T] + others


def is_odd_row():
    return lax.rem(lax.axis_index("row"), 2) == 1


def estimate(flops, nbytes):
    return pl.CostEstimate(flops=flops, bytes_accessed=nbytes, transcendentals=0)


def corner_kernel(matrix_ref, block_ref, sem):
    copy = pltpu.make_async_copy(matrix_ref.at[0, :, 0, :], block_ref, sem)
    copy.start()
    copy.wait()


def corner_block(matrix):
    n = matrix.shape[1]
    return pl.pallas_call(
        corner_kernel,
        out_shape=jax.ShapeDtypeStruct((n, n), jnp.float32),
        in_specs=[HBM],
        out_specs=VMEM,
        scratch_shapes=[pltpu.SemaphoreType.DMA(())],
        compiler_params=pltpu.CompilerParams(vmem_limit_bytes=2 * MIB),
        cost_estimate=estimate(0, 3 * MIB),
        name="corner_block",
    )(matrix)


def panels_kernel(matrix_ref, column_ref, upper_ref, lower_ref, sems):
    local_cols, half, _ = upper_ref.shape
    copies = [pltpu.make_async_copy(matrix_ref.at[pl.ds(1, column_ref.shape[0]), :, 0, :], column_ref, sems.at[0])]
    for j in range(local_cols):
        copies.append(pltpu.make_async_copy(matrix_ref.at[0, pl.ds(0, half), j, :], upper_ref.at[j], sems.at[1 + j]))
        copies.append(pltpu.make_async_copy(
            matrix_ref.at[0, pl.ds(half, half), j, :], lower_ref.at[j], sems.at[1 + local_cols + j]))
    for copy in copies:
        copy.start()
    for copy in copies:
        copy.wait()


def panels(matrix):
    local_rows, n, local_cols, _ = matrix.shape
    strip = jax.ShapeDtypeStruct((local_cols, n // 2, n), jnp.float32)
    return pl.pallas_call(
        panels_kernel,
        out_shape=[jax.ShapeDtypeStruct((local_rows - 1, n, n), jnp.float32), strip, strip],
        in_specs=[HBM],
        out_specs=[VMEM] * 3,
        scratch_shapes=[pltpu.SemaphoreType.DMA((1 + 2 * local_cols,))],
        compiler_params=pltpu.CompilerParams(vmem_limit_bytes=4 * MIB),
        cost_estimate=estimate(0, 4 * MIB),
        name="panels",
    )(matrix)


def pack_kernel(across_ref, block_ref, both_ref, message_ref):
    n = block_ref.shape[0]
    odd = is_odd_row()
    right = bit_set(lax.axis_index("col"), 0)
    across, block = across_ref[...], block_ref[...]
    left_block = jnp.where(right, across, block)
    right_block = jnp.where(right, block, across)
    both_ref[0] = left_block
    both_ref[1] = right_block
    message_ref[:n] = jnp.where(odd, right_block, left_block)
    message_ref[n:] = jnp.where(odd, left_block.T[n // 2:], right_block[:n // 2])


def pack(across, block):
    n = block.shape[0]
    return pl.pallas_call(
        pack_kernel,
        out_shape=[jax.ShapeDtypeStruct((2, n, n), jnp.float32), jax.ShapeDtypeStruct((n + n // 2, n), jnp.float32)],
        in_specs=[VMEM] * 2,
        out_specs=[VMEM] * 2,
        compiler_params=pltpu.CompilerParams(vmem_limit_bytes=2 * MIB),
        cost_estimate=estimate(1000, 1000),
        name="pack",
    )(across, block)


def first_factor_kernel(a_ref, side_ref, f_ref, w_ref, cross_ref, *scratch):
    f_ref[...], w_ref[...], cross_ref[...] = eliminate(a_ref[...], [side_ref[...]], scratch)


def elimination_scratch(n, matrices):
    return [pltpu.VMEM((n // SUB, SUB, n), jnp.float32)] * matrices


def first_factor(a, side):
    n = a.shape[1]
    square = jax.ShapeDtypeStruct((n, n), jnp.float32)
    return pl.pallas_call(
        first_factor_kernel,
        out_shape=[square] * 3,
        in_specs=[VMEM] * 2,
        out_specs=[VMEM] * 3,
        scratch_shapes=elimination_scratch(n, 3),
        compiler_params=pltpu.CompilerParams(vmem_limit_bytes=4 * MIB),
        cost_estimate=estimate(8 * 10**9, 2 * MIB),
        name="first_factor",
    )(a, side)


def second_factor_kernel(a_ref, cross_ref, w0_ref, first_ref, rows_ref, rows_other_ref, ha_ref, hb_ref, oa_ref, ob_ref, matrix_ref,
                         f_ref, w_ref, solved_ref, rows_left_ref, top_left_ref, blocks_ref, left, right, sems, *scratch):
    n = w0_ref.shape[0]
    local_cols = matrix_ref.shape[2]
    local_rows = matrix_ref.shape[0]
    copies = [pltpu.make_async_copy(matrix_ref.at[:, :, j, :], blocks_ref.at[j], sems.at[j]) for j in range(local_cols)]
    for copy in copies:
        copy.start()
    odd = is_odd_row()
    w0 = w0_ref[...]
    cross = cross_ref[...]

    def solve_rows():
        solved = times(wide(panel_rows(0, first_ref, rows_ref, rows_other_ref)), tall(w0.T))
        solved_ref[...] = solved
        left[...] = wide(solved)

    def update_rows():
        rows_left_ref[...] = wide(panel_rows(1, first_ref, rows_ref, rows_other_ref) - times(left[...], tall(cross)))

    def top(panel, j):
        here = odd == (panel == 1)
        return jnp.concatenate([
            jnp.concatenate([jnp.where(here, ha_ref[b], oa_ref[b]), jnp.where(here, hb_ref[b], ob_ref[b])], axis=0)
            for b in (j, j + 1)], axis=1)

    def solve_top(j):
        def step():
            right[...] = tall(times(wide(w0), tall(top(0, j))))
            top_left_ref[:, j * n:(j + 2) * n] = tall(top(1, j) - times(wide(cross.T), right[...]))
        return step

    def update(j, i):
        def step():
            if i == 0:
                copies[j].wait()
                copies[j + 1].wait()
            change = times(left[i * n:(i + 2) * n], right[...])
            for b in range(2):
                part = change[:, b * n:(b + 1) * n].reshape(2, n, n)
                blocks_ref[j + b, i:i + 2] = blocks_ref[j + b, i:i + 2] - part
        return step

    steps = [solve_rows, update_rows]
    for j in range(0, local_cols, 2):
        steps.append(solve_top(j))
        steps.extend(update(j, i) for i in range(0, local_rows, 2))

    groups = n // SUB
    each = -(-len(steps) // groups)

    def several(some):
        def run():
            for step in some:
                step()
        return run

    beside = [several(steps[at:at + each]) for at in range(0, len(steps), each)]
    f_ref[...], w_ref[...] = eliminate(a_ref[...] - dot_over_rows(cross, cross), [], scratch, beside)


def second_factor(a, cross, w0, first_rows, rows, rows_other, ha, hb, oa, ob, matrix):
    local_rows, n, local_cols, _ = matrix.shape
    square = jax.ShapeDtypeStruct((n, n), jnp.float32)
    solved = jax.ShapeDtypeStruct((local_rows * n, n), jnp.float32)
    rows_left = jax.ShapeDtypeStruct((local_rows * n, 6 * n), jnp.bfloat16)
    top_left = jax.ShapeDtypeStruct((6 * n, local_cols * n), jnp.bfloat16)
    blocks = jax.ShapeDtypeStruct((local_cols, local_rows, n, n), jnp.float32)
    return pl.pallas_call(
        second_factor_kernel,
        out_shape=[square, square, solved, rows_left, top_left, blocks],
        in_specs=[VMEM] * 10 + [HBM],
        out_specs=[VMEM] * 6,
        scratch_shapes=[
            pltpu.VMEM((local_rows * n, 6 * n), jnp.bfloat16),
            pltpu.VMEM((6 * n, 2 * n), jnp.bfloat16),
            pltpu.SemaphoreType.DMA((local_cols,)),
        ] + elimination_scratch(n, 2),
        compiler_params=pltpu.CompilerParams(vmem_limit_bytes=20 * MIB),
        cost_estimate=estimate(8 * 10**9, 4 * MIB),
        name="second_factor",
    )(a, cross, w0, first_rows, rows, rows_other, ha, hb, oa, ob, matrix)


def settle_kernel(f0_ref, f1_ref, w_ref, solved_ref, rows_left_ref, top_left_ref, blocks_ref, out_ref, result, sems):
    grid_row = lax.axis_index("row")
    grid_col = lax.axis_index("col")
    n = f0_ref.shape[0]
    local_cols, local_rows, _, _ = blocks_ref.shape
    w1 = w_ref[...]
    solved = times(rows_left_ref[...], tall(w1.T))
    left = wide(solved)
    inverse = wide(w1)
    copies = []
    for j in range(0, local_cols, 2):
        pair = (j, j + 1)
        update = times(left, tall(times(inverse, top_left_ref[:, j * n:(j + 2) * n])))
        for b in pair:
            part = update[:, (b - j) * n:(b - j + 1) * n].reshape(local_rows, n, n)
            result[b] = blocks_ref[b] - part
        if j == 0:
            @pl.when(grid_col == 0)
            def _():
                result[0] = solved_ref[...].reshape(local_rows, n, n)

            @pl.when(grid_col == 1)
            def _():
                result[0] = solved.reshape(local_rows, n, n)

        @pl.when(grid_row <= 1)
        def _():
            for b in pair:
                if b > 0:
                    result[b, 0] = jnp.zeros((n, n), jnp.float32)
            if j == 0:
                @pl.when(grid_col > grid_row)
                def _():
                    result[0, 0] = jnp.zeros((n, n), jnp.float32)

                @pl.when((grid_row == 0) & (grid_col == 0))
                def _():
                    result[0, 0] = f0_ref[...]

                @pl.when((grid_row == 1) & (grid_col == 1))
                def _():
                    result[0, 0] = f1_ref[...]
        for b in pair:
            copy = pltpu.make_async_copy(result.at[b], out_ref.at[:, :, b, :], sems.at[b])
            copy.start()
            copies.append(copy)
    for copy in copies:
        copy.wait()


def settle(f0, f1, w1, solved, rows_left, top_left, blocks):
    local_cols, local_rows, n, _ = blocks.shape
    return pl.pallas_call(
        settle_kernel,
        out_shape=jax.ShapeDtypeStruct((local_rows, n, local_cols, n), jnp.float32),
        in_specs=[VMEM] * 7,
        out_specs=HBM,
        scratch_shapes=[pltpu.VMEM(blocks.shape, jnp.float32), pltpu.SemaphoreType.DMA((local_cols,))],
        compiler_params=pltpu.CompilerParams(vmem_limit_bytes=32 * MIB),
        cost_estimate=estimate(4 * 10**9, 6 * MIB),
        name="settle",
    )(f0, f1, w1, solved, rows_left, top_left, blocks)


def exchange(value, axis, mask, size):
    return lax.ppermute(value, axis, [(i, i ^ mask) for i in range(size)])


def bit_set(index, bit):
    return ((index >> bit) & 1) == 1


def spread(own, axis, index, size, bits):
    held = own
    for bit in bits:
        held = jnp.where(bit_set(index, bit), exchange(held, axis, 1 << bit, size), held)
    return held


def region(run, *values):
    shapes = jax.eval_shape(run, *values)

    def skip(*_):
        return jax.tree.map(lambda leaf: jnp.zeros(leaf.shape, leaf.dtype), shapes)

    everywhere = lax.axis_index("row") < lax.axis_size("row")
    return lax.cond(everywhere, run, skip, *values)


def after(value, *others):
    return lax.optimization_barrier((value,) + others)


def shards(kernel):
    grid_row = lax.axis_index("row")
    grid_col = lax.axis_index("col")
    n_row = lax.axis_size("row")
    n_col = lax.axis_size("col")
    row_bits = list(range(1, n_row.bit_length() - 1))
    col_bits = list(range(1, n_col.bit_length() - 1))
    odd = (grid_row % 2) == 1

    block = corner_block(kernel)
    column, upper, lower = panels(kernel)
    first_bit, last_bit = row_bits[0], row_bits[-1]

    moved = exchange(block, "col", 1 << col_bits[0], n_col)
    upper_moved = exchange(upper, "row", 1 << first_bit, n_row)
    lower_moved = exchange(lower, "row", 1 << last_bit, n_row)

    def along_col(new, old):
        block = jnp.where(bit_set(grid_col, col_bits[0]), new, old)
        return spread(block, "col", grid_col, n_col, col_bits[1:])

    block = region(along_col, moved, block)
    across = exchange(block, "col", 1, n_col)
    ha = jnp.where(bit_set(grid_row, first_bit), upper_moved, upper)
    hb = jnp.where(bit_set(grid_row, last_bit), lower_moved, lower)
    across, block, ha, hb, column = after(across, block, ha, hb, column)

    first_rows, pair = pack(across, block)
    moved = exchange(pair, "row", 1 << first_bit, n_row)
    column_moved = exchange(column, "col", 1 << col_bits[0], n_col)
    pair = jnp.where(bit_set(grid_row, first_bit), moved, pair)
    pair, ha, hb = after(pair, ha, hb)
    moved = exchange(pair, "row", 1 << row_bits[1], n_row)
    ha_moved = exchange(ha, "row", 1 << row_bits[1], n_row)
    hb_moved = exchange(hb, "row", 1 << row_bits[-2], n_row)
    rows = jnp.where(bit_set(grid_col, col_bits[0]), column_moved, column)
    moved, pair, rows = after(moved, pair, rows)
    pair = jnp.where(bit_set(grid_row, row_bits[1]), moved, pair)
    pair = spread(pair, "row", grid_row, n_row, row_bits[2:])
    other = exchange(pair, "row", 1, n_row)
    ha = jnp.where(bit_set(grid_row, row_bits[1]), ha_moved, ha)
    hb = jnp.where(bit_set(grid_row, row_bits[-2]), hb_moved, hb)
    ha = spread(ha, "row", grid_row, n_row, row_bits[2:])
    hb = spread(hb, "row", grid_row, n_row, row_bits[:-2][::-1])
    other, pair, ha, hb = after(other, pair, ha, hb)
    oa = exchange(ha, "row", 1, n_row)
    ob = exchange(hb, "row", 1, n_row)

    n = block.shape[0]
    a00 = jnp.where(odd, other[:n], pair[:n])
    a11 = jnp.where(odd, pair[:n], other[:n])
    a01 = jnp.concatenate([jnp.where(odd, other[n:], pair[n:]), jnp.where(odd, pair[n:], other[n:])], axis=0)
    f0, w0, cross = first_factor(a00, a01)

    rows = spread(rows, "col", grid_col, n_col, col_bits[1:])
    rows_other = exchange(rows, "col", 1, n_col)
    f1, w1, solved, rows_left, top_left, blocks = second_factor(
        a11, cross, w0, first_rows, rows, rows_other, ha, hb, oa, ob, kernel)
    return settle(f0, f1, w1, solved, rows_left, top_left, blocks)


def solution(mesh):
    in_specs = (P(None, "row", None, "col"),)
    out_specs = P(None, "row", None, "col")
    return jax.shard_map(shards, mesh=mesh, in_specs=in_specs, out_specs=out_specs, check_vma=False)
```

```python
import jax
import jax.numpy as jnp
from jax import lax
from jax.experimental import pallas as pl
from jax.experimental.pallas import tpu as pltpu
from jax.sharding import PartitionSpec as P

SUB = 8
PANEL = 4
MIB = 1024 * 1024
VMEM = pl.BlockSpec(memory_space=pltpu.VMEM)
HBM = pl.BlockSpec(memory_space=pltpu.HBM)


def parts(x):
    high = x.astype(jnp.bfloat16)
    rest = x - high.astype(jnp.float32)
    middle = rest.astype(jnp.bfloat16)
    return high, middle, (rest - middle.astype(jnp.float32)).astype(jnp.bfloat16)


def dot_over_rows(a, b):
    a, b = parts(a), parts(b)
    lhs = jnp.concatenate([a[2], a[0], a[1], a[1], a[0], a[0]], axis=0)
    rhs = jnp.concatenate([b[0], b[2], b[1], b[0], b[1], b[0]], axis=0)
    return lax.dot_general(lhs, rhs, (((0,), (0,)), ((), ())), preferred_element_type=jnp.float32)


def wide(a):
    a = parts(a)
    return jnp.concatenate([a[2], a[0], a[1], a[1], a[0], a[0]], axis=1)


def tall(b):
    b = parts(b)
    return jnp.concatenate([b[0], b[2], b[1], b[0], b[1], b[0]], axis=0)


def times(a, b):
    return jnp.dot(a, b, preferred_element_type=jnp.float32)


def panel_rows(panel, first_ref, rows_ref, rows_other_ref):
    n = rows_ref.shape[-1]
    flat = rows_ref.shape[0] * n
    here = lax.rem(lax.axis_index("col"), 2) == panel
    rest = jnp.where(here, rows_ref[...].reshape(flat, n), rows_other_ref[...].reshape(flat, n))
    return jnp.concatenate([first_ref[panel], rest], axis=0)


def full(row):
    return jnp.broadcast_to(row, (SUB, row.shape[-1]))


def eliminate(s, extra, scratch, beside=()):
    n = s.shape[0]
    groups = n // SUB
    sub = lax.broadcasted_iota(jnp.int32, (SUB, n), 0)
    lane = lax.broadcasted_iota(jnp.int32, (SUB, n), 1)
    rows = lax.broadcasted_iota(jnp.int32, (n, n), 0)
    cols = lax.broadcasted_iota(jnp.int32, (n, n), 1)
    for ref, value in zip(scratch, [s, jnp.where(rows == cols, 1.0, 0.0)] + list(extra)):
        ref[...] = value.reshape(groups, SUB, n)
    sides = range(len(scratch))
    for g in range(groups):
        start = g * SUB
        until = (g // PANEL + 1) * PANEL
        left = until - g
        rest = scratch[0][g:until]
        spread = [jnp.broadcast_to(rest[:, :, start + j:start + j + 1], (left, SUB, n)) for j in range(SUB)]
        unit = {(i, j): full(spread[j][0, i:i + 1, :]) for j in range(SUB) for i in range(j, SUB)}
        row = [[full(ref[g, k:k + 1, :]) for k in range(SUB)] for ref in scratch]
        scaled = [[] for _ in sides]
        tops = [None for _ in sides]
        for k in range(SUB):
            pivot = unit[k, k]
            guess = pl.reciprocal(pivot, approx=True)
            rest_of = 2.0 - pivot * guess
            recip = guess * rest_of
            root = lax.rsqrt(pivot)
            factors = {j: unit[j, k] * recip for j in range(k + 1, SUB)}
            for j in range(k + 1, SUB):
                for i in range(j, SUB):
                    if i == j == k + 1:
                        unit[i, j] = unit[i, j] - (unit[i, k] * unit[j, k] * guess) * rest_of
                    else:
                        unit[i, j] = unit[i, j] - unit[i, k] * factors[j]
            for j in range(k + 1, SUB):
                spread[j] = spread[j] - spread[k] * factors[j][None]
            for m in sides:
                for j in range(k + 1, SUB):
                    row[m][j] = row[m][j] - row[m][k] * factors[j]
                scaled[m].append(row[m][k] * recip)
                final = row[m][k] * root
                tops[m] = final if k == 0 else jnp.where(sub == k, final, tops[m])
        scratch[0][g] = jnp.where(lane >= start + sub, tops[0], 0.0)
        for m in sides[1:]:
            scratch[m][g] = tops[m]
        if left > 1:
            for m in sides:
                low = scratch[m][g + 1:until]
                for k in range(SUB):
                    low = low - spread[k][1:] * scaled[m][k][None]
                scratch[m][g + 1:until] = low
        elif until < groups:
            done = [ref[until - PANEL:until].reshape(PANEL * SUB, n) for ref in scratch]
            update = dot_over_rows(done[0], jnp.concatenate(done, axis=1))
            for m in sides:
                part = update[until * SUB:, m * n:(m + 1) * n]
                scratch[m][until:] = scratch[m][until:] - part.reshape(groups - until, SUB, n)
        if g < len(beside):
            beside[g]()
    upper, *others = [ref[...].reshape(n, n) for ref in scratch]
    return [upper.T] + others


def is_odd_row():
    return lax.rem(lax.axis_index("row"), 2) == 1


def estimate(flops, nbytes):
    return pl.CostEstimate(flops=flops, bytes_accessed=nbytes, transcendentals=0)


def corner_kernel(matrix_ref, block_ref, sem):
    copy = pltpu.make_async_copy(matrix_ref.at[0, :, 0, :], block_ref, sem)
    copy.start()
    copy.wait()


def corner_block(matrix):
    n = matrix.shape[1]
    return pl.pallas_call(
        corner_kernel,
        out_shape=jax.ShapeDtypeStruct((n, n), jnp.float32),
        in_specs=[HBM],
        out_specs=VMEM,
        scratch_shapes=[pltpu.SemaphoreType.DMA(())],
        compiler_params=pltpu.CompilerParams(vmem_limit_bytes=2 * MIB),
        cost_estimate=estimate(0, 3 * MIB),
        name="corner_block",
    )(matrix)


def panels_kernel(matrix_ref, column_ref, upper_ref, lower_ref, sems):
    local_cols, half, _ = upper_ref.shape
    copies = [pltpu.make_async_copy(matrix_ref.at[pl.ds(1, column_ref.shape[0]), :, 0, :], column_ref, sems.at[0])]
    for j in range(local_cols):
        copies.append(pltpu.make_async_copy(matrix_ref.at[0, pl.ds(0, half), j, :], upper_ref.at[j], sems.at[1 + j]))
        copies.append(pltpu.make_async_copy(
            matrix_ref.at[0, pl.ds(half, half), j, :], lower_ref.at[j], sems.at[1 + local_cols + j]))
    for copy in copies:
        copy.start()
    for copy in copies:
        copy.wait()


def panels(matrix):
    local_rows, n, local_cols, _ = matrix.shape
    strip = jax.ShapeDtypeStruct((local_cols, n // 2, n), jnp.float32)
    return pl.pallas_call(
        panels_kernel,
        out_shape=[jax.ShapeDtypeStruct((local_rows - 1, n, n), jnp.float32), strip, strip],
        in_specs=[HBM],
        out_specs=[VMEM] * 3,
        scratch_shapes=[pltpu.SemaphoreType.DMA((1 + 2 * local_cols,))],
        compiler_params=pltpu.CompilerParams(vmem_limit_bytes=4 * MIB),
        cost_estimate=estimate(0, 4 * MIB),
        name="panels",
    )(matrix)


def pack_kernel(across_ref, block_ref, both_ref, message_ref):
    n = block_ref.shape[0]
    odd = is_odd_row()
    right = bit_set(lax.axis_index("col"), 0)
    across, block = across_ref[...], block_ref[...]
    left_block = jnp.where(right, across, block)
    right_block = jnp.where(right, block, across)
    both_ref[0] = left_block
    both_ref[1] = right_block
    message_ref[:n] = jnp.where(odd, right_block, left_block)
    message_ref[n:] = jnp.where(odd, left_block.T[n // 2:], right_block[:n // 2])


def pack(across, block):
    n = block.shape[0]
    return pl.pallas_call(
        pack_kernel,
        out_shape=[jax.ShapeDtypeStruct((2, n, n), jnp.float32), jax.ShapeDtypeStruct((n + n // 2, n), jnp.float32)],
        in_specs=[VMEM] * 2,
        out_specs=[VMEM] * 2,
        compiler_params=pltpu.CompilerParams(vmem_limit_bytes=2 * MIB),
        cost_estimate=estimate(1000, 1000),
        name="pack",
    )(across, block)


def first_factor_kernel(a_ref, side_ref, f_ref, w_ref, cross_ref, *scratch):
    f_ref[...], w_ref[...], cross_ref[...] = eliminate(a_ref[...], [side_ref[...]], scratch)


def elimination_scratch(n, matrices):
    return [pltpu.VMEM((n // SUB, SUB, n), jnp.float32)] * matrices


def first_factor(a, side):
    n = a.shape[1]
    square = jax.ShapeDtypeStruct((n, n), jnp.float32)
    return pl.pallas_call(
        first_factor_kernel,
        out_shape=[square] * 3,
        in_specs=[VMEM] * 2,
        out_specs=[VMEM] * 3,
        scratch_shapes=elimination_scratch(n, 3),
        compiler_params=pltpu.CompilerParams(vmem_limit_bytes=4 * MIB),
        cost_estimate=estimate(8 * 10**9, 2 * MIB),
        name="first_factor",
    )(a, side)


def second_factor_kernel(a_ref, cross_ref, w0_ref, first_ref, rows_ref, rows_other_ref, ha_ref, hb_ref, oa_ref, ob_ref, matrix_ref,
                         f_ref, w_ref, solved_ref, rows_left_ref, top_left_ref, blocks_ref, left, right, sems, *scratch):
    n = w0_ref.shape[0]
    local_cols = matrix_ref.shape[2]
    local_rows = matrix_ref.shape[0]
    copies = [pltpu.make_async_copy(matrix_ref.at[:, :, j, :], blocks_ref.at[j], sems.at[j]) for j in range(local_cols)]
    for copy in copies:
        copy.start()
    odd = is_odd_row()
    w0 = w0_ref[...]
    cross = cross_ref[...]

    def solve_rows():
        solved = times(wide(panel_rows(0, first_ref, rows_ref, rows_other_ref)), tall(w0.T))
        solved_ref[...] = solved
        left[...] = wide(solved)

    def update_rows():
        rows_left_ref[...] = wide(panel_rows(1, first_ref, rows_ref, rows_other_ref) - times(left[...], tall(cross)))

    def top(panel, j):
        here = odd == (panel == 1)
        return jnp.concatenate([
            jnp.concatenate([jnp.where(here, ha_ref[b], oa_ref[b]), jnp.where(here, hb_ref[b], ob_ref[b])], axis=0)
            for b in (j, j + 1)], axis=1)

    def solve_top(j):
        def step():
            right[...] = tall(times(wide(w0), tall(top(0, j))))
            top_left_ref[:, j * n:(j + 2) * n] = tall(top(1, j) - times(wide(cross.T), right[...]))
        return step

    def update(j, i):
        def step():
            if i == 0:
                copies[j].wait()
                copies[j + 1].wait()
            change = times(left[i * n:(i + 2) * n], right[...])
            for b in range(2):
                part = change[:, b * n:(b + 1) * n].reshape(2, n, n)
                blocks_ref[j + b, i:i + 2] = blocks_ref[j + b, i:i + 2] - part
        return step

    steps = [solve_rows, update_rows]
    for j in range(0, local_cols, 2):
        steps.append(solve_top(j))
        steps.extend(update(j, i) for i in range(0, local_rows, 2))

    groups = n // SUB
    each = -(-len(steps) // groups)

    def several(some):
        def run():
            for step in some:
                step()
        return run

    beside = [several(steps[at:at + each]) for at in range(0, len(steps), each)]
    f_ref[...], w_ref[...] = eliminate(a_ref[...] - dot_over_rows(cross, cross), [], scratch, beside)


def second_factor(a, cross, w0, first_rows, rows, rows_other, ha, hb, oa, ob, matrix):
    local_rows, n, local_cols, _ = matrix.shape
    square = jax.ShapeDtypeStruct((n, n), jnp.float32)
    solved = jax.ShapeDtypeStruct((local_rows * n, n), jnp.float32)
    rows_left = jax.ShapeDtypeStruct((local_rows * n, 6 * n), jnp.bfloat16)
    top_left = jax.ShapeDtypeStruct((6 * n, local_cols * n), jnp.bfloat16)
    blocks = jax.ShapeDtypeStruct((local_cols, local_rows, n, n), jnp.float32)
    return pl.pallas_call(
        second_factor_kernel,
        out_shape=[square, square, solved, rows_left, top_left, blocks],
        in_specs=[VMEM] * 10 + [HBM],
        out_specs=[VMEM] * 6,
        scratch_shapes=[
            pltpu.VMEM((local_rows * n, 6 * n), jnp.bfloat16),
            pltpu.VMEM((6 * n, 2 * n), jnp.bfloat16),
            pltpu.SemaphoreType.DMA((local_cols,)),
        ] + elimination_scratch(n, 2),
        compiler_params=pltpu.CompilerParams(vmem_limit_bytes=20 * MIB),
        cost_estimate=estimate(8 * 10**9, 4 * MIB),
        name="second_factor",
    )(a, cross, w0, first_rows, rows, rows_other, ha, hb, oa, ob, matrix)


def settle_kernel(f0_ref, f1_ref, w_ref, solved_ref, rows_left_ref, top_left_ref, blocks_ref, out_ref, result, sems):
    grid_row = lax.axis_index("row")
    grid_col = lax.axis_index("col")
    n = f0_ref.shape[0]
    local_cols, local_rows, _, _ = blocks_ref.shape
    w1 = w_ref[...]
    solved = times(rows_left_ref[...], tall(w1.T))
    left = wide(solved)
    inverse = wide(w1)

    def solve_top(j):
        return tall(times(inverse, top_left_ref[:, j * n:(j + 2) * n]))

    copies = []
    top = solve_top(0)
    for j in range(0, local_cols, 2):
        now = top
        if j + 2 < local_cols:
            top = solve_top(j + 2)
        update = times(left, now)
        for b in (j, j + 1):
            value = blocks_ref[b] - update[:, (b - j) * n:(b - j + 1) * n].reshape(local_rows, n, n)
            zero = jnp.zeros((n, n), jnp.float32)
            if b == 0:
                value = jnp.where(grid_col == 0, solved_ref[...].reshape(local_rows, n, n), value)
                value = jnp.where(grid_col == 1, solved.reshape(local_rows, n, n), value)
                head = jnp.where((grid_row <= 1) & (grid_col > grid_row), zero, value[0])
                head = jnp.where((grid_row == 0) & (grid_col == 0), f0_ref[...], head)
                head = jnp.where((grid_row == 1) & (grid_col == 1), f1_ref[...], head)
            else:
                head = jnp.where(grid_row <= 1, zero, value[0])
            result[b, 0] = head
            result[b, 1:] = value[1:]
            copy = pltpu.make_async_copy(result.at[b], out_ref.at[:, :, b, :], sems.at[b])
            copy.start()
            copies.append(copy)
    for copy in copies:
        copy.wait()


def settle(f0, f1, w1, solved, rows_left, top_left, blocks):
    local_cols, local_rows, n, _ = blocks.shape
    return pl.pallas_call(
        settle_kernel,
        out_shape=jax.ShapeDtypeStruct((local_rows, n, local_cols, n), jnp.float32),
        in_specs=[VMEM] * 7,
        out_specs=HBM,
        scratch_shapes=[pltpu.VMEM(blocks.shape, jnp.float32), pltpu.SemaphoreType.DMA((local_cols,))],
        compiler_params=pltpu.CompilerParams(vmem_limit_bytes=32 * MIB),
        cost_estimate=estimate(4 * 10**9, 6 * MIB),
        name="settle",
    )(f0, f1, w1, solved, rows_left, top_left, blocks)


def exchange(value, axis, mask, size):
    return lax.ppermute(value, axis, [(i, i ^ mask) for i in range(size)])


def bit_set(index, bit):
    return ((index >> bit) & 1) == 1


def spread(own, axis, index, size, bits):
    held = own
    for bit in bits:
        held = jnp.where(bit_set(index, bit), exchange(held, axis, 1 << bit, size), held)
    return held


def region(run, *values):
    shapes = jax.eval_shape(run, *values)

    def skip(*_):
        return jax.tree.map(lambda leaf: jnp.zeros(leaf.shape, leaf.dtype), shapes)

    everywhere = lax.axis_index("row") < lax.axis_size("row")
    return lax.cond(everywhere, run, skip, *values)


def after(value, *others):
    return lax.optimization_barrier((value,) + others)


def shards(kernel):
    grid_row = lax.axis_index("row")
    grid_col = lax.axis_index("col")
    n_row = lax.axis_size("row")
    n_col = lax.axis_size("col")
    row_bits = list(range(1, n_row.bit_length() - 1))
    col_bits = list(range(1, n_col.bit_length() - 1))
    odd = (grid_row % 2) == 1

    block = corner_block(kernel)
    column, upper, lower = panels(kernel)
    first_bit, last_bit = row_bits[0], row_bits[-1]

    moved = exchange(block, "col", 1 << col_bits[0], n_col)
    upper_moved = exchange(upper, "row", 1 << first_bit, n_row)
    lower_moved = exchange(lower, "row", 1 << last_bit, n_row)

    def along_col(new, old):
        block = jnp.where(bit_set(grid_col, col_bits[0]), new, old)
        return spread(block, "col", grid_col, n_col, col_bits[1:])

    block = region(along_col, moved, block)
    across = exchange(block, "col", 1, n_col)
    ha = jnp.where(bit_set(grid_row, first_bit), upper_moved, upper)
    hb = jnp.where(bit_set(grid_row, last_bit), lower_moved, lower)
    across, block, ha, hb, column = after(across, block, ha, hb, column)

    first_rows, pair = pack(across, block)
    moved = exchange(pair, "row", 1 << first_bit, n_row)
    column_moved = exchange(column, "col", 1 << col_bits[0], n_col)
    pair = jnp.where(bit_set(grid_row, first_bit), moved, pair)
    pair, ha, hb = after(pair, ha, hb)
    moved = exchange(pair, "row", 1 << row_bits[1], n_row)
    ha_moved = exchange(ha, "row", 1 << row_bits[1], n_row)
    hb_moved = exchange(hb, "row", 1 << row_bits[-2], n_row)
    rows = jnp.where(bit_set(grid_col, col_bits[0]), column_moved, column)
    moved, pair, rows = after(moved, pair, rows)
    pair = jnp.where(bit_set(grid_row, row_bits[1]), moved, pair)
    pair = spread(pair, "row", grid_row, n_row, row_bits[2:])
    other = exchange(pair, "row", 1, n_row)
    ha = jnp.where(bit_set(grid_row, row_bits[1]), ha_moved, ha)
    hb = jnp.where(bit_set(grid_row, row_bits[-2]), hb_moved, hb)
    ha = spread(ha, "row", grid_row, n_row, row_bits[2:])
    hb = spread(hb, "row", grid_row, n_row, row_bits[:-2][::-1])
    other, pair, ha, hb = after(other, pair, ha, hb)
    oa = exchange(ha, "row", 1, n_row)
    ob = exchange(hb, "row", 1, n_row)

    n = block.shape[0]
    a00 = jnp.where(odd, other[:n], pair[:n])
    a11 = jnp.where(odd, pair[:n], other[:n])
    a01 = jnp.concatenate([jnp.where(odd, other[n:], pair[n:]), jnp.where(odd, pair[n:], other[n:])], axis=0)
    f0, w0, cross = first_factor(a00, a01)

    rows = spread(rows, "col", grid_col, n_col, col_bits[1:])
    rows_other = exchange(rows, "col", 1, n_col)
    f1, w1, solved, rows_left, top_left, blocks = second_factor(
        a11, cross, w0, first_rows, rows, rows_other, ha, hb, oa, ob, kernel)
    return settle(f0, f1, w1, solved, rows_left, top_left, blocks)


def solution(mesh):
    in_specs = (P(None, "row", None, "col"),)
    out_specs = P(None, "row", None, "col")
    return jax.shard_map(shards, mesh=mesh, in_specs=in_specs, out_specs=out_specs, check_vma=False)
```

```python
import functools

import jax
import jax.numpy as jnp
from jax import lax
from jax.experimental import pallas as pl
from jax.experimental.pallas import tpu as pltpu
from jax.sharding import PartitionSpec as P

SUB = 8
PANEL = 4
MIB = 1024 * 1024
VMEM = pl.BlockSpec(memory_space=pltpu.VMEM)
HBM = pl.BlockSpec(memory_space=pltpu.HBM)


def parts(x):
    high = x.astype(jnp.bfloat16)
    rest = x - high.astype(jnp.float32)
    middle = rest.astype(jnp.bfloat16)
    return high, middle, (rest - middle.astype(jnp.float32)).astype(jnp.bfloat16)


def dot_over_rows(a, b):
    a, b = parts(a), parts(b)
    lhs = jnp.concatenate([a[2], a[0], a[1], a[1], a[0], a[0]], axis=0)
    rhs = jnp.concatenate([b[0], b[2], b[1], b[0], b[1], b[0]], axis=0)
    return lax.dot_general(lhs, rhs, (((0,), (0,)), ((), ())), preferred_element_type=jnp.float32)


def wide(a):
    a = parts(a)
    return jnp.concatenate([a[2], a[0], a[1], a[1], a[0], a[0]], axis=1)


def tall(b):
    b = parts(b)
    return jnp.concatenate([b[0], b[2], b[1], b[0], b[1], b[0]], axis=0)


def times(a, b):
    return jnp.dot(a, b, preferred_element_type=jnp.float32)


def panel_rows(panel, first_ref, rows_ref, rows_other_ref):
    n = rows_ref.shape[-1]
    flat = rows_ref.shape[0] * n
    here = lax.rem(lax.axis_index("col"), 2) == panel
    rest = jnp.where(here, rows_ref[...].reshape(flat, n), rows_other_ref[...].reshape(flat, n))
    return jnp.concatenate([first_ref[panel], rest], axis=0)


def full(row):
    return jnp.broadcast_to(row, (SUB, row.shape[-1]))


def eliminate(s, extra, scratch, beside=()):
    n = s.shape[0]
    groups = n // SUB
    sub = lax.broadcasted_iota(jnp.int32, (SUB, n), 0)
    lane = lax.broadcasted_iota(jnp.int32, (SUB, n), 1)
    rows = lax.broadcasted_iota(jnp.int32, (n, n), 0)
    cols = lax.broadcasted_iota(jnp.int32, (n, n), 1)
    for ref, value in zip(scratch, [s, jnp.where(rows == cols, 1.0, 0.0)] + list(extra)):
        ref[...] = value.reshape(groups, SUB, n)
    sides = range(len(scratch))
    for g in range(groups):
        start = g * SUB
        until = (g // PANEL + 1) * PANEL
        left = until - g
        rest = scratch[0][g:until]
        spread = [jnp.broadcast_to(rest[:, :, start + j:start + j + 1], (left, SUB, n)) for j in range(SUB)]
        unit = {(i, j): full(spread[j][0, i:i + 1, :]) for j in range(SUB) for i in range(j, SUB)}
        row = [[full(ref[g, k:k + 1, :]) for k in range(SUB)] for ref in scratch]
        scaled = [[] for _ in sides]
        tops = [None for _ in sides]
        for k in range(SUB):
            pivot = unit[k, k]
            guess = pl.reciprocal(pivot, approx=True)
            rest_of = 2.0 - pivot * guess
            recip = guess * rest_of
            root = lax.rsqrt(pivot)
            factors = {j: unit[j, k] * recip for j in range(k + 1, SUB)}
            for j in range(k + 1, SUB):
                for i in range(j, SUB):
                    if i == j == k + 1:
                        unit[i, j] = unit[i, j] - (unit[i, k] * unit[j, k] * guess) * rest_of
                    else:
                        unit[i, j] = unit[i, j] - unit[i, k] * factors[j]
            for j in range(k + 1, SUB):
                spread[j] = spread[j] - spread[k] * factors[j][None]
            for m in sides:
                for j in range(k + 1, SUB):
                    row[m][j] = row[m][j] - row[m][k] * factors[j]
                scaled[m].append(row[m][k] * recip)
                final = row[m][k] * root
                tops[m] = final if k == 0 else jnp.where(sub == k, final, tops[m])
        scratch[0][g] = jnp.where(lane >= start + sub, tops[0], 0.0)
        for m in sides[1:]:
            scratch[m][g] = tops[m]
        if left > 1:
            for m in sides:
                low = scratch[m][g + 1:until]
                for k in range(SUB):
                    low = low - spread[k][1:] * scaled[m][k][None]
                scratch[m][g + 1:until] = low
        elif until < groups:
            done = [ref[until - PANEL:until].reshape(PANEL * SUB, n) for ref in scratch]
            update = dot_over_rows(done[0], jnp.concatenate(done, axis=1))
            for m in sides:
                part = update[until * SUB:, m * n:(m + 1) * n]
                scratch[m][until:] = scratch[m][until:] - part.reshape(groups - until, SUB, n)
        if g < len(beside):
            beside[g]()
    upper, *others = [ref[...].reshape(n, n) for ref in scratch]
    return [upper.T] + others


def is_odd_row():
    return lax.rem(lax.axis_index("row"), 2) == 1


def estimate(flops, nbytes):
    return pl.CostEstimate(flops=flops, bytes_accessed=nbytes, transcendentals=0)


def panels_kernel(matrix_ref, block_ref, column_ref, upper_ref, lower_ref, sems):
    local_cols, half, _ = upper_ref.shape
    copies = [
        pltpu.make_async_copy(matrix_ref.at[0, :, 0, :], block_ref, sems.at[2 * local_cols + 1]),
        pltpu.make_async_copy(matrix_ref.at[pl.ds(1, column_ref.shape[0]), :, 0, :], column_ref, sems.at[0])]
    for j in range(local_cols):
        copies.append(pltpu.make_async_copy(matrix_ref.at[0, pl.ds(0, half), j, :], upper_ref.at[j], sems.at[1 + j]))
        copies.append(pltpu.make_async_copy(
            matrix_ref.at[0, pl.ds(half, half), j, :], lower_ref.at[j], sems.at[1 + local_cols + j]))
    for copy in copies:
        copy.start()
    for copy in copies:
        copy.wait()


def panels(matrix):
    local_rows, n, local_cols, _ = matrix.shape
    strip = jax.ShapeDtypeStruct((local_cols, n // 2, n), jnp.float32)
    return pl.pallas_call(
        panels_kernel,
        out_shape=[
            jax.ShapeDtypeStruct((n, n), jnp.float32), jax.ShapeDtypeStruct((local_rows - 1, n, n), jnp.float32), strip, strip],
        in_specs=[HBM],
        out_specs=[VMEM] * 4,
        scratch_shapes=[pltpu.SemaphoreType.DMA((2 + 2 * local_cols,))],
        compiler_params=pltpu.CompilerParams(vmem_limit_bytes=4 * MIB),
        cost_estimate=estimate(0, 4 * MIB),
        name="panels",
    )(matrix)


def pick_kernel(bit, new_ref, old_ref, out_ref):
    out_ref[...] = jnp.where(bit_set(lax.axis_index("col"), bit), new_ref[...], old_ref[...])


def pick(new, old, bit):
    return pl.pallas_call(
        functools.partial(pick_kernel, bit),
        out_shape=jax.ShapeDtypeStruct(old.shape, old.dtype),
        in_specs=[VMEM] * 2,
        out_specs=VMEM,
        compiler_params=pltpu.CompilerParams(vmem_limit_bytes=2 * MIB),
        cost_estimate=estimate(8 * 10**9, 2 * MIB),
        name="pick",
    )(new, old)


def pack_kernel(across_ref, block_ref, both_ref, message_ref):
    n = block_ref.shape[0]
    odd = is_odd_row()
    right = bit_set(lax.axis_index("col"), 0)
    across, block = across_ref[...], block_ref[...]
    left_block = jnp.where(right, across, block)
    right_block = jnp.where(right, block, across)
    both_ref[0] = left_block
    both_ref[1] = right_block
    message_ref[:n] = jnp.where(odd, right_block, left_block)
    message_ref[n:] = jnp.where(odd, left_block.T[n // 2:], right_block[:n // 2])


def pack(across, block):
    n = block.shape[0]
    return pl.pallas_call(
        pack_kernel,
        out_shape=[jax.ShapeDtypeStruct((2, n, n), jnp.float32), jax.ShapeDtypeStruct((n + n // 2, n), jnp.float32)],
        in_specs=[VMEM] * 2,
        out_specs=[VMEM] * 2,
        compiler_params=pltpu.CompilerParams(vmem_limit_bytes=2 * MIB),
        cost_estimate=estimate(1000, 1000),
        name="pack",
    )(across, block)


def first_factor_kernel(a_ref, side_ref, f_ref, w_ref, cross_ref, *scratch):
    f_ref[...], w_ref[...], cross_ref[...] = eliminate(a_ref[...], [side_ref[...]], scratch)


def elimination_scratch(n, matrices):
    return [pltpu.VMEM((n // SUB, SUB, n), jnp.float32)] * matrices


def first_factor(a, side):
    n = a.shape[1]
    square = jax.ShapeDtypeStruct((n, n), jnp.float32)
    return pl.pallas_call(
        first_factor_kernel,
        out_shape=[square] * 3,
        in_specs=[VMEM] * 2,
        out_specs=[VMEM] * 3,
        scratch_shapes=elimination_scratch(n, 3),
        compiler_params=pltpu.CompilerParams(vmem_limit_bytes=4 * MIB),
        cost_estimate=estimate(8 * 10**9, 2 * MIB),
        name="first_factor",
    )(a, side)


def second_factor_kernel(a_ref, cross_ref, w0_ref, first_ref, rows_ref, rows_other_ref, ha_ref, hb_ref, oa_ref, ob_ref, matrix_ref,
                         f_ref, w_ref, solved_ref, rows_left_ref, top_left_ref, blocks_ref, left, right, sems, *scratch):
    n = w0_ref.shape[0]
    local_cols = matrix_ref.shape[2]
    local_rows = matrix_ref.shape[0]
    copies = [pltpu.make_async_copy(matrix_ref.at[:, :, j, :], blocks_ref.at[j], sems.at[j]) for j in range(local_cols)]
    for copy in copies:
        copy.start()
    odd = is_odd_row()
    w0 = w0_ref[...]
    cross = cross_ref[...]

    def solve_rows():
        solved = times(wide(panel_rows(0, first_ref, rows_ref, rows_other_ref)), tall(w0.T))
        solved_ref[...] = solved
        left[...] = wide(solved)

    def update_rows():
        rows_left_ref[...] = wide(panel_rows(1, first_ref, rows_ref, rows_other_ref) - times(left[...], tall(cross)))

    def top(panel, j):
        here = odd == (panel == 1)
        return jnp.concatenate([
            jnp.concatenate([jnp.where(here, ha_ref[b], oa_ref[b]), jnp.where(here, hb_ref[b], ob_ref[b])], axis=0)
            for b in (j, j + 1)], axis=1)

    def solve_top(j):
        def step():
            solved = tall(times(wide(w0), tall(top(0, j))))
            right[:, j * n:(j + 2) * n] = solved
            top_left_ref[:, j * n:(j + 2) * n] = tall(top(1, j) - times(wide(cross.T), solved))
        return step

    def update(j, i):
        def step():
            if i == 0 and j == 0:
                for copy in copies:
                    copy.wait()
            change = times(left[i * n:(i + 2) * n], right[:, j * n:(j + 2) * n])
            for b in range(2):
                part = change[:, b * n:(b + 1) * n].reshape(2, n, n)
                blocks_ref[j + b, i:i + 2] = blocks_ref[j + b, i:i + 2] - part
        return step

    steps = [solve_rows, update_rows]
    steps.extend(solve_top(j) for j in range(0, local_cols, 2))
    steps.extend(update(j, i) for j in range(0, local_cols, 2) for i in range(0, local_rows, 2))

    groups = n // SUB
    each = -(-len(steps) // groups)

    def several(some):
        def run():
            for step in some:
                step()
        return run

    beside = [several(steps[at:at + each]) for at in range(0, len(steps), each)]
    f_ref[...], w_ref[...] = eliminate(a_ref[...] - dot_over_rows(cross, cross), [], scratch, beside)


def second_factor(a, cross, w0, first_rows, rows, rows_other, ha, hb, oa, ob, matrix):
    local_rows, n, local_cols, _ = matrix.shape
    square = jax.ShapeDtypeStruct((n, n), jnp.float32)
    solved = jax.ShapeDtypeStruct((local_rows * n, n), jnp.float32)
    rows_left = jax.ShapeDtypeStruct((local_rows * n, 6 * n), jnp.bfloat16)
    top_left = jax.ShapeDtypeStruct((6 * n, local_cols * n), jnp.bfloat16)
    blocks = jax.ShapeDtypeStruct((local_cols, local_rows, n, n), jnp.float32)
    return pl.pallas_call(
        second_factor_kernel,
        out_shape=[square, square, solved, rows_left, top_left, blocks],
        in_specs=[VMEM] * 10 + [HBM],
        out_specs=[VMEM] * 6,
        scratch_shapes=[
            pltpu.VMEM((local_rows * n, 6 * n), jnp.bfloat16),
            pltpu.VMEM((6 * n, local_cols * n), jnp.bfloat16),
            pltpu.SemaphoreType.DMA((local_cols,)),
        ] + elimination_scratch(n, 2),
        compiler_params=pltpu.CompilerParams(vmem_limit_bytes=20 * MIB),
        cost_estimate=estimate(8 * 10**9, 4 * MIB),
        name="second_factor",
    )(a, cross, w0, first_rows, rows, rows_other, ha, hb, oa, ob, matrix)


def settle_kernel(f0_ref, f1_ref, w_ref, solved_ref, rows_left_ref, top_left_ref, blocks_ref, out_ref, result, sems):
    grid_row = lax.axis_index("row")
    grid_col = lax.axis_index("col")
    n = f0_ref.shape[0]
    local_cols, local_rows, _, _ = blocks_ref.shape
    w1 = w_ref[...]
    solved = times(rows_left_ref[...], tall(w1.T))
    left = wide(solved)
    inverse = wide(w1)

    def solve_top(j):
        return tall(times(inverse, top_left_ref[:, j * n:(j + 2) * n]))

    copies = []
    top = solve_top(0)
    for j in range(0, local_cols, 2):
        now = top
        if j + 2 < local_cols:
            top = solve_top(j + 2)
        update = times(left, now)
        for b in (j, j + 1):
            value = blocks_ref[b] - update[:, (b - j) * n:(b - j + 1) * n].reshape(local_rows, n, n)
            zero = jnp.zeros((n, n), jnp.float32)
            if b == 0:
                value = jnp.where(grid_col == 0, solved_ref[...].reshape(local_rows, n, n), value)
                value = jnp.where(grid_col == 1, solved.reshape(local_rows, n, n), value)
                head = jnp.where((grid_row <= 1) & (grid_col > grid_row), zero, value[0])
                head = jnp.where((grid_row == 0) & (grid_col == 0), f0_ref[...], head)
                head = jnp.where((grid_row == 1) & (grid_col == 1), f1_ref[...], head)
            else:
                head = jnp.where(grid_row <= 1, zero, value[0])
            result[b, 0] = head
            result[b, 1:] = value[1:]
            copy = pltpu.make_async_copy(result.at[b], out_ref.at[:, :, b, :], sems.at[b])
            copy.start()
            copies.append(copy)
    for copy in copies:
        copy.wait()


def settle(f0, f1, w1, solved, rows_left, top_left, blocks):
    local_cols, local_rows, n, _ = blocks.shape
    return pl.pallas_call(
        settle_kernel,
        out_shape=jax.ShapeDtypeStruct((local_rows, n, local_cols, n), jnp.float32),
        in_specs=[VMEM] * 7,
        out_specs=HBM,
        scratch_shapes=[pltpu.VMEM(blocks.shape, jnp.float32), pltpu.SemaphoreType.DMA((local_cols,))],
        compiler_params=pltpu.CompilerParams(vmem_limit_bytes=32 * MIB),
        cost_estimate=estimate(4 * 10**9, 6 * MIB),
        name="settle",
    )(f0, f1, w1, solved, rows_left, top_left, blocks)


def exchange(value, axis, mask, size):
    return lax.ppermute(value, axis, [(i, i ^ mask) for i in range(size)])


def bit_set(index, bit):
    return ((index >> bit) & 1) == 1


def spread(own, axis, index, size, bits):
    held = own
    for bit in bits:
        held = jnp.where(bit_set(index, bit), exchange(held, axis, 1 << bit, size), held)
    return held


def after(value, *others):
    return lax.optimization_barrier((value,) + others)


def shards(kernel):
    grid_row = lax.axis_index("row")
    grid_col = lax.axis_index("col")
    n_row = lax.axis_size("row")
    n_col = lax.axis_size("col")
    row_bits = list(range(1, n_row.bit_length() - 1))
    col_bits = list(range(1, n_col.bit_length() - 1))
    odd = (grid_row % 2) == 1

    block, column, upper, lower = panels(kernel)
    first_bit, last_bit = row_bits[0], row_bits[-1]

    moved = exchange(block, "col", 1 << col_bits[0], n_col)
    upper_moved = exchange(upper, "row", 1 << first_bit, n_row)
    lower_moved = exchange(lower, "row", 1 << last_bit, n_row)

    block = pick(moved, block, col_bits[0])
    block = spread(block, "col", grid_col, n_col, col_bits[1:])
    across = exchange(block, "col", 1, n_col)
    ha = jnp.where(bit_set(grid_row, first_bit), upper_moved, upper)
    hb = jnp.where(bit_set(grid_row, last_bit), lower_moved, lower)
    across, block, ha, hb, column = after(across, block, ha, hb, column)

    first_rows, pair = pack(across, block)
    moved = exchange(pair, "row", 1 << first_bit, n_row)
    column_moved = exchange(column, "col", 1 << col_bits[0], n_col)
    pair = jnp.where(bit_set(grid_row, first_bit), moved, pair)
    pair, ha, hb = after(pair, ha, hb)
    moved = exchange(pair, "row", 1 << row_bits[1], n_row)
    ha_moved = exchange(ha, "row", 1 << row_bits[1], n_row)
    hb_moved = exchange(hb, "row", 1 << row_bits[-2], n_row)
    rows = jnp.where(bit_set(grid_col, col_bits[0]), column_moved, column)
    moved, pair, rows = after(moved, pair, rows)
    pair = jnp.where(bit_set(grid_row, row_bits[1]), moved, pair)
    pair = spread(pair, "row", grid_row, n_row, row_bits[2:])
    other = exchange(pair, "row", 1, n_row)
    ha = jnp.where(bit_set(grid_row, row_bits[1]), ha_moved, ha)
    hb = jnp.where(bit_set(grid_row, row_bits[-2]), hb_moved, hb)
    ha = spread(ha, "row", grid_row, n_row, row_bits[2:])
    hb = spread(hb, "row", grid_row, n_row, row_bits[:-2][::-1])
    other, pair, ha, hb = after(other, pair, ha, hb)
    oa = exchange(ha, "row", 1, n_row)
    ob = exchange(hb, "row", 1, n_row)

    n = block.shape[0]
    a00 = jnp.where(odd, other[:n], pair[:n])
    a11 = jnp.where(odd, pair[:n], other[:n])
    a01 = jnp.concatenate([jnp.where(odd, other[n:], pair[n:]), jnp.where(odd, pair[n:], other[n:])], axis=0)
    f0, w0, cross = first_factor(a00, a01)

    rows = spread(rows, "col", grid_col, n_col, col_bits[1:])
    rows_other = exchange(rows, "col", 1, n_col)
    f1, w1, solved, rows_left, top_left, blocks = second_factor(
        a11, cross, w0, first_rows, rows, rows_other, ha, hb, oa, ob, kernel)
    return settle(f0, f1, w1, solved, rows_left, top_left, blocks)


def solution(mesh):
    in_specs = (P(None, "row", None, "col"),)
    out_specs = P(None, "row", None, "col")
    return jax.shard_map(shards, mesh=mesh, in_specs=in_specs, out_specs=out_specs, check_vma=False)
```

```python
import functools

import jax
import jax.numpy as jnp
from jax import lax
from jax.experimental import pallas as pl
from jax.experimental.pallas import tpu as pltpu
from jax.sharding import PartitionSpec as P

SUB = 8
PANEL = 4
MIB = 1024 * 1024
VMEM = pl.BlockSpec(memory_space=pltpu.VMEM)
HBM = pl.BlockSpec(memory_space=pltpu.HBM)


def parts(x):
    high = x.astype(jnp.bfloat16)
    rest = x - high.astype(jnp.float32)
    middle = rest.astype(jnp.bfloat16)
    return high, middle, (rest - middle.astype(jnp.float32)).astype(jnp.bfloat16)


def dot_over_rows(a, b):
    a, b = parts(a), parts(b)
    lhs = jnp.concatenate([a[2], a[0], a[1], a[1], a[0], a[0]], axis=0)
    rhs = jnp.concatenate([b[0], b[2], b[1], b[0], b[1], b[0]], axis=0)
    return lax.dot_general(lhs, rhs, (((0,), (0,)), ((), ())), preferred_element_type=jnp.float32)


def wide(a):
    a = parts(a)
    return jnp.concatenate([a[2], a[0], a[1], a[1], a[0], a[0]], axis=1)


def tall(b):
    b = parts(b)
    return jnp.concatenate([b[0], b[2], b[1], b[0], b[1], b[0]], axis=0)


def times(a, b):
    return jnp.dot(a, b, preferred_element_type=jnp.float32)


def panel_rows(panel, first_ref, rows_ref, rows_other_ref):
    n = rows_ref.shape[-1]
    flat = rows_ref.shape[0] * n
    here = lax.rem(lax.axis_index("col"), 2) == panel
    rest = jnp.where(here, rows_ref[...].reshape(flat, n), rows_other_ref[...].reshape(flat, n))
    return jnp.concatenate([first_ref[panel], rest], axis=0)


def full(row):
    return jnp.broadcast_to(row, (SUB, row.shape[-1]))


def eliminate(s, extra, scratch, beside=()):
    n = s.shape[0]
    groups = n // SUB
    sub = lax.broadcasted_iota(jnp.int32, (SUB, n), 0)
    lane = lax.broadcasted_iota(jnp.int32, (SUB, n), 1)
    rows = lax.broadcasted_iota(jnp.int32, (n, n), 0)
    cols = lax.broadcasted_iota(jnp.int32, (n, n), 1)
    for ref, value in zip(scratch, [s, jnp.where(rows == cols, 1.0, 0.0)] + list(extra)):
        ref[...] = value.reshape(groups, SUB, n)
    sides = range(len(scratch))
    for g in range(groups):
        start = g * SUB
        until = (g // PANEL + 1) * PANEL
        left = until - g
        rest = scratch[0][g:until]
        spread = [jnp.broadcast_to(rest[:, :, start + j:start + j + 1], (left, SUB, n)) for j in range(SUB)]
        unit = {(i, j): full(spread[j][0, i:i + 1, :]) for j in range(SUB) for i in range(j, SUB)}
        row = [[full(ref[g, k:k + 1, :]) for k in range(SUB)] for ref in scratch]
        scaled = [[] for _ in sides]
        tops = [None for _ in sides]
        for k in range(SUB):
            pivot = unit[k, k]
            guess = pl.reciprocal(pivot, approx=True)
            rest_of = 2.0 - pivot * guess
            recip = guess * rest_of
            root = lax.rsqrt(pivot)
            factors = {j: unit[j, k] * recip for j in range(k + 1, SUB)}
            for j in range(k + 1, SUB):
                for i in range(j, SUB):
                    if i == j == k + 1:
                        unit[i, j] = unit[i, j] - (unit[i, k] * unit[j, k] * guess) * rest_of
                    else:
                        unit[i, j] = unit[i, j] - unit[i, k] * factors[j]
            for j in range(k + 1, SUB):
                spread[j] = spread[j] - spread[k] * factors[j][None]
            for m in sides:
                for j in range(k + 1, SUB):
                    row[m][j] = row[m][j] - row[m][k] * factors[j]
                scaled[m].append(row[m][k] * recip)
                final = row[m][k] * root
                tops[m] = final if k == 0 else jnp.where(sub == k, final, tops[m])
        scratch[0][g] = jnp.where(lane >= start + sub, tops[0], 0.0)
        for m in sides[1:]:
            scratch[m][g] = tops[m]
        if left > 1:
            for m in sides:
                low = scratch[m][g + 1:until]
                for k in range(SUB):
                    low = low - spread[k][1:] * scaled[m][k][None]
                scratch[m][g + 1:until] = low
        elif until < groups:
            done = [ref[until - PANEL:until].reshape(PANEL * SUB, n) for ref in scratch]
            update = dot_over_rows(done[0], jnp.concatenate(done, axis=1))
            for m in sides:
                part = update[until * SUB:, m * n:(m + 1) * n]
                scratch[m][until:] = scratch[m][until:] - part.reshape(groups - until, SUB, n)
        if g < len(beside):
            beside[g]()
    upper, *others = [ref[...].reshape(n, n) for ref in scratch]
    return [upper.T] + others


def is_odd_row():
    return lax.rem(lax.axis_index("row"), 2) == 1


def estimate(flops, nbytes):
    return pl.CostEstimate(flops=flops, bytes_accessed=nbytes, transcendentals=0)


def panels_kernel(matrix_ref, block_ref, column_ref, upper_ref, lower_ref, sems):
    local_cols, half, _ = upper_ref.shape
    copies = [
        pltpu.make_async_copy(matrix_ref.at[0, :, 0, :], block_ref, sems.at[2 * local_cols + 1]),
        pltpu.make_async_copy(matrix_ref.at[pl.ds(1, column_ref.shape[0]), :, 0, :], column_ref, sems.at[0])]
    for j in range(local_cols):
        copies.append(pltpu.make_async_copy(matrix_ref.at[0, pl.ds(0, half), j, :], upper_ref.at[j], sems.at[1 + j]))
        copies.append(pltpu.make_async_copy(
            matrix_ref.at[0, pl.ds(half, half), j, :], lower_ref.at[j], sems.at[1 + local_cols + j]))
    for copy in copies:
        copy.start()
    for copy in copies:
        copy.wait()


def panels(matrix):
    local_rows, n, local_cols, _ = matrix.shape
    strip = jax.ShapeDtypeStruct((local_cols, n // 2, n), jnp.float32)
    return pl.pallas_call(
        panels_kernel,
        out_shape=[
            jax.ShapeDtypeStruct((n, n), jnp.float32), jax.ShapeDtypeStruct((local_rows - 1, n, n), jnp.float32), strip, strip],
        in_specs=[HBM],
        out_specs=[VMEM] * 4,
        scratch_shapes=[pltpu.SemaphoreType.DMA((2 + 2 * local_cols,))],
        compiler_params=pltpu.CompilerParams(vmem_limit_bytes=4 * MIB),
        cost_estimate=estimate(0, 4 * MIB),
        name="panels",
    )(matrix)


def pick_kernel(bit, new_ref, old_ref, out_ref):
    out_ref[...] = jnp.where(bit_set(lax.axis_index("col"), bit), new_ref[...], old_ref[...])


def pick(new, old, bit):
    return pl.pallas_call(
        functools.partial(pick_kernel, bit),
        out_shape=jax.ShapeDtypeStruct(old.shape, old.dtype),
        in_specs=[VMEM] * 2,
        out_specs=VMEM,
        compiler_params=pltpu.CompilerParams(vmem_limit_bytes=2 * MIB),
        cost_estimate=estimate(8 * 10**9, 2 * MIB),
        name="pick",
    )(new, old)


def pack_kernel(across_ref, block_ref, both_ref, message_ref):
    n = block_ref.shape[0]
    odd = is_odd_row()
    right = bit_set(lax.axis_index("col"), 0)
    across, block = across_ref[...], block_ref[...]
    left_block = jnp.where(right, across, block)
    right_block = jnp.where(right, block, across)
    both_ref[0] = left_block
    both_ref[1] = right_block
    message_ref[:n] = jnp.where(odd, right_block, left_block)
    message_ref[n:] = jnp.where(odd, left_block.T[n // 2:], right_block[:n // 2])


def pack(across, block):
    n = block.shape[0]
    return pl.pallas_call(
        pack_kernel,
        out_shape=[jax.ShapeDtypeStruct((2, n, n), jnp.float32), jax.ShapeDtypeStruct((n + n // 2, n), jnp.float32)],
        in_specs=[VMEM] * 2,
        out_specs=[VMEM] * 2,
        compiler_params=pltpu.CompilerParams(vmem_limit_bytes=2 * MIB),
        cost_estimate=estimate(1000, 1000),
        name="pack",
    )(across, block)


def first_factor_kernel(a_ref, side_ref, f_ref, w_ref, cross_ref, *scratch):
    f_ref[...], w_ref[...], cross_ref[...] = eliminate(a_ref[...], [side_ref[...]], scratch)


def elimination_scratch(n, matrices):
    return [pltpu.VMEM((n // SUB, SUB, n), jnp.float32)] * matrices


def first_factor(a, side):
    n = a.shape[1]
    square = jax.ShapeDtypeStruct((n, n), jnp.float32)
    return pl.pallas_call(
        first_factor_kernel,
        out_shape=[square] * 3,
        in_specs=[VMEM] * 2,
        out_specs=[VMEM] * 3,
        scratch_shapes=elimination_scratch(n, 3),
        compiler_params=pltpu.CompilerParams(vmem_limit_bytes=4 * MIB),
        cost_estimate=estimate(8 * 10**9, 2 * MIB),
        name="first_factor",
    )(a, side)


def second_factor_kernel(a_ref, cross_ref, w0_ref, first_ref, rows_ref, rows_other_ref, ha_ref, hb_ref, oa_ref, ob_ref, matrix_ref,
                         f_ref, w_ref, solved_ref, rows_left_ref, top_left_ref, blocks_ref, left, right, sems, *scratch):
    n = w0_ref.shape[0]
    local_cols = matrix_ref.shape[2]
    local_rows = matrix_ref.shape[0]
    copies = [pltpu.make_async_copy(matrix_ref.at[:, :, j, :], blocks_ref.at[j], sems.at[j]) for j in range(local_cols)]
    for copy in copies:
        copy.start()
    odd = is_odd_row()
    w0 = w0_ref[...]
    cross = cross_ref[...]

    def solve_rows():
        solved = times(wide(panel_rows(0, first_ref, rows_ref, rows_other_ref)), tall(w0.T))
        solved_ref[...] = solved
        left[...] = wide(solved)

    def update_rows():
        rows_left_ref[...] = wide(panel_rows(1, first_ref, rows_ref, rows_other_ref) - times(left[...], tall(cross)))

    def top(panel, j):
        here = odd == (panel == 1)
        return jnp.concatenate([
            jnp.concatenate([jnp.where(here, ha_ref[b], oa_ref[b]), jnp.where(here, hb_ref[b], ob_ref[b])], axis=0)
            for b in (j, j + 1)], axis=1)

    def solve_top(j):
        def step():
            solved = tall(times(wide(w0), tall(top(0, j))))
            right[:, j * n:(j + 2) * n] = solved
            top_left_ref[:, j * n:(j + 2) * n] = tall(top(1, j) - times(wide(cross.T), solved))
        return step

    def update(j, i):
        def step():
            if i == 0 and j == 0:
                for copy in copies:
                    copy.wait()
            change = times(left[i * n:(i + 2) * n], right[:, j * n:(j + 2) * n])
            for b in range(2):
                part = change[:, b * n:(b + 1) * n].reshape(2, n, n)
                blocks_ref[j + b, i:i + 2] = blocks_ref[j + b, i:i + 2] - part
        return step

    steps = [solve_rows, update_rows]
    steps.extend(solve_top(j) for j in range(0, local_cols, 2))
    steps.extend(update(j, i) for j in range(0, local_cols, 2) for i in range(0, local_rows, 2))

    groups = n // SUB
    each = -(-len(steps) // groups)

    def several(some):
        def run():
            for step in some:
                step()
        return run

    beside = [several(steps[at:at + each]) for at in range(0, len(steps), each)]
    f_ref[...], w_ref[...] = eliminate(a_ref[...] - dot_over_rows(cross, cross), [], scratch, beside)


def second_factor(a, cross, w0, first_rows, rows, rows_other, ha, hb, oa, ob, matrix):
    local_rows, n, local_cols, _ = matrix.shape
    square = jax.ShapeDtypeStruct((n, n), jnp.float32)
    solved = jax.ShapeDtypeStruct((local_rows * n, n), jnp.float32)
    rows_left = jax.ShapeDtypeStruct((local_rows * n, 6 * n), jnp.bfloat16)
    top_left = jax.ShapeDtypeStruct((6 * n, local_cols * n), jnp.bfloat16)
    blocks = jax.ShapeDtypeStruct((local_cols, local_rows, n, n), jnp.float32)
    return pl.pallas_call(
        second_factor_kernel,
        out_shape=[square, square, solved, rows_left, top_left, blocks],
        in_specs=[VMEM] * 10 + [HBM],
        out_specs=[VMEM] * 6,
        scratch_shapes=[
            pltpu.VMEM((local_rows * n, 6 * n), jnp.bfloat16),
            pltpu.VMEM((6 * n, local_cols * n), jnp.bfloat16),
            pltpu.SemaphoreType.DMA((local_cols,)),
        ] + elimination_scratch(n, 2),
        compiler_params=pltpu.CompilerParams(vmem_limit_bytes=20 * MIB),
        cost_estimate=estimate(8 * 10**9, 4 * MIB),
        name="second_factor",
    )(a, cross, w0, first_rows, rows, rows_other, ha, hb, oa, ob, matrix)


def settle_kernel(f0_ref, f1_ref, w_ref, solved_ref, rows_left_ref, top_left_ref, blocks_ref, out_ref, result, sems):
    grid_row = lax.axis_index("row")
    grid_col = lax.axis_index("col")
    n = f0_ref.shape[0]
    local_cols, local_rows, _, _ = blocks_ref.shape
    w1 = w_ref[...]
    solved = times(rows_left_ref[...], tall(w1.T))
    left = wide(solved)
    inverse = wide(w1)

    def solve_top(j):
        return tall(times(inverse, top_left_ref[:, j * n:(j + 2) * n]))

    copies = []
    top = solve_top(0)
    for j in range(0, local_cols, 2):
        now = top
        if j + 2 < local_cols:
            top = solve_top(j + 2)
        update = times(left, now)
        for b in (j, j + 1):
            value = blocks_ref[b] - update[:, (b - j) * n:(b - j + 1) * n].reshape(local_rows, n, n)
            zero = jnp.zeros((n, n), jnp.float32)
            if b == 0:
                value = jnp.where(grid_col == 0, solved_ref[...].reshape(local_rows, n, n), value)
                value = jnp.where(grid_col == 1, solved.reshape(local_rows, n, n), value)
                head = jnp.where((grid_row <= 1) & (grid_col > grid_row), zero, value[0])
                head = jnp.where((grid_row == 0) & (grid_col == 0), f0_ref[...], head)
                head = jnp.where((grid_row == 1) & (grid_col == 1), f1_ref[...], head)
            else:
                head = jnp.where(grid_row <= 1, zero, value[0])
            result[b, 0] = head
            result[b, 1:] = value[1:]
            copy = pltpu.make_async_copy(result.at[b], out_ref.at[:, :, b, :], sems.at[b])
            copy.start()
            copies.append(copy)
    for copy in copies:
        copy.wait()


def settle(f0, f1, w1, solved, rows_left, top_left, blocks):
    local_cols, local_rows, n, _ = blocks.shape
    return pl.pallas_call(
        settle_kernel,
        out_shape=jax.ShapeDtypeStruct((local_rows, n, local_cols, n), jnp.float32),
        in_specs=[VMEM] * 7,
        out_specs=HBM,
        scratch_shapes=[pltpu.VMEM(blocks.shape, jnp.float32), pltpu.SemaphoreType.DMA((local_cols,))],
        compiler_params=pltpu.CompilerParams(vmem_limit_bytes=32 * MIB),
        cost_estimate=estimate(4 * 10**9, 6 * MIB),
        name="settle",
    )(f0, f1, w1, solved, rows_left, top_left, blocks)


def exchange(value, axis, mask, size):
    return lax.ppermute(value, axis, [(i, i ^ mask) for i in range(size)])


def bit_set(index, bit):
    return ((index >> bit) & 1) == 1


def spread(own, axis, index, size, bits):
    held = own
    for bit in bits:
        held = jnp.where(bit_set(index, bit), exchange(held, axis, 1 << bit, size), held)
    return held


def after(value, *others):
    return lax.optimization_barrier((value,) + others)


def shards(kernel):
    grid_row = lax.axis_index("row")
    grid_col = lax.axis_index("col")
    n_row = lax.axis_size("row")
    n_col = lax.axis_size("col")
    row_bits = list(range(1, n_row.bit_length() - 1))
    col_bits = list(range(1, n_col.bit_length() - 1))
    odd = (grid_row % 2) == 1

    block, column, upper, lower = panels(kernel)
    first_bit, last_bit = row_bits[0], row_bits[-1]

    moved = exchange(block, "col", 1 << col_bits[0], n_col)
    upper_moved = exchange(upper, "row", 1 << first_bit, n_row)
    lower_moved = exchange(lower, "row", 1 << last_bit, n_row)

    block = pick(moved, block, col_bits[0])
    block = spread(block, "col", grid_col, n_col, col_bits[1:])
    part = (column.shape[0] + 1) // 2
    block, early = after(block, column[:part])
    early_moved = exchange(early, "col", 1 << col_bits[0], n_col)
    across = exchange(block, "col", 1, n_col)
    ha = jnp.where(bit_set(grid_row, first_bit), upper_moved, upper)
    hb = jnp.where(bit_set(grid_row, last_bit), lower_moved, lower)
    across, block, ha, hb, late = after(across, block, ha, hb, column[part:])

    first_rows, pair = pack(across, block)
    pair, col_then = after(pair, grid_col)
    moved = exchange(pair, "row", 1 << first_bit, n_row)
    late_moved = exchange(late, "col", 1 << col_bits[0], n_col)
    early = jnp.where(bit_set(col_then, col_bits[0]), early_moved, early)
    pair = jnp.where(bit_set(grid_row, first_bit), moved, pair)
    pair, ha, hb, early = after(pair, ha, hb, early)
    moved = exchange(pair, "row", 1 << row_bits[1], n_row)
    ha_moved = exchange(ha, "row", 1 << row_bits[1], n_row)
    hb_moved = exchange(hb, "row", 1 << row_bits[-2], n_row)
    moved, col_then = after(moved, grid_col)
    late = jnp.where(bit_set(col_then, col_bits[0]), late_moved, late)
    rows = jnp.concatenate([early, late], axis=0)
    moved, pair, rows = after(moved, pair, rows)
    pair = jnp.where(bit_set(grid_row, row_bits[1]), moved, pair)
    pair = spread(pair, "row", grid_row, n_row, row_bits[2:])
    other = exchange(pair, "row", 1, n_row)
    ha = jnp.where(bit_set(grid_row, row_bits[1]), ha_moved, ha)
    hb = jnp.where(bit_set(grid_row, row_bits[-2]), hb_moved, hb)
    ha = spread(ha, "row", grid_row, n_row, row_bits[2:])
    hb = spread(hb, "row", grid_row, n_row, row_bits[:-2][::-1])
    other, pair, ha, hb = after(other, pair, ha, hb)
    oa = exchange(ha, "row", 1, n_row)
    ob = exchange(hb, "row", 1, n_row)

    n = block.shape[0]
    a00 = jnp.where(odd, other[:n], pair[:n])
    a11 = jnp.where(odd, pair[:n], other[:n])
    a01 = jnp.concatenate([jnp.where(odd, other[n:], pair[n:]), jnp.where(odd, pair[n:], other[n:])], axis=0)
    f0, w0, cross = first_factor(a00, a01)

    rows = spread(rows, "col", grid_col, n_col, col_bits[1:])
    rows_other = exchange(rows, "col", 1, n_col)
    f1, w1, solved, rows_left, top_left, blocks = second_factor(
        a11, cross, w0, first_rows, rows, rows_other, ha, hb, oa, ob, kernel)
    return settle(f0, f1, w1, solved, rows_left, top_left, blocks)


def solution(mesh):
    in_specs = (P(None, "row", None, "col"),)
    out_specs = P(None, "row", None, "col")
    return jax.shard_map(shards, mesh=mesh, in_specs=in_specs, out_specs=out_specs, check_vma=False)
```
